32 devices in a mesh: leaf: 4 (over y, x), grp: 8 (over z, core).
Axes of the slice: x: 2, y: 2, z: 4, core: 2. Of those that a mesh axis runs over, the one named last changes fastest.
Arguments:
- rhs_leaf: float32 [4, 8192, 256], P('leaf', 'grp'), may hold values from -6 to 6
- rhs_group: float32 [4, 512, 256], P('leaf'), may hold values from -6 to 6
- rhs_middle: float32 [1024, 256], replicated, may hold values from -6 to 6
- rhs_top: float32 [1024, 256], replicated, may hold values from -6 to 6
- inv_leaf: bfloat16 [4, 64, 128, 128], P('leaf', 'grp')
- inv_group: bfloat16 [4, 512, 512], P('leaf')
- inv_middle: bfloat16 [1024, 1024], replicated
- inv_top: bfloat16 [1024, 1024], replicated
- leaf_tiles: bfloat16 [4, 2048, 128, 128], P('leaf', 'grp'), may hold values from -0.03125 to 0.03125
- tile_column: int32 [4, 2048], P('leaf', 'grp'), may hold values from 0 to 7
- tile_target: int32 [4, 2048], P('leaf', 'grp'), may hold values from 0 to 19
- tile_count: int32 [4, 8], P('leaf', 'grp'), may hold values from 64 to 256, as said below
- group_panel: bfloat16 [4, 2048, 512], P('leaf', 'grp'), may hold values from -0.125 to 0.125
- middle_panel: bfloat16 [1024, 1024], P(('leaf', 'grp')), may hold values from -0.1875 to 0.1875
Outputs:
- leaf_out: float32 [4, 8192, 256], P('leaf', 'grp')
- group_out: float32 [4, 512, 256], P('leaf')
- mid_out: float32 [1024, 256], replicated
- top_out: float32 [1024, 256], replicated
The draws below stay inside these ranges and needn't reach their ends.
Inputs may be any that keep to these rules, and one draw needn't show every extreme that they name: Only the first tile_count slots of a device hold blocks of the factor; the other slots are ignored. Some device has all 256 slots live.
All inputs are finite; a program needn't handle non-finite values.
Results may differ from the reference program's by a relative error of at most 0.018.
Values may be sent and summed in bfloat16 or wider, within the bound.
No kernel may reach another device: no remote copies, remote signals or barrier semaphores. Data moves between devices by JAX's collectives and lax.ppermute only.
A program may use at most 128 MiB of HBM per device.

```python
import math
import jax
import jax.numpy as jnp
from jax import lax

BLOCK = 128
RHS = 256
GROUP_COLS = 512
MID_COLS = 1024
TOP_COLS = 1024
LEAF_SN = 8
TILES = 256
UPPER_BLOCKS = 20
N_LEAF = 4
N_GRP = 8


def unit_lower(key, leading, matrix_order):
    key_strict = jax.random.fold_in(key, 0)
    full_shape = leading + (matrix_order, matrix_order)
    strict = jax.random.normal(key_strict, full_shape, jnp.float32)
    diagonal = jnp.ones(full_shape, jnp.float32)
    lower_mask = jnp.tril(jnp.ones((matrix_order, matrix_order), jnp.float32), -1)
    eye_mask = jnp.eye(matrix_order, dtype=jnp.float32)
    values = strict * lower_mask * (0.5 / math.sqrt(matrix_order)) + diagonal * eye_mask
    return values.astype(jnp.bfloat16)


def draw_inv_leaf(key, part):
    return unit_lower(key, (N_LEAF, N_GRP * LEAF_SN), BLOCK)


def draw_inv_group(key, part):
    return unit_lower(key, (N_LEAF,), GROUP_COLS)


def draw_inv_middle(key, part):
    return unit_lower(key, (), MID_COLS)


def draw_inv_top(key, part):
    return unit_lower(key, (), TOP_COLS)


def draw_tile_count(key, part):
    key_counts, key_busiest = jax.random.split(jax.random.fold_in(key, 7))
    counts = jax.random.randint(key_counts, (N_LEAF * N_GRP,), TILES // 4, TILES + 1, jnp.int32)
    busiest = jax.random.randint(key_busiest, (), 0, N_LEAF * N_GRP, jnp.int32)
    counts = counts.at[busiest].set(TILES)
    return counts.reshape(N_LEAF, N_GRP).astype(jnp.int32)


def place_ends(entries, key, smallest, high):
    longest = entries.shape.index(max(entries.shape))
    spots = []
    for shift in (0, 1):
        where = [jax.random.randint(jax.random.fold_in(key, axis), (), 0, length) for axis, length in enumerate(entries.shape)]
        where[longest] = (where[longest] + shift) % entries.shape[longest]
        spots.append(tuple(where))
    return entries.at[spots[0]].set(smallest).at[spots[1]].set(high)


def steps_of(stream_key, extent, pieces, least, high):
    def one(position, parts):
        draws = jax.random.uniform(jax.random.fold_in(jax.random.fold_in(stream_key, 6), position), (parts,), jnp.float32, least / len(pieces), high / len(pieces))
        return jnp.repeat(jnp.exp(draws), extent[position] // parts).reshape((-1,) + (1,) * (len(extent) - position - 1))

    loudness = one(*pieces[0])
    for cut in pieces[1:]:
        loudness = loudness * one(*cut)
    return loudness


def bell_draw(own_key, dims, spread, bound, shards=(), kind=jnp.bfloat16):
    values = spread * jax.random.normal(own_key, dims, jnp.float32)
    if shards:
        values = values * steps_of(own_key, dims, shards, -0.22, 0.18)
    return jnp.clip(values, -bound, bound).astype(kind)


def setup_inputs(seed: int = 0) -> dict:
    key_of = jax.random.split(jax.random.key(seed), 15)
    rhs_leaf = bell_draw(key_of[0], (N_LEAF, N_GRP * LEAF_SN * BLOCK, RHS), 1.0, 6.0, ((0, 4), (1, 8)), jnp.float32)
    rhs_group = bell_draw(key_of[1], (N_LEAF, GROUP_COLS, RHS), 1.0, 6.0, ((0, 4),), jnp.float32)
    rhs_middle = bell_draw(key_of[2], (MID_COLS, RHS), 1.0, 6.0, (), jnp.float32)
    rhs_top = bell_draw(key_of[3], (TOP_COLS, RHS), 1.0, 6.0, (), jnp.float32)
    inv_leaf = draw_inv_leaf(jax.random.fold_in(key_of[14], 71), 0)
    inv_group = draw_inv_group(jax.random.fold_in(key_of[14], 71), 0)
    inv_middle = draw_inv_middle(jax.random.fold_in(key_of[14], 71), 0)
    inv_top = draw_inv_top(jax.random.fold_in(key_of[14], 71), 0)
    leaf_tiles = bell_draw(key_of[8], (N_LEAF, N_GRP * TILES, BLOCK, BLOCK), (BLOCK * N_LEAF * N_GRP * TILES // 32) ** -0.5, 0.03125, ((0, 4), (1, 8)))
    tile_column = place_ends(jax.random.randint(key_of[9], (N_LEAF, N_GRP * TILES), 0, LEAF_SN), jax.random.fold_in(key_of[9], 1), 0, LEAF_SN - 1).astype(jnp.int32)
    tile_target = place_ends(jax.random.randint(key_of[10], (N_LEAF, N_GRP * TILES), 0, UPPER_BLOCKS), jax.random.fold_in(key_of[10], 1), 0, UPPER_BLOCKS - 1).astype(jnp.int32)
    tile_count = draw_tile_count(jax.random.fold_in(key_of[14], 71), 0)
    group_panel = bell_draw(key_of[12], (N_LEAF, MID_COLS + TOP_COLS, GROUP_COLS), (GROUP_COLS * N_LEAF) ** -0.5, 0.125, ((0, 4), (1, 8)))
    middle_panel = bell_draw(key_of[13], (TOP_COLS, MID_COLS), MID_COLS ** -0.5, 0.1875, ((0, 32),))
    return {"rhs_leaf": rhs_leaf, "rhs_group": rhs_group, "rhs_middle": rhs_middle, "rhs_top": rhs_top, "inv_leaf": inv_leaf, "inv_group": inv_group, "inv_middle": inv_middle, "inv_top": inv_top, "leaf_tiles": leaf_tiles, "tile_column": tile_column, "tile_target": tile_target, "tile_count": tile_count, "group_panel": group_panel, "middle_panel": middle_panel}


def rounded(values):
    return lax.optimization_barrier(values.astype(jnp.bfloat16))


def reference(rhs_leaf, rhs_group, rhs_middle, rhs_top, inv_leaf, inv_group, inv_middle, inv_top, leaf_tiles, tile_column, tile_target, tile_count, group_panel, middle_panel):
    device_total = N_LEAF * N_GRP
    leaf_rhs = rhs_leaf.reshape(device_total, LEAF_SN, BLOCK, RHS)
    leaf_inv = inv_leaf.reshape(device_total, LEAF_SN, BLOCK, BLOCK)
    leaf_solved = jnp.einsum("dsij,dsjr->dsir", leaf_inv.astype(jnp.float32), rounded(leaf_rhs).astype(jnp.float32)).astype(jnp.bfloat16)
    tiles_all = leaf_tiles.reshape(device_total, TILES, BLOCK, BLOCK)
    columns_all = tile_column.reshape(device_total, TILES)
    targets_all = tile_target.reshape(device_total, TILES)
    live_all = jnp.arange(TILES)[None, :] < tile_count.reshape(device_total, 1)

    def forward_device(items):
        tiles_one, columns_one, targets_one, live_one, solved_one = items
        picked = solved_one[columns_one].astype(jnp.float32)
        terms = jnp.einsum("pij,pjr->pir", tiles_one.astype(jnp.float32), picked)
        terms = jnp.where(live_one[:, None, None], terms, 0.0)
        return jax.ops.segment_sum(terms, targets_one, num_segments=UPPER_BLOCKS)

    partial_sums = lax.map(forward_device, (tiles_all, columns_all, targets_all, live_all, leaf_solved))
    upper_sums = jnp.sum(partial_sums.reshape(N_LEAF, N_GRP, UPPER_BLOCKS * BLOCK, RHS), axis=1)
    middle_end = GROUP_COLS + MID_COLS
    group_list = []
    panel_terms = jnp.zeros((MID_COLS + TOP_COLS, RHS), jnp.float32)
    for leaf_index in range(N_LEAF):
        residual = rhs_group[leaf_index] - upper_sums[leaf_index, :GROUP_COLS]
        solved = jnp.dot(inv_group[leaf_index], rounded(residual), preferred_element_type=jnp.float32).astype(jnp.bfloat16)
        group_list.append(solved)
        panel_terms = panel_terms + jnp.dot(group_panel[leaf_index], solved, preferred_element_type=jnp.float32)
    group_solved = jnp.stack(group_list)
    lower_total = jnp.sum(upper_sums, axis=0)
    mid_residual = rhs_middle - lower_total[GROUP_COLS:middle_end] - panel_terms[:MID_COLS]
    mid_solved = jnp.dot(inv_middle, rounded(mid_residual), preferred_element_type=jnp.float32).astype(jnp.bfloat16)
    top_residual = rhs_top - lower_total[middle_end:] - panel_terms[MID_COLS:] - jnp.dot(middle_panel, mid_solved, preferred_element_type=jnp.float32)
    top_solved = jnp.dot(inv_top, rounded(top_residual), preferred_element_type=jnp.float32).astype(jnp.bfloat16)
    top_out = jnp.dot(inv_top.T, top_solved, preferred_element_type=jnp.float32)
    top_round = top_out.astype(jnp.bfloat16)
    mid_back = mid_solved.astype(jnp.float32) - jnp.dot(middle_panel.T, top_round, preferred_element_type=jnp.float32)
    mid_out = jnp.dot(inv_middle.T, rounded(mid_back), preferred_element_type=jnp.float32)
    upper_round = jnp.concatenate([mid_out.astype(jnp.bfloat16), top_round], axis=0)
    out_list = []
    for leaf_index in range(N_LEAF):
        back = group_solved[leaf_index].astype(jnp.float32) - jnp.dot(group_panel[leaf_index].T, upper_round, preferred_element_type=jnp.float32)
        out_list.append(jnp.dot(inv_group[leaf_index].T, rounded(back), preferred_element_type=jnp.float32))
    group_out = jnp.stack(out_list)
    shared_rows = jnp.broadcast_to(upper_round[None], (N_LEAF, MID_COLS + TOP_COLS, RHS))
    above = jnp.concatenate([group_out.astype(jnp.bfloat16), shared_rows], axis=1).reshape(N_LEAF, UPPER_BLOCKS, BLOCK, RHS)
    leaf_of_device = (jnp.arange(device_total) // N_GRP).astype(jnp.int32)

    def backward_device(items):
        tiles_one, columns_one, targets_one, live_one, solved_one, inv_one, leaf_one = items
        picked = above[leaf_one][targets_one].astype(jnp.float32)
        terms = jnp.einsum("pji,pjr->pir", tiles_one.astype(jnp.float32), picked)
        terms = jnp.where(live_one[:, None, None], terms, 0.0)
        back = solved_one.astype(jnp.float32) - jax.ops.segment_sum(terms, columns_one, num_segments=LEAF_SN)
        return jnp.einsum("sji,sjr->sir", inv_one.astype(jnp.float32), rounded(back).astype(jnp.float32))

    leaf_result = lax.map(backward_device, (tiles_all, columns_all, targets_all, live_all, leaf_solved, leaf_inv, leaf_of_device))
    leaf_out = leaf_result.reshape(N_LEAF, N_GRP * LEAF_SN * BLOCK, RHS)
    return (leaf_out, group_out, mid_out, top_out)
```

```python
import functools

import jax
import jax.numpy as jnp
from jax import lax
from jax.experimental import pallas as pl
from jax.experimental.pallas import tpu as pltpu
from jax.sharding import PartitionSpec as P

BF = jnp.bfloat16
F32 = jnp.float32
MIB = 1024 * 1024
CHUNKS = 16


def dot(a, b):
    return jnp.dot(a, b, preferred_element_type=F32)


def forward_kernel(
    group_cols,
    cols,
    tgts,
    count,
    rhs_ref,
    inv_ref,
    tiles_hbm,
    out_ref,
    solved_ref,
    dense_hbm,
    tiles,
    acc,
    dense,
    tile_sems,
    dense_sems,
):
    slots, block, _ = tiles_hbm.shape
    supernodes = inv_ref.shape[0]
    targets = acc.shape[0]
    chunks = tile_sems.shape[0]
    step = slots // chunks
    parts, part_rows, _ = out_ref.shape
    group_rows = group_cols // parts
    upper_rows = part_rows - group_rows

    def tile_copy(k):
        span = pl.ds(k * step, step)
        return pltpu.make_async_copy(tiles_hbm.at[span], tiles.at[span], tile_sems.at[k])

    for k in range(chunks):
        tile_copy(k).start()

    acc[...] = jnp.zeros_like(acc)
    for s in range(supernodes):
        rows = pl.ds(s * block, block)
        solved_ref[rows, :] = dot(inv_ref[s], rhs_ref[rows, :].astype(BF)).astype(BF)

    live = count[0]
    for k in range(chunks):
        tile_copy(k).wait()

        def add(p, carry):
            t = tgts[p]
            c = cols[p]
            acc[t, c] = acc[t, c] + tiles[p].astype(F32)
            return carry

        lax.fori_loop(k * step, jnp.clip(live, k * step, (k + 1) * step), add, 0)

    def dense_copy(t):
        rows = pl.ds(t * block, block)
        return pltpu.make_async_copy(dense.at[rows], dense_hbm.at[rows], dense_sems.at[t])

    group_blocks = group_cols // block
    for t in range(targets):
        rows = pl.ds(t * block, block)
        for c in range(supernodes):
            dense[rows, c * block : (c + 1) * block] = acc[t, c].astype(BF)
        dense_copy(t).start()
        total = dot(dense[rows, :], solved_ref[...]).astype(BF)
        if t < group_blocks:
            first, per, shift = t * block, group_rows, 0
        else:
            first, per, shift = (t - group_blocks) * block, upper_rows, group_rows
        piece = min(per, block)
        for q in range(0, block, piece):
            row = first + q
            place = shift + row % per
            out_ref[row // per, place : place + piece, :] = total[q : q + piece, :]
    for t in range(targets):
        dense_copy(t).wait()


def leaf_forward(rhs, inverse, tiles, cols, tgts, count, parts, group_cols, upper_cols):
    slots, block, _ = tiles.shape
    supernodes = inverse.shape[0]
    targets = (group_cols + upper_cols) // block
    width = rhs.shape[-1]
    any_space = pl.BlockSpec(memory_space=pl.ANY)
    vmem = pl.BlockSpec(memory_space=pltpu.VMEM)
    smem = pl.BlockSpec(memory_space=pltpu.SMEM)
    return pl.pallas_call(
        functools.partial(forward_kernel, group_cols),
        out_shape=(
            jax.ShapeDtypeStruct((parts, (group_cols + upper_cols) // parts, width), BF),
            jax.ShapeDtypeStruct((supernodes * block, width), BF),
            jax.ShapeDtypeStruct((targets * block, supernodes * block), BF),
        ),
        in_specs=[smem, smem, smem, vmem, vmem, any_space],
        out_specs=(vmem, vmem, any_space),
        scratch_shapes=[
            pltpu.VMEM((slots, block, block), BF),
            pltpu.VMEM((targets, supernodes, block, block), F32),
            pltpu.VMEM((targets * block, supernodes * block), BF),
            pltpu.SemaphoreType.DMA((CHUNKS,)),
            pltpu.SemaphoreType.DMA((targets,)),
        ],
        compiler_params=pltpu.CompilerParams(vmem_limit_bytes=40 * MIB),
        name="leaf_forward",
    )(cols, tgts, count, rhs, inverse, tiles)


def group_kernel(residual_ref, inv_ref, panel_ref, section_ref, solved_ref, out_ref):
    solved_ref[...] = dot(inv_ref[...], residual_ref[...]).astype(BF)
    out_ref[...] = (section_ref[...] + dot(panel_ref[...], solved_ref[...])).astype(BF)


def group_forward(residual, inverse, panel, section):
    vmem = pl.BlockSpec(memory_space=pltpu.VMEM)
    return pl.pallas_call(
        group_kernel,
        out_shape=(
            jax.ShapeDtypeStruct(residual.shape, BF),
            jax.ShapeDtypeStruct(section.shape, BF),
        ),
        in_specs=[vmem] * 4,
        out_specs=(vmem, vmem),
        compiler_params=pltpu.CompilerParams(vmem_limit_bytes=16 * MIB),
        name="group_forward",
    )(residual, inverse, panel, section)


def backward_kernel(
    upper_ref,
    group_solved_ref,
    leaf_solved_ref,
    inv_leaf_ref,
    inv_mid_hbm,
    panel_mid_hbm,
    inv_top_hbm,
    panel_group_hbm,
    inv_group_hbm,
    dense_hbm,
    leaf_hbm,
    group_hbm,
    mid_hbm,
    top_hbm,
    inv_mid,
    panel_mid,
    inv_top,
    panel_group,
    inv_group,
    dense,
    leaf_out,
    group_out,
    mid_out,
    top_out,
    above,
    sems,
    out_sems,
):
    pairs = (
        (inv_mid_hbm, inv_mid),
        (panel_mid_hbm, panel_mid),
        (inv_top_hbm, inv_top),
        (panel_group_hbm, panel_group),
        (inv_group_hbm, inv_group),
        (dense_hbm, dense),
    )
    loads = [pltpu.make_async_copy(a, b, sems.at[i]) for i, (a, b) in enumerate(pairs)]
    for load in loads:
        load.start()
    mid_rows = inv_mid.shape[0]
    top_rows = inv_top.shape[0]
    group_rows = inv_group.shape[0]
    supernodes, block, _ = inv_leaf_ref.shape
    upper_cols = pl.ds(group_rows, mid_rows + top_rows)
    mid_cols = pl.ds(group_rows, mid_rows)
    top_cols = pl.ds(group_rows + mid_rows, top_rows)

    loads[0].wait()
    mid_solved = dot(inv_mid[...], upper_ref[0:mid_rows, :]).astype(BF)
    loads[1].wait()
    top_residual = upper_ref[mid_rows:, :].astype(F32) - dot(panel_mid[...], mid_solved)
    loads[2].wait()
    top_solved = dot(inv_top[...], top_residual.astype(BF))
    top_t = dot(top_solved.T.astype(BF), inv_top[...])
    above[:, top_cols] = top_t.astype(BF)
    top_out[...] = top_t.T
    stores = [pltpu.make_async_copy(top_out, top_hbm, out_sems.at[0])]
    stores[0].start()
    mid_back = mid_solved.astype(F32).T - dot(above[:, top_cols], panel_mid[...])
    mid_t = dot(mid_back.astype(BF), inv_mid[...])
    above[:, mid_cols] = mid_t.astype(BF)
    mid_out[...] = mid_t.T
    stores.append(pltpu.make_async_copy(mid_out, mid_hbm, out_sems.at[1]))
    stores[1].start()
    loads[3].wait()
    group_back = group_solved_ref[...].astype(F32).T - dot(above[:, upper_cols], panel_group[...])
    loads[4].wait()
    group_t = dot(group_back.astype(BF), inv_group[...])
    above[:, 0:group_rows] = group_t.astype(BF)
    group_out[...] = group_t.T
    stores.append(pltpu.make_async_copy(group_out, group_hbm, out_sems.at[2]))
    stores[2].start()
    loads[5].wait()
    for s in range(supernodes):
        cols = pl.ds(s * block, block)
        terms = dot(above[...], dense[:, cols])
        back = (leaf_solved_ref[cols, :].astype(F32).T - terms).astype(BF)
        leaf_out[cols, :] = dot(back, inv_leaf_ref[s]).T
    stores.append(pltpu.make_async_copy(leaf_out, leaf_hbm, out_sems.at[3]))
    stores[3].start()
    for store in stores:
        store.wait()


def backward(
    upper, group_solved, leaf_solved, inv_leaf, inv_mid, panel_mid, inv_top, panel_group, inv_group, dense
):
    width = upper.shape[-1]
    any_space = pl.BlockSpec(memory_space=pl.ANY)
    vmem = pl.BlockSpec(memory_space=pltpu.VMEM)
    heavy = (inv_mid, panel_mid, inv_top, panel_group, inv_group, dense)
    outs = (
        jax.ShapeDtypeStruct(leaf_solved.shape, F32),
        jax.ShapeDtypeStruct(group_solved.shape, F32),
        jax.ShapeDtypeStruct((inv_mid.shape[0], width), F32),
        jax.ShapeDtypeStruct((inv_top.shape[0], width), F32),
    )
    return pl.pallas_call(
        backward_kernel,
        out_shape=outs,
        in_specs=[vmem] * 4 + [any_space] * 6,
        out_specs=(any_space,) * 4,
        scratch_shapes=[pltpu.VMEM(a.shape, a.dtype) for a in heavy]
        + [pltpu.VMEM(a.shape, a.dtype) for a in outs]
        + [
            pltpu.VMEM((width, dense.shape[0]), BF),
            pltpu.SemaphoreType.DMA((len(heavy),)),
            pltpu.SemaphoreType.DMA((len(outs),)),
        ],
        compiler_params=pltpu.CompilerParams(vmem_limit_bytes=48 * MIB),
        name="backward",
    )(upper, group_solved, leaf_solved, inv_leaf, *heavy)


def body(
    n_leaf,
    n_grp,
    rhs_leaf,
    rhs_group,
    rhs_middle,
    rhs_top,
    inv_leaf,
    inv_group,
    inv_middle,
    inv_top,
    leaf_tiles,
    tile_column,
    tile_target,
    tile_count,
    group_panel,
    middle_panel,
):
    group_cols = rhs_group.shape[1]
    upper_cols = rhs_middle.shape[0] + rhs_top.shape[0]
    width = rhs_top.shape[-1]
    group_rows = group_cols // n_grp
    upper_rows = upper_cols // n_grp
    mine = lax.axis_index("grp")

    with jax.named_scope("gather_panels"):
        panel_mid = lax.all_gather(middle_panel, ("leaf", "grp"), axis=0, tiled=True)
        panel_group = lax.all_gather(group_panel[0], "grp", axis=0, tiled=True)

    sums, leaf_solved, dense = leaf_forward(
        rhs_leaf[0],
        inv_leaf[0],
        leaf_tiles[0],
        tile_column[0],
        tile_target[0],
        tile_count[0],
        n_grp,
        group_cols,
        upper_cols,
    )
    with jax.named_scope("reduce_group"):
        pieces = lax.all_to_all(sums, "grp", 0, 0, tiled=True)
        section = jnp.sum(pieces.astype(F32), axis=0)
    with jax.named_scope("gather_group"):
        rhs_mine = lax.dynamic_slice_in_dim(rhs_group[0], mine * group_rows, group_rows, 0)
        residual = (rhs_mine - section[:group_rows]).astype(BF)
        spread = jnp.broadcast_to(residual[None], (n_grp,) + residual.shape)
        residual = lax.all_to_all(spread, "grp", 0, 0, tiled=True).reshape(group_cols, width)
    group_solved, partial = group_forward(
        residual, inv_group[0], group_panel[0], section[group_rows:]
    )
    with jax.named_scope("sum_leaf"):
        members = [partial]
        for other in range(1, n_leaf):
            pairs = [(i, i ^ other) for i in range(n_leaf)]
            members.append(lax.ppermute(partial, "leaf", pairs))
        members = [m.astype(F32) for m in members]
        while len(members) > 1:
            members = [members[i] + members[i + 1] for i in range(0, len(members), 2)]
        rhs_upper = jnp.concatenate([rhs_middle, rhs_top], axis=0)
        rhs_mine = lax.dynamic_slice_in_dim(rhs_upper, mine * upper_rows, upper_rows, 0)
        upper = (rhs_mine - members[0]).astype(BF)
    with jax.named_scope("gather_upper"):
        upper = lax.all_gather(upper, "grp", axis=0, tiled=True)
    leaf_out, group_out, mid_out, top_out = backward(
        upper,
        group_solved,
        leaf_solved,
        inv_leaf[0],
        inv_middle,
        panel_mid,
        inv_top,
        panel_group,
        inv_group[0],
        dense,
    )
    return leaf_out[None], group_out[None], mid_out, top_out


def solution(mesh):
    n_leaf = mesh.shape["leaf"]
    n_grp = mesh.shape["grp"]
    placed = (
        P("leaf", "grp", None),
        P("leaf", None, None),
        P(),
        P(),
        P("leaf", "grp", None, None),
        P("leaf", None, None),
        P(),
        P(),
        P("leaf", "grp", None, None),
        P("leaf", "grp"),
        P("leaf", "grp"),
        P("leaf", "grp"),
        P("leaf", "grp", None),
        P(("leaf", "grp"), None),
    )
    return jax.shard_map(
        functools.partial(body, n_leaf, n_grp),
        mesh=mesh,
        in_specs=placed,
        out_specs=(P("leaf", "grp", None), P("leaf", None, None), P(), P()),
        check_vma=False,
    )
```

```python
import functools

import jax
import jax.numpy as jnp
from jax import lax
from jax.experimental import pallas as pl
from jax.experimental.pallas import tpu as pltpu
from jax.sharding import PartitionSpec as P

BF = jnp.bfloat16
F32 = jnp.float32
MIB = 1024 * 1024
CHUNKS = 16
UNROLL = 4
HBM = pl.BlockSpec(memory_space=pltpu.HBM)
VMEM = pl.BlockSpec(memory_space=pltpu.VMEM)
SMEM = pl.BlockSpec(memory_space=pltpu.SMEM)


def dot(a, b):
    return jnp.dot(a, b, preferred_element_type=F32)


def place():
    g = lax.axis_index("grp")
    return lax.axis_index("leaf"), g >> 1, g & 1


def forward_kernel(
    sec,
    count,
    cols_hbm,
    tgts_hbm,
    rhs_hbm,
    inv_hbm,
    tiles_hbm,
    keep_hbm,
    send_hbm,
    solved_hbm,
    dense_hbm,
    cols,
    tgts,
    rhs,
    inv,
    tiles,
    acc,
    dense,
    solved,
    stage,
    in_sems,
    tile_sems,
    out_sems,
):
    slots, block, _ = tiles.shape
    supernodes = inv.shape[0]
    targets = acc.shape[0]
    chunks = tile_sems.shape[0]
    step = slots // chunks
    group_cols = stage.shape[1] - (targets * block - stage.shape[1])
    _, _, core = place()

    def tile_copy(k):
        span = pl.ds(k * step, step)
        return pltpu.make_async_copy(tiles_hbm.at[span], tiles.at[span], tile_sems.at[k])

    pairs = ((cols_hbm, cols), (tgts_hbm, tgts), (rhs_hbm, rhs), (inv_hbm, inv))
    loads = [pltpu.make_async_copy(a, b, in_sems.at[i]) for i, (a, b) in enumerate(pairs)]
    for load in loads:
        load.start()
    for k in range(chunks):
        tile_copy(k).start()

    acc[...] = jnp.zeros_like(acc)
    for load in loads:
        load.wait()
    for s in range(supernodes):
        rows = pl.ds(s * block, block)
        solved[rows, :] = dot(inv[s], rhs[rows, :].astype(BF)).astype(BF)
    stores = [pltpu.make_async_copy(solved, solved_hbm, out_sems.at[0])]
    stores[0].start()

    live = count[0]

    def add(p):
        t = tgts[0, p]
        c = cols[0, p]
        acc[t, c] = acc[t, c] + tiles[p].astype(F32)

    def add_some(i, carry):
        for u in range(UNROLL):
            add(i * UNROLL + u)
        return carry

    def add_one(p, carry):
        add(p)
        return carry

    whole = live // UNROLL
    per = step // UNROLL
    for k in range(chunks):
        tile_copy(k).wait()
        lax.fori_loop(k * per, jnp.clip(whole, k * per, (k + 1) * per), add_some, 0)
    lax.fori_loop(whole * UNROLL, live, add_one, 0)

    span = group_cols
    blocks = span // block
    for i in range(targets // blocks):
        for t in range(i * blocks, (i + 1) * blocks):
            for c in range(supernodes):
                dense[t * block : (t + 1) * block, c * block : (c + 1) * block] = acc[t, c].astype(BF)
        rows = pl.ds(i * span, span)
        stores.append(pltpu.make_async_copy(dense.at[rows], dense_hbm.at[rows], out_sems.at[3 + i]))
        stores[-1].start()
        total = dot(dense[rows, :], solved[...]).astype(BF)
        if i == 0:
            stage[0, 0:span, :] = total
            stage[1, 0:span, :] = total
        else:
            for q in range(0, span, sec):
                section = ((i - 1) * span + q) // sec
                begin = group_cols + (section // 2) * sec
                stage[(section % 2) ^ core, begin : begin + sec, :] = total[q : q + sec, :]
    for k, target in enumerate((keep_hbm, send_hbm)):
        stores.append(pltpu.make_async_copy(stage.at[k], target, out_sems.at[1 + k]))
        stores[-1].start()
    for store in stores:
        store.wait()


def leaf_forward(rhs, inverse, tiles, cols, tgts, count, sec, group_cols, upper_cols):
    slots, block, _ = tiles.shape
    supernodes = inverse.shape[0]
    targets = (group_cols + upper_cols) // block
    width = rhs.shape[-1]
    half = group_cols + upper_cols // 2
    return pl.pallas_call(
        functools.partial(forward_kernel, sec),
        out_shape=(
            jax.ShapeDtypeStruct((half, width), BF),
            jax.ShapeDtypeStruct((half, width), BF),
            jax.ShapeDtypeStruct((supernodes * block, width), BF),
            jax.ShapeDtypeStruct((targets * block, supernodes * block), BF),
        ),
        in_specs=[SMEM] + [HBM] * 5,
        out_specs=(HBM,) * 4,
        scratch_shapes=[
            pltpu.SMEM(cols.shape, cols.dtype),
            pltpu.SMEM(tgts.shape, tgts.dtype),
            pltpu.VMEM(rhs.shape, rhs.dtype),
            pltpu.VMEM(inverse.shape, inverse.dtype),
            pltpu.VMEM((slots, block, block), BF),
            pltpu.VMEM((targets, supernodes, block, block), F32),
            pltpu.VMEM((targets * block, supernodes * block), BF),
            pltpu.VMEM((supernodes * block, width), BF),
            pltpu.VMEM((2, half, width), BF),
            pltpu.SemaphoreType.DMA((4,)),
            pltpu.SemaphoreType.DMA((CHUNKS,)),
            pltpu.SemaphoreType.DMA((3 + targets * block // group_cols,)),
        ],
        compiler_params=pltpu.CompilerParams(vmem_limit_bytes=40 * MIB),
        name="leaf_forward",
    )(count, cols, tgts, rhs, inverse, tiles)


def fold_kernel(n_leaf, n_pos, keep, recv, inv, rhs, panel, *refs):
    outs, (gsum, stage) = refs[: n_leaf + 1], refs[n_leaf + 1 :]
    leaf, pos, core = place()
    group_cols = inv.shape[0]
    sec = panel.shape[0] // n_pos
    q = sec // n_leaf
    gq = group_cols // (2 * n_pos)
    gsum[...] = keep[0:group_cols, :].astype(F32) + recv[0:group_cols, :].astype(F32)
    residual = rhs[...] * (1.0 / n_pos) - gsum[...]
    solved = dot(inv[...], residual.astype(BF)).astype(BF)
    for p in range(n_pos):
        rows = pl.ds(group_cols + p * sec, sec)
        terms = dot(panel[p * sec : (p + 1) * sec, :], solved)
        terms = (terms + (keep[rows, :].astype(F32) + recv[rows, :].astype(F32))).astype(BF)
        for j in range(n_leaf):
            stage[j ^ leaf, p * q : (p + 1) * q, :] = terms[j * q : (j + 1) * q, :]
        begin = pl.multiple_of(core * (group_cols // 2) + p * gq, gq)
        outs[n_leaf][p ^ pos] = gsum[pl.ds(begin, gq), :].astype(BF)
    for k in range(n_leaf):
        outs[k][...] = stage[k]


def fold(keep, recv, inverse, rhs, panel, n_leaf, n_pos):
    width = rhs.shape[-1]
    part = (panel.shape[0] // n_leaf, width)
    gq = inverse.shape[0] // (2 * n_pos)
    return pl.pallas_call(
        functools.partial(fold_kernel, n_leaf, n_pos),
        out_shape=[jax.ShapeDtypeStruct(part, BF)] * n_leaf
        + [jax.ShapeDtypeStruct((n_pos, gq, width), BF)],
        in_specs=[VMEM] * 5,
        out_specs=[VMEM] * (n_leaf + 1),
        scratch_shapes=[pltpu.VMEM(rhs.shape, F32), pltpu.VMEM((n_leaf,) + part, BF)],
        compiler_params=pltpu.CompilerParams(vmem_limit_bytes=24 * MIB),
        name="fold_group",
    )(keep, recv, inverse, rhs, panel)


def sum_leaf_kernel(n_leaf, n_pos, *refs):
    parts, group, outs, stage = refs[:n_leaf], refs[n_leaf], refs[n_leaf + 1 : -1], refs[-1]
    _, pos, _ = place()
    q = stage.shape[1]
    total = parts[0][...].astype(F32)
    for part in parts[1:]:
        total = total + part[...].astype(F32)
    total = total.astype(BF)
    for p in range(n_pos):
        stage[p ^ pos] = total[p * q : (p + 1) * q, :]
    for k in range(n_pos):
        outs[k][0:q, :] = stage[k]
        outs[k][q:, :] = group[k]


def sum_leaf(parts, group):
    n_pos, gq, width = group.shape
    q = parts[0].shape[0] // n_pos
    return pl.pallas_call(
        functools.partial(sum_leaf_kernel, len(parts), n_pos),
        out_shape=[jax.ShapeDtypeStruct((q + gq, width), BF)] * n_pos,
        in_specs=[VMEM] * (len(parts) + 1),
        out_specs=[VMEM] * n_pos,
        scratch_shapes=[pltpu.VMEM((n_pos, q, width), BF)],
        name="sum_leaf",
    )(*parts, group)


def sum_pos_kernel(rhs, *refs):
    total = refs[0][...].astype(F32)
    for part in refs[1:-1]:
        total = total + part[...].astype(F32)
    refs[-1][...] = (rhs[...] - total).astype(BF)


def sum_pos(rhs, parts):
    return pl.pallas_call(
        sum_pos_kernel,
        out_shape=jax.ShapeDtypeStruct(rhs.shape, BF),
        in_specs=[VMEM] * (len(parts) + 1),
        out_specs=VMEM,
        name="sum_pos",
    )(rhs, *parts)


def backward_kernel(
    n_leaf,
    n_pos,
    mine,
    theirs,
    leaf_solved_hbm,
    inv_leaf_hbm,
    inv_mid_hbm,
    panel_mid_hbm,
    inv_top_hbm,
    inv_group_hbm,
    panel_group_hbm,
    dense_hbm,
    leaf_hbm,
    group_hbm,
    mid_hbm,
    top_hbm,
    leaf_solved,
    inv_leaf,
    inv_mid,
    panel_mid,
    inv_top,
    inv_group,
    panel_group,
    dense,
    leaf_out,
    group_out,
    mid_out,
    top_out,
    upper,
    residual,
    above,
    sems,
    out_sems,
):
    pairs = (
        (inv_mid_hbm, inv_mid),
        (panel_mid_hbm, panel_mid),
        (inv_top_hbm, inv_top),
        (inv_group_hbm, inv_group),
        (panel_group_hbm, panel_group),
        (dense_hbm, dense),
        (leaf_solved_hbm, leaf_solved),
        (inv_leaf_hbm, inv_leaf),
    )
    loads = [pltpu.make_async_copy(a, b, sems.at[i]) for i, (a, b) in enumerate(pairs)]
    for load in loads:
        load.start()
    mid_rows = inv_mid.shape[0]
    top_rows = inv_top.shape[0]
    group_rows = inv_group.shape[0]
    supernodes, block, _ = inv_leaf.shape
    upper_cols = pl.ds(group_rows, mid_rows + top_rows)
    mid_cols = pl.ds(group_rows, mid_rows)
    top_cols = pl.ds(group_rows + mid_rows, top_rows)
    leaf, pos, core = place()
    sec = (mid_rows + top_rows) // (2 * n_pos)
    q = sec // n_leaf
    gq = group_rows // (2 * n_pos)
    for kc, got in enumerate((mine, theirs)):
        for kz in range(n_pos):
            for kl in range(n_leaf):
                row = sec * (2 * (pos ^ kz) + (core ^ kc)) + q * (leaf ^ kl)
                begin = (kl * n_pos + kz) * q
                upper[pl.ds(pl.multiple_of(row, q), q), :] = got[begin : begin + q, :]
            row = (group_rows // 2) * (core ^ kc) + gq * (pos ^ kz)
            begin = n_leaf * n_pos * q + kz * gq
            residual[pl.ds(pl.multiple_of(row, gq), gq), :] = got[begin : begin + gq, :]

    loads[0].wait()
    mid_solved = dot(inv_mid[...], upper[0:mid_rows, :]).astype(BF)
    loads[1].wait()
    top_residual = upper[mid_rows:, :].astype(F32) - dot(panel_mid[...], mid_solved)
    loads[2].wait()
    top_solved = dot(inv_top[...], top_residual.astype(BF))
    top_t = dot(top_solved.T.astype(BF), inv_top[...])
    above[:, top_cols] = top_t.astype(BF)
    top_out[...] = top_t.T
    stores = [pltpu.make_async_copy(top_out, top_hbm, out_sems.at[0])]
    stores[0].start()
    mid_back = mid_solved.astype(F32).T - dot(above[:, top_cols], panel_mid[...])
    mid_t = dot(mid_back.astype(BF), inv_mid[...])
    above[:, mid_cols] = mid_t.astype(BF)
    mid_out[...] = mid_t.T
    stores.append(pltpu.make_async_copy(mid_out, mid_hbm, out_sems.at[1]))
    stores[1].start()
    loads[3].wait()
    group_solved = dot(inv_group[...], residual[...]).astype(BF).astype(F32).T
    loads[4].wait()
    group_back = group_solved - dot(above[:, upper_cols], panel_group[...])
    group_t = dot(group_back.astype(BF), inv_group[...])
    above[:, 0:group_rows] = group_t.astype(BF)
    group_out[...] = group_t.T
    stores.append(pltpu.make_async_copy(group_out, group_hbm, out_sems.at[2]))
    stores[2].start()
    for load in loads[5:]:
        load.wait()
    for s in range(supernodes):
        cols = pl.ds(s * block, block)
        terms = dot(above[...], dense[:, cols])
        back = (leaf_solved[cols, :].astype(F32).T - terms).astype(BF)
        leaf_out[cols, :] = dot(back, inv_leaf[s]).T
    stores.append(pltpu.make_async_copy(leaf_out, leaf_hbm, out_sems.at[3]))
    stores[3].start()
    for store in stores:
        store.wait()


def backward(
    mine,
    theirs,
    leaf_solved,
    inv_leaf,
    inv_mid,
    panel_mid,
    inv_top,
    inv_group,
    panel_group,
    dense,
    n_leaf,
    n_pos,
):
    width = mine.shape[-1]
    upper_rows = inv_mid.shape[0] + inv_top.shape[0]
    group_rows = inv_group.shape[0]
    heavy = (leaf_solved, inv_leaf, inv_mid, panel_mid, inv_top, inv_group, panel_group, dense)
    outs = (
        jax.ShapeDtypeStruct(leaf_solved.shape, F32),
        jax.ShapeDtypeStruct((group_rows, width), F32),
        jax.ShapeDtypeStruct((inv_mid.shape[0], width), F32),
        jax.ShapeDtypeStruct((inv_top.shape[0], width), F32),
    )
    return pl.pallas_call(
        functools.partial(backward_kernel, n_leaf, n_pos),
        out_shape=outs,
        in_specs=[VMEM] * 2 + [HBM] * len(heavy),
        out_specs=(HBM,) * 4,
        scratch_shapes=[pltpu.VMEM(a.shape, a.dtype) for a in heavy]
        + [pltpu.VMEM(a.shape, a.dtype) for a in outs]
        + [
            pltpu.VMEM((upper_rows, width), BF),
            pltpu.VMEM((group_rows, width), BF),
            pltpu.VMEM((width, dense.shape[0]), BF),
            pltpu.SemaphoreType.DMA((len(heavy),)),
            pltpu.SemaphoreType.DMA((len(outs),)),
        ],
        compiler_params=pltpu.CompilerParams(vmem_limit_bytes=48 * MIB),
        name="backward",
    )(mine, theirs, *heavy)


def swap(x, axis, size, bits):
    return lax.ppermute(x, axis, [(i, i ^ bits) for i in range(size)])


def weave(own, other, core):
    first = jnp.where(core == 0, own, other)
    second = jnp.where(core == 0, other, own)
    both = jnp.stack([first, second], axis=1)
    return both.reshape(-1, both.shape[-1])


def body(
    n_leaf,
    n_grp,
    rhs_leaf,
    rhs_group,
    rhs_middle,
    rhs_top,
    inv_leaf,
    inv_group,
    inv_middle,
    inv_top,
    leaf_tiles,
    tile_column,
    tile_target,
    tile_count,
    group_panel,
    middle_panel,
):
    n_pos = n_grp // 2
    group_cols = rhs_group.shape[1]
    mid_cols = rhs_middle.shape[0]
    upper_cols = mid_cols + rhs_top.shape[0]
    sec = upper_cols // n_grp
    q = sec // n_leaf
    gq = group_cols // n_grp
    leaf, pos, core = place()
    pos_groups = [[2 * p + c for p in range(n_pos)] for c in range(2)]
    chip_groups = [
        [a * n_grp + 2 * p + c for a in range(n_leaf) for p in range(n_pos)] for c in range(2)
    ]

    with jax.named_scope("gather_panels"):
        panel_half = lax.all_gather(group_panel[0], "grp", axis_index_groups=pos_groups)
        middle_half = lax.all_gather(
            middle_panel, ("leaf", "grp"), axis_index_groups=chip_groups
        )

    keep, send, leaf_solved, dense = leaf_forward(
        rhs_leaf[0],
        inv_leaf[0],
        leaf_tiles[0],
        tile_column,
        tile_target,
        tile_count[0],
        sec,
        group_cols,
        upper_cols,
    )
    with jax.named_scope("swap_cores"):
        recv = swap(send, "grp", n_grp, 1)
    *parts, group = fold(
        keep,
        recv,
        inv_group[0],
        rhs_group[0],
        panel_half.reshape(-1, group_cols),
        n_leaf,
        n_pos,
    )
    with jax.named_scope("sum_over_leaf"):
        parts = parts[:1] + [swap(parts[k], "leaf", n_leaf, k) for k in range(1, n_leaf)]
    sends = list(sum_leaf(parts, group))
    with jax.named_scope("sum_over_pos"):
        got = sends[:1] + [swap(sends[k], "grp", n_grp, 2 * k) for k in range(1, n_pos)]
    begin = sec * lax.axis_index("grp") + q * leaf
    low = lax.dynamic_slice_in_dim(rhs_middle, jnp.minimum(begin, mid_cols - q), q, 0)
    high = lax.dynamic_slice_in_dim(rhs_top, jnp.maximum(begin - mid_cols, 0), q, 0)
    group_begin = (group_cols // 2) * core + gq * pos
    group_rhs = lax.dynamic_slice_in_dim(rhs_group[0], group_begin, gq, 0)
    rhs_mine = jnp.concatenate([jnp.where(begin < mid_cols, low, high), group_rhs], axis=0)
    residual = sum_pos(rhs_mine, got)
    with jax.named_scope("gather_pos"):
        got = [residual] + [swap(residual, "grp", n_grp, 2 * k) for k in range(1, n_pos)]
        uppers = jnp.concatenate([x[:q] for x in got], axis=0)
        groups = [x[q:] for x in got]
    with jax.named_scope("gather_leaf"):
        stacks = [uppers] + [swap(uppers, "leaf", n_leaf, k) for k in range(1, n_leaf)]
        mine = jnp.concatenate(stacks + groups, axis=0)
    with jax.named_scope("gather_cores"):
        theirs = swap(mine, "grp", n_grp, 1)
    with jax.named_scope("swap_panels"):
        panel_group = weave(panel_half, swap(panel_half, "grp", n_grp, 1), core)
        panel_mid = weave(middle_half, swap(middle_half, "grp", n_grp, 1), core)
    leaf_out, group_out, mid_out, top_out = backward(
        mine,
        theirs,
        leaf_solved,
        inv_leaf[0],
        inv_middle,
        panel_mid,
        inv_top,
        inv_group[0],
        panel_group,
        dense,
        n_leaf,
        n_pos,
    )
    return leaf_out[None], group_out[None], mid_out, top_out


def solution(mesh):
    n_leaf = mesh.shape["leaf"]
    n_grp = mesh.shape["grp"]
    placed = (
        P("leaf", "grp", None),
        P("leaf", None, None),
        P(),
        P(),
        P("leaf", "grp", None, None),
        P("leaf", None, None),
        P(),
        P(),
        P("leaf", "grp", None, None),
        P("leaf", "grp"),
        P("leaf", "grp"),
        P("leaf", "grp"),
        P("leaf", "grp", None),
        P(("leaf", "grp"), None),
    )
    return jax.shard_map(
        functools.partial(body, n_leaf, n_grp),
        mesh=mesh,
        in_specs=placed,
        out_specs=(P("leaf", "grp", None), P("leaf", None, None), P(), P()),
        check_vma=False,
    )
```

```python
import functools

import jax
import jax.numpy as jnp
from jax import lax
from jax.experimental import pallas as pl
from jax.experimental.pallas import tpu as pltpu
from jax.sharding import PartitionSpec as P

BF = jnp.bfloat16
F32 = jnp.float32
MIB = 1024 * 1024
CHUNKS = 16
UNROLL = 4
HBM = pl.BlockSpec(memory_space=pltpu.HBM)
VMEM = pl.BlockSpec(memory_space=pltpu.VMEM)
BIG = 58 * MIB
SMALL = 4 * MIB


def dot(a, b):
    return jnp.dot(a, b, preferred_element_type=F32)


def place():
    g = lax.axis_index("grp")
    return lax.axis_index("leaf"), g >> 1, g & 1


def forward_kernel(
    sec,
    inv_rows,
    count_hbm,
    cols_hbm,
    tgts_hbm,
    rhs_hbm,
    inv_hbm,
    tiles_hbm,
    keep_hbm,
    send_hbm,
    solved_hbm,
    dense_hbm,
    count,
    cols,
    tgts,
    rhs,
    inv,
    tiles,
    acc,
    dense,
    solved,
    stage,
    in_sems,
    tile_sems,
    out_sems,
):
    slots, block, _ = tiles.shape
    supernodes = inv.shape[0]
    targets = acc.shape[0]
    chunks = tile_sems.shape[0]
    step = slots // chunks
    group_cols = inv_rows
    _, _, core = place()

    def tile_copy(k):
        span = pl.ds(k * step, step)
        return pltpu.make_async_copy(tiles_hbm.at[span], tiles.at[span], tile_sems.at[k])

    pairs = (
        (count_hbm, count),
        (cols_hbm, cols),
        (tgts_hbm, tgts),
        (rhs_hbm, rhs),
        (inv_hbm, inv),
    )
    loads = [pltpu.make_async_copy(a, b, in_sems.at[i]) for i, (a, b) in enumerate(pairs)]
    for load in loads:
        load.start()
    for k in range(chunks):
        tile_copy(k).start()

    acc[...] = jnp.zeros_like(acc)
    for load in loads:
        load.wait()
    for s in range(supernodes):
        rows = pl.ds(s * block, block)
        solved[rows, :] = dot(inv[s], rhs[rows, :].astype(BF)).astype(BF)
    stores = [pltpu.make_async_copy(solved, solved_hbm, out_sems.at[0])]
    stores[0].start()

    live = count[0, 0]

    def add(p):
        t = tgts[0, p]
        c = cols[0, p]
        acc[t, c] = acc[t, c] + tiles[p].astype(F32)

    def add_some(i, carry):
        for u in range(UNROLL):
            add(i * UNROLL + u)
        return carry

    def add_one(p, carry):
        add(p)
        return carry

    whole = live // UNROLL
    per = step // UNROLL
    for k in range(chunks):
        tile_copy(k).wait()
        lax.fori_loop(k * per, jnp.clip(whole, k * per, (k + 1) * per), add_some, 0)
    lax.fori_loop(whole * UNROLL, live, add_one, 0)

    span = group_cols
    blocks = span // block
    for i in range(targets // blocks):
        for t in range(i * blocks, (i + 1) * blocks):
            for c in range(supernodes):
                dense[t * block : (t + 1) * block, c * block : (c + 1) * block] = acc[t, c].astype(BF)
        rows = pl.ds(i * span, span)
        stores.append(pltpu.make_async_copy(dense.at[rows], dense_hbm.at[rows], out_sems.at[3 + i]))
        stores[-1].start()
        total = dot(dense[rows, :], solved[...]).astype(BF)
        if i == 0:
            for c in range(2):
                stage[c ^ core, 0 : span // 2, :] = total[c * span // 2 : (c + 1) * span // 2, :]
        else:
            for q in range(0, span, sec):
                section = ((i - 1) * span + q) // sec
                begin = group_cols // 2 + (section // 2) * sec
                stage[(section % 2) ^ core, begin : begin + sec, :] = total[q : q + sec, :]
    for k, target in enumerate((keep_hbm, send_hbm)):
        stores.append(pltpu.make_async_copy(stage.at[k], target, out_sems.at[1 + k]))
        stores[-1].start()
    for store in stores:
        store.wait()


def leaf_forward(rhs, inverse, tiles, cols, tgts, count, sec, group_cols, upper_cols):
    slots, block, _ = tiles.shape
    supernodes = inverse.shape[0]
    targets = (group_cols + upper_cols) // block
    width = rhs.shape[-1]
    half = (group_cols + upper_cols) // 2
    return pl.pallas_call(
        functools.partial(forward_kernel, sec, group_cols),
        out_shape=(
            jax.ShapeDtypeStruct((half, width), BF),
            jax.ShapeDtypeStruct((half, width), BF),
            jax.ShapeDtypeStruct((supernodes * block, width), BF),
            jax.ShapeDtypeStruct((targets * block, supernodes * block), BF),
        ),
        in_specs=[HBM] * 6,
        out_specs=(HBM,) * 4,
        scratch_shapes=[
            pltpu.SMEM(count.shape, count.dtype),
            pltpu.SMEM(cols.shape, cols.dtype),
            pltpu.SMEM(tgts.shape, tgts.dtype),
            pltpu.VMEM(rhs.shape, rhs.dtype),
            pltpu.VMEM(inverse.shape, inverse.dtype),
            pltpu.VMEM((slots, block, block), BF),
            pltpu.VMEM((targets, supernodes, block, block), F32),
            pltpu.VMEM((targets * block, supernodes * block), BF),
            pltpu.VMEM((supernodes * block, width), BF),
            pltpu.VMEM((2, half, width), BF),
            pltpu.SemaphoreType.DMA((5,)),
            pltpu.SemaphoreType.DMA((CHUNKS,)),
            pltpu.SemaphoreType.DMA((3 + targets * block // group_cols,)),
        ],
        compiler_params=pltpu.CompilerParams(vmem_limit_bytes=BIG),
        cost_estimate=pl.CostEstimate(
            flops=2 * targets * block * supernodes * block * width,
            bytes_accessed=2 * tiles.size + 4 * rhs.size,
            transcendentals=0,
        ),
        name="leaf_forward",
    )(count, cols, tgts, rhs, inverse, tiles)


def small(kernel, name, shapes, *args):
    return pl.pallas_call(
        kernel,
        out_shape=[jax.ShapeDtypeStruct(shape, BF) for shape in shapes],
        in_specs=[VMEM] * len(args),
        out_specs=[VMEM] * len(shapes),
        compiler_params=pltpu.CompilerParams(vmem_limit_bytes=SMALL),
        name=name,
    )(*args)


def total_of(refs):
    total = refs[0][...].astype(F32)
    for ref in refs[1:]:
        total = total + ref[...].astype(F32)
    return total


def pair_sum_kernel(n_leaf, n_pos, keep, recv, *refs):
    groups, parts = refs[:n_pos], refs[n_pos:]
    leaf, pos, _ = place()
    gq = groups[0].shape[0]
    q = parts[0].shape[0] // n_pos

    def both(begin, rows):
        span = pl.ds(pl.multiple_of(begin, rows), rows)
        return (keep[span, :].astype(F32) + recv[span, :].astype(F32)).astype(BF)

    for k in range(n_pos):
        p = pos ^ k
        groups[k][...] = both(p * gq, gq)
        for j in range(n_leaf):
            begin = n_pos * gq + (p * n_leaf + (leaf ^ j)) * q
            parts[j][k * q : (k + 1) * q, :] = both(begin, q)


def pair_sum(keep, recv, n_leaf, n_pos, gq, q):
    width = keep.shape[-1]
    shapes = [(gq, width)] * n_pos + [(n_pos * q, width)] * n_leaf
    kernel = functools.partial(pair_sum_kernel, n_leaf, n_pos)
    outs = small(kernel, "pair_sum", shapes, keep, recv)
    return list(outs[:n_pos]), list(outs[n_pos:])


def residual_kernel(rhs, *refs):
    refs[-1][...] = (rhs[...] - total_of(refs[:-1])).astype(BF)


def residual_of(rhs, parts):
    return small(residual_kernel, "residual", [rhs.shape], rhs, *parts)[0]


def group_kernel(n_leaf, n_pos, mine, theirs, inv, panel, *refs):
    solved, outs, residual = refs[0], refs[1:-1], refs[-1]
    leaf, pos, core = place()
    rows = inv.shape[0] // (2 * n_pos)
    for kc, got in enumerate((mine, theirs)):
        for k in range(n_pos):
            begin = ((core ^ kc) * n_pos + (pos ^ k)) * rows
            span = pl.ds(pl.multiple_of(begin, rows), rows)
            residual[span, :] = got[k * rows : (k + 1) * rows, :]
    solved[...] = dot(inv[...], residual[...]).astype(BF)
    q = panel.shape[0] // n_leaf
    for j in range(n_leaf):
        span = pl.ds(pl.multiple_of((leaf ^ j) * q, q), q)
        outs[j][...] = dot(panel[span, :], solved[...]).astype(BF)


def group_forward(mine, theirs, inverse, panel, n_leaf, n_pos):
    group_cols, width = inverse.shape[0], mine.shape[-1]
    part = (panel.shape[0] // n_leaf, width)
    outs = pl.pallas_call(
        functools.partial(group_kernel, n_leaf, n_pos),
        out_shape=[jax.ShapeDtypeStruct((group_cols, width), BF)]
        + [jax.ShapeDtypeStruct(part, BF)] * n_leaf,
        in_specs=[VMEM] * 4,
        out_specs=[VMEM] * (1 + n_leaf),
        scratch_shapes=[pltpu.VMEM((group_cols, width), BF)],
        compiler_params=pltpu.CompilerParams(vmem_limit_bytes=SMALL),
        name="group_forward",
    )(mine, theirs, inverse, panel)
    return outs[0], list(outs[1:])


def sum_leaf_kernel(n_leaf, *refs):
    total = total_of(refs[:n_leaf]).astype(BF)
    for k, out in enumerate(refs[n_leaf:]):
        q = out.shape[0]
        out[...] = total[k * q : (k + 1) * q, :]


def sum_leaf(parts, n_pos):
    rows, width = parts[0].shape
    kernel = functools.partial(sum_leaf_kernel, len(parts))
    return list(small(kernel, "sum_leaf", [(rows // n_pos, width)] * n_pos, *parts))


def stack_kernel(*refs):
    begin = 0
    for part in refs[:-1]:
        rows = part.shape[0]
        refs[-1][begin : begin + rows, :] = part[...]
        begin += rows


def stack(parts):
    rows = sum(part.shape[0] for part in parts)
    return small(stack_kernel, "stack", [(rows, parts[0].shape[1])], *parts)[0]


def backward_kernel(
    n_leaf,
    n_pos,
    n_mid,
    mine,
    theirs,
    group_solved_ref,
    leaf_solved_hbm,
    inv_leaf_hbm,
    inv_mid_hbm,
    inv_top_hbm,
    inv_group_hbm,
    dense_hbm,
    *refs,
):
    backward_steps(
        n_leaf,
        n_pos,
        refs[:n_mid],
        refs[n_mid : n_mid + 2],
        mine,
        theirs,
        group_solved_ref,
        leaf_solved_hbm,
        inv_leaf_hbm,
        inv_mid_hbm,
        inv_top_hbm,
        inv_group_hbm,
        dense_hbm,
        *refs[n_mid + 2 :],
    )


def backward_steps(
    n_leaf,
    n_pos,
    mid_parts,
    group_parts,
    mine,
    theirs,
    group_solved_ref,
    leaf_solved_hbm,
    inv_leaf_hbm,
    inv_mid_hbm,
    inv_top_hbm,
    inv_group_hbm,
    dense_hbm,
    leaf_hbm,
    group_hbm,
    mid_hbm,
    top_hbm,
    leaf_solved,
    inv_leaf,
    inv_mid,
    inv_top,
    inv_group,
    dense,
    panel_mid,
    panel_group,
    leaf_out,
    group_out,
    mid_out,
    top_out,
    upper,
    above,
    sems,
    mid_sems,
    group_sems,
    out_sems,
):
    leaf, pos, core = place()
    pairs = (
        (inv_mid_hbm, inv_mid),
        (inv_top_hbm, inv_top),
        (inv_group_hbm, inv_group),
        (dense_hbm, dense),
        (leaf_solved_hbm, leaf_solved),
        (inv_leaf_hbm, inv_leaf),
    )
    loads = [pltpu.make_async_copy(a, b, sems.at[i]) for i, (a, b) in enumerate(pairs)]
    mid_loads = []
    if len(mid_parts) == 1:
        mid_loads.append(pltpu.make_async_copy(mid_parts[0], panel_mid, mid_sems.at[0]))
    else:
        rows = mid_parts[0].shape[0] // n_pos
        for i, part in enumerate(mid_parts):
            kc, kl = divmod(i, n_leaf)
            for kz in range(n_pos):
                block = (leaf ^ kl) * (2 * n_pos) + 2 * (pos ^ kz) + (core ^ kc)
                span = pl.ds(pl.multiple_of(block * rows, rows), rows)
                got = part.at[pl.ds(kz * rows, rows)]
                sem = mid_sems.at[i * n_pos + kz]
                mid_loads.append(pltpu.make_async_copy(got, panel_mid.at[span], sem))
    group_loads = []
    for kc, part in enumerate(group_parts):
        rows = part.shape[1]
        for p in range(n_pos):
            span = pl.ds(pl.multiple_of((2 * p + (core ^ kc)) * rows, rows), rows)
            sem = group_sems.at[kc * n_pos + p]
            group_loads.append(pltpu.make_async_copy(part.at[p], panel_group.at[span], sem))
    for load in loads[:1] + mid_loads + loads[1:3] + group_loads + loads[3:]:
        load.start()
    mid_rows = inv_mid.shape[0]
    top_rows = inv_top.shape[0]
    group_rows = inv_group.shape[0]
    supernodes, block, _ = inv_leaf.shape
    upper_cols = pl.ds(group_rows, mid_rows + top_rows)
    mid_cols = pl.ds(group_rows, mid_rows)
    top_cols = pl.ds(group_rows + mid_rows, top_rows)
    sec = (mid_rows + top_rows) // (2 * n_pos)
    q = sec // n_leaf
    for kc, got in enumerate((mine, theirs)):
        for kz in range(n_pos):
            for kl in range(n_leaf):
                row = sec * (2 * (pos ^ kz) + (core ^ kc)) + q * (leaf ^ kl)
                begin = (kl * n_pos + kz) * q
                upper[pl.ds(pl.multiple_of(row, q), q), :] = got[begin : begin + q, :]

    loads[0].wait()
    mid_solved = dot(inv_mid[...], upper[0:mid_rows, :]).astype(BF)
    for load in mid_loads:
        load.wait()
    top_residual = upper[mid_rows:, :].astype(F32) - dot(panel_mid[...], mid_solved)
    loads[1].wait()
    top_solved = dot(inv_top[...], top_residual.astype(BF))
    top_t = dot(top_solved.T.astype(BF), inv_top[...])
    above[:, top_cols] = top_t.astype(BF)
    top_out[...] = top_t.T
    stores = [pltpu.make_async_copy(top_out, top_hbm, out_sems.at[0])]
    stores[0].start()
    mid_back = mid_solved.astype(F32).T - dot(above[:, top_cols], panel_mid[...])
    mid_t = dot(mid_back.astype(BF), inv_mid[...])
    above[:, mid_cols] = mid_t.astype(BF)
    mid_out[...] = mid_t.T
    stores.append(pltpu.make_async_copy(mid_out, mid_hbm, out_sems.at[1]))
    stores[1].start()
    loads[2].wait()
    group_solved = group_solved_ref[...].astype(F32).T
    for load in group_loads:
        load.wait()
    group_back = group_solved - dot(above[:, upper_cols], panel_group[...])
    group_t = dot(group_back.astype(BF), inv_group[...])
    above[:, 0:group_rows] = group_t.astype(BF)
    group_out[...] = group_t.T
    stores.append(pltpu.make_async_copy(group_out, group_hbm, out_sems.at[2]))
    stores[2].start()
    for load in loads[3:]:
        load.wait()
    for s in range(supernodes):
        cols = pl.ds(s * block, block)
        terms = dot(above[...], dense[:, cols])
        back = (leaf_solved[cols, :].astype(F32).T - terms).astype(BF)
        leaf_out[cols, :] = dot(back, inv_leaf[s]).T
    stores.append(pltpu.make_async_copy(leaf_out, leaf_hbm, out_sems.at[3]))
    stores[3].start()
    for store in stores:
        store.wait()


def backward(
    mine,
    theirs,
    group_solved,
    leaf_solved,
    inv_leaf,
    inv_mid,
    inv_top,
    inv_group,
    dense,
    mid_parts,
    group_parts,
    n_leaf,
    n_pos,
):
    width = mine.shape[-1]
    upper_rows = inv_mid.shape[0] + inv_top.shape[0]
    group_rows = inv_group.shape[0]
    heavy = (leaf_solved, inv_leaf, inv_mid, inv_top, inv_group, dense)
    outs = (
        jax.ShapeDtypeStruct(leaf_solved.shape, F32),
        jax.ShapeDtypeStruct((group_rows, width), F32),
        jax.ShapeDtypeStruct((inv_mid.shape[0], width), F32),
        jax.ShapeDtypeStruct((inv_top.shape[0], width), F32),
    )
    return pl.pallas_call(
        functools.partial(backward_kernel, n_leaf, n_pos, len(mid_parts)),
        out_shape=outs,
        in_specs=[VMEM] * 3 + [HBM] * (len(heavy) + len(mid_parts) + len(group_parts)),
        out_specs=(HBM,) * 4,
        scratch_shapes=[pltpu.VMEM(a.shape, a.dtype) for a in heavy]
        + [
            pltpu.VMEM((inv_top.shape[0], inv_mid.shape[0]), BF),
            pltpu.VMEM((upper_rows, group_rows), BF),
        ]
        + [pltpu.VMEM(a.shape, a.dtype) for a in outs]
        + [
            pltpu.VMEM((upper_rows, width), BF),
            pltpu.VMEM((width, dense.shape[0]), BF),
            pltpu.SemaphoreType.DMA((len(heavy),)),
            pltpu.SemaphoreType.DMA((len(mid_parts) * n_pos,)),
            pltpu.SemaphoreType.DMA((2 * n_pos,)),
            pltpu.SemaphoreType.DMA((len(outs),)),
        ],
        compiler_params=pltpu.CompilerParams(vmem_limit_bytes=36 * MIB),
        name="backward",
    )(mine, theirs, group_solved, *heavy, *mid_parts, *group_parts)


def swap(x, axis, size, bits):
    return lax.ppermute(x, axis, [(i, i ^ bits) for i in range(size)])


def swaps(x, axis, size, unit=1):
    return [x] + [swap(x, axis, size, unit * k) for k in range(1, size // unit)]


def after(x, *others):
    return lax.optimization_barrier((x, others))[0]


def body(
    n_leaf,
    n_grp,
    rhs_leaf,
    rhs_group,
    rhs_middle,
    rhs_top,
    inv_leaf,
    inv_group,
    inv_middle,
    inv_top,
    leaf_tiles,
    tile_column,
    tile_target,
    tile_count,
    group_panel,
    middle_panel,
):
    n_pos = n_grp // 2
    group_cols = rhs_group.shape[1]
    mid_cols = rhs_middle.shape[0]
    upper_cols = mid_cols + rhs_top.shape[0]
    sec = upper_cols // n_grp
    q = sec // n_leaf
    gq = group_cols // n_grp
    leaf, pos, core = place()
    by_parts = middle_panel.shape[0] % 16 == 0
    pos_groups = [[2 * p + c for p in range(n_pos)] for c in range(2)]
    with jax.named_scope("gather_group_panel"):
        panel_half = lax.all_gather(group_panel[0], "grp", axis_index_groups=pos_groups)
    with jax.named_scope("gather_middle_panel"):
        if by_parts:
            middles = swaps(middle_panel, "grp", n_grp, 2)
        else:
            middles = [lax.all_gather(middle_panel, ("leaf", "grp"), axis=0, tiled=True)]
    keep, send, leaf_solved, dense = leaf_forward(
        rhs_leaf[0],
        inv_leaf[0],
        leaf_tiles[0],
        tile_column,
        tile_target,
        tile_count,
        sec,
        group_cols,
        upper_cols,
    )
    with jax.named_scope("swap_cores"):
        if by_parts:
            send = after(send, middles)
        recv = swap(send, "grp", n_grp, 1)
    groups, parts = pair_sum(keep, recv, n_leaf, n_pos, gq, q)
    with jax.named_scope("sum_group_over_pos"):
        groups = groups[:1] + [swap(groups[k], "grp", n_grp, 2 * k) for k in range(1, n_pos)]
    with jax.named_scope("sum_upper_over_leaf"):
        parts = parts[:1] + [swap(parts[k], "leaf", n_leaf, k) for k in range(1, n_leaf)]
    with jax.named_scope("gather_middle_panel"):
        if by_parts:
            middle = stack(middles)
            groups = after(groups, middle)
            middles = swaps(middle, "leaf", n_leaf)
    group_begin = (group_cols // 2) * core + gq * pos
    group_rhs = lax.dynamic_slice_in_dim(rhs_group[0], group_begin, gq, 0)
    residual = residual_of(group_rhs, groups)
    with jax.named_scope("gather_group"):
        mine = stack(after(swaps(residual, "grp", n_grp, 2), parts))
        theirs = swap(mine, "grp", n_grp, 1)
    with jax.named_scope("sum_upper_over_pos"):
        uppers = sum_leaf(parts, n_pos)
        uppers = uppers[:1] + [swap(uppers[k], "grp", n_grp, 2 * k) for k in range(1, n_pos)]
    if by_parts:
        theirs = after(theirs, middles)
    group_solved, terms = group_forward(mine, theirs, inv_group[0], group_panel[0], n_leaf, n_pos)
    with jax.named_scope("sum_panel_over_leaf"):
        terms = terms[:1] + [swap(terms[k], "leaf", n_leaf, k) for k in range(1, n_leaf)]
    begin = sec * lax.axis_index("grp") + q * leaf
    low = lax.dynamic_slice_in_dim(rhs_middle, jnp.minimum(begin, mid_cols - q), q, 0)
    high = lax.dynamic_slice_in_dim(rhs_top, jnp.maximum(begin - mid_cols, 0), q, 0)
    with jax.named_scope("gather_middle_panel"):
        if by_parts:
            middles = middles + [swap(x, "grp", n_grp, 1) for x in middles]
    residual = residual_of(jnp.where(begin < mid_cols, low, high), uppers + terms)
    with jax.named_scope("gather_pos"):
        uppers = stack(swaps(residual, "grp", n_grp, 2))
    with jax.named_scope("swap_group_panel"):
        uppers = after(uppers, panel_half)
        panels = [panel_half, swap(panel_half, "grp", n_grp, 1)]
    with jax.named_scope("gather_leaf"):
        stacks = swaps(uppers, "leaf", n_leaf)
    with jax.named_scope("gather_cores"):
        mine = stack(after(stacks, middles, panels))
        theirs = swap(mine, "grp", n_grp, 1)
    leaf_out, group_out, mid_out, top_out = backward(
        mine,
        theirs,
        group_solved,
        leaf_solved,
        inv_leaf[0],
        inv_middle,
        inv_top,
        inv_group[0],
        dense,
        middles,
        panels,
        n_leaf,
        n_pos,
    )
    return leaf_out[None], group_out[None], mid_out, top_out


def solution(mesh):
    n_leaf = mesh.shape["leaf"]
    n_grp = mesh.shape["grp"]
    placed = (
        P("leaf", "grp", None),
        P("leaf", None, None),
        P(),
        P(),
        P("leaf", "grp", None, None),
        P("leaf", None, None),
        P(),
        P(),
        P("leaf", "grp", None, None),
        P("leaf", "grp"),
        P("leaf", "grp"),
        P("leaf", "grp"),
        P("leaf", "grp", None),
        P(("leaf", "grp"), None),
    )
    return jax.shard_map(
        functools.partial(body, n_leaf, n_grp),
        mesh=mesh,
        in_specs=placed,
        out_specs=(P("leaf", "grp", None), P("leaf", None, None), P(), P()),
        check_vma=False,
    )
```

```python
import functools

import jax
import jax.numpy as jnp
from jax import lax
from jax.experimental import pallas as pl
from jax.experimental.pallas import tpu as pltpu
from jax.sharding import PartitionSpec as P

BF = jnp.bfloat16
F32 = jnp.float32
MIB = 1024 * 1024
CHUNKS = 16
UNROLL = 4
HBM = pl.BlockSpec(memory_space=pltpu.HBM)
VMEM = pl.BlockSpec(memory_space=pltpu.VMEM)
BIG = 40 * MIB
SMALL = 12 * MIB


def in_hbm(*arrays):
    return [pltpu.with_memory_space_constraint(x, pltpu.HBM) for x in arrays]


def in_vmem(*arrays):
    return [pltpu.with_memory_space_constraint(x, pltpu.VMEM) for x in arrays]


def small(kernel, name, shapes, scratch, *args):
    return pl.pallas_call(
        kernel,
        out_shape=[pltpu.VMEM(shape, BF) for shape in shapes],
        in_specs=[VMEM] * len(args),
        out_specs=[VMEM] * len(shapes),
        scratch_shapes=scratch,
        compiler_params=pltpu.CompilerParams(vmem_limit_bytes=SMALL),
        name=name,
    )(*in_vmem(*args))


def dot(a, b):
    return jnp.dot(a, b, preferred_element_type=F32)


def place():
    g = lax.axis_index("grp")
    return lax.axis_index("leaf"), g >> 1, g & 1


def forward_kernel(
    sec,
    count_hbm,
    cols_hbm,
    tgts_hbm,
    rhs_hbm,
    inv_hbm,
    tiles_hbm,
    keep,
    send,
    solved_hbm,
    dense_hbm,
    count,
    cols,
    tgts,
    rhs,
    inv,
    tiles,
    acc,
    dense,
    solved,
    stage,
    in_sems,
    tile_sems,
    out_sems,
):
    slots, block, _ = tiles.shape
    supernodes = inv.shape[0]
    targets = acc.shape[0]
    chunks = tile_sems.shape[0]
    step = slots // chunks
    group_cols = stage.shape[1] - (targets * block - stage.shape[1])
    _, _, core = place()

    def tile_copy(k):
        span = pl.ds(k * step, step)
        return pltpu.make_async_copy(tiles_hbm.at[span], tiles.at[span], tile_sems.at[k])

    pairs = (
        (count_hbm, count),
        (cols_hbm, cols),
        (tgts_hbm, tgts),
        (rhs_hbm, rhs),
        (inv_hbm, inv),
    )
    loads = [pltpu.make_async_copy(a, b, in_sems.at[i]) for i, (a, b) in enumerate(pairs)]
    for load in loads:
        load.start()
    for k in range(chunks):
        tile_copy(k).start()

    acc[...] = jnp.zeros_like(acc)
    for load in loads:
        load.wait()
    for s in range(supernodes):
        rows = pl.ds(s * block, block)
        solved[rows, :] = dot(inv[s], rhs[rows, :].astype(BF)).astype(BF)
    stores = [pltpu.make_async_copy(solved, solved_hbm, out_sems.at[0])]
    stores[0].start()

    live = count[0, 0]

    def add(p):
        t = tgts[0, p]
        c = cols[0, p]
        acc[t, c] = acc[t, c] + tiles[p].astype(F32)

    def add_some(i, carry):
        for u in range(UNROLL):
            add(i * UNROLL + u)
        return carry

    def add_one(p, carry):
        add(p)
        return carry

    whole = live // UNROLL
    per = step // UNROLL
    for k in range(chunks):
        tile_copy(k).wait()
        lax.fori_loop(k * per, jnp.clip(whole, k * per, (k + 1) * per), add_some, 0)
    lax.fori_loop(whole * UNROLL, live, add_one, 0)

    span = group_cols
    blocks = span // block
    for i in range(targets // blocks):
        for t in range(i * blocks, (i + 1) * blocks):
            for c in range(supernodes):
                dense[t * block : (t + 1) * block, c * block : (c + 1) * block] = acc[t, c].astype(BF)
        rows = pl.ds(i * span, span)
        stores.append(pltpu.make_async_copy(dense.at[rows], dense_hbm.at[rows], out_sems.at[1 + i]))
        stores[-1].start()
        total = dot(dense[rows, :], solved[...]).astype(BF)
        if i == 0:
            stage[0, 0:span, :] = total
            stage[1, 0:span, :] = total
        else:
            for q in range(0, span, sec):
                section = ((i - 1) * span + q) // sec
                begin = group_cols + (section // 2) * sec
                stage[(section % 2) ^ core, begin : begin + sec, :] = total[q : q + sec, :]
    keep[...] = stage[0]
    send[...] = stage[1]
    for store in stores:
        store.wait()


def leaf_forward(rhs, inverse, tiles, cols, tgts, count, sec, group_cols, upper_cols):
    slots, block, _ = tiles.shape
    supernodes = inverse.shape[0]
    targets = (group_cols + upper_cols) // block
    width = rhs.shape[-1]
    half = group_cols + upper_cols // 2
    return pl.pallas_call(
        functools.partial(forward_kernel, sec),
        out_shape=(
            pltpu.VMEM((half, width), BF),
            pltpu.VMEM((half, width), BF),
            pltpu.HBM((supernodes * block, width), BF),
            pltpu.HBM((targets * block, supernodes * block), BF),
        ),
        in_specs=[HBM] * 6,
        out_specs=(VMEM, VMEM, HBM, HBM),
        scratch_shapes=[
            pltpu.SMEM(count.shape, count.dtype),
            pltpu.SMEM(cols.shape, cols.dtype),
            pltpu.SMEM(tgts.shape, tgts.dtype),
            pltpu.VMEM(rhs.shape, rhs.dtype),
            pltpu.VMEM(inverse.shape, inverse.dtype),
            pltpu.VMEM((slots, block, block), BF),
            pltpu.VMEM((targets, supernodes, block, block), F32),
            pltpu.VMEM((targets * block, supernodes * block), BF),
            pltpu.VMEM((supernodes * block, width), BF),
            pltpu.VMEM((2, half, width), BF),
            pltpu.SemaphoreType.DMA((5,)),
            pltpu.SemaphoreType.DMA((CHUNKS,)),
            pltpu.SemaphoreType.DMA((1 + targets * block // group_cols,)),
        ],
        compiler_params=pltpu.CompilerParams(vmem_limit_bytes=BIG),
        cost_estimate=pl.CostEstimate(
            flops=2 * targets * block * supernodes * block * width,
            bytes_accessed=2 * tiles.size + 4 * rhs.size,
            transcendentals=0,
        ),
        name="leaf_forward",
    )(count, *in_hbm(cols, tgts, rhs, inverse, tiles))


def fold_kernel(n_leaf, n_pos, keep, recv, inv, rhs, late, *refs):
    early, outs = refs[:n_pos], refs[n_pos : n_pos + n_leaf + 1]
    gsum, stage = refs[n_pos + n_leaf + 1 :]
    leaf, pos, core = place()
    group_cols = inv.shape[0]
    cut = early[0].shape[0]
    sec = cut + late.shape[1]
    q = sec // n_leaf
    gq = group_cols // (2 * n_pos)
    gsum[...] = keep[0:group_cols, :].astype(F32) + recv[0:group_cols, :].astype(F32)
    residual = rhs[...] * (1.0 / n_pos) - gsum[...]
    solved = dot(inv[...], residual.astype(BF)).astype(BF)
    for k in range(n_pos):
        p = pos ^ k
        for begin, panel in ((0, early[k]), (cut, late.at[p])):
            span = panel.shape[0]
            rows = pl.ds(pl.multiple_of(group_cols + p * sec + begin, cut), span)
            terms = dot(panel[...], solved)
            terms = (terms + (keep[rows, :].astype(F32) + recv[rows, :].astype(F32))).astype(BF)
            for j in range(begin // q, (begin + span) // q):
                stage[j ^ leaf, k * q : (k + 1) * q, :] = terms[j * q - begin : (j + 1) * q - begin, :]
        begin = pl.multiple_of(core * (group_cols // 2) + p * gq, gq)
        outs[n_leaf][k * gq : (k + 1) * gq, :] = gsum[pl.ds(begin, gq), :].astype(BF)
    for k in range(n_leaf):
        outs[k][...] = stage[k]


def fold(keep, recv, inverse, rhs, early, late, n_leaf):
    width = rhs.shape[-1]
    n_pos = len(early)
    part = (n_pos * (early[0].shape[0] + late.shape[1]) // n_leaf, width)
    outs = small(
        functools.partial(fold_kernel, n_leaf, n_pos),
        "fold_group",
        [part] * n_leaf + [(inverse.shape[0] // 2, width)],
        [pltpu.VMEM(rhs.shape, F32), pltpu.VMEM((n_leaf,) + part, BF)],
        keep,
        recv,
        inverse,
        rhs,
        late,
        *early,
    )
    return list(outs[:n_leaf]), outs[n_leaf]


def total_of(refs):
    total = refs[0][...].astype(F32)
    for ref in refs[1:]:
        total = total + ref[...].astype(F32)
    return total


def sum_leaf_kernel(n_leaf, *refs):
    group, outs = refs[n_leaf], refs[n_leaf + 1 :]
    n_pos = len(outs)
    q = refs[0].shape[0] // n_pos
    gq = group.shape[0] // n_pos
    total = total_of(refs[:n_leaf]).astype(BF)
    for k, out in enumerate(outs):
        out[0:q, :] = total[k * q : (k + 1) * q, :]
        out[q:, :] = group[k * gq : (k + 1) * gq, :]


def sum_leaf(parts, group, n_pos):
    rows = (parts[0].shape[0] + group.shape[0]) // n_pos
    kernel = functools.partial(sum_leaf_kernel, len(parts))
    shapes = [(rows, group.shape[1])] * n_pos
    return list(small(kernel, "sum_leaf", shapes, [], *parts, group))


def sum_pos_kernel(high, group, *refs):
    parts, out = refs[:-1], refs[-1]
    q = high.shape[0]
    total = total_of(parts)
    out[0:q, :] = (high[...] - total[0:q, :]).astype(BF)
    out[q:, :] = (group[...] - total[q:, :]).astype(BF)


def sum_pos(high, group, parts):
    return small(sum_pos_kernel, "sum_pos", [parts[0].shape], [], high, group, *parts)[0]


def stack_pos_kernel(q, *refs):
    parts, (uppers, groups) = refs[:-2], refs[-2:]
    gq = parts[0].shape[0] - q
    for k, part in enumerate(parts):
        uppers[k * q : (k + 1) * q, :] = part[0:q, :]
        groups[k * gq : (k + 1) * gq, :] = part[q:, :]


def stack_pos(parts, q):
    n_pos, (rows, width) = len(parts), parts[0].shape
    shapes = [(n_pos * q, width), (n_pos * (rows - q), width)]
    return small(functools.partial(stack_pos_kernel, q), "stack_pos", shapes, [], *parts)


def stack_kernel(*refs):
    begin = 0
    for part in refs[:-1]:
        rows = part.shape[0]
        refs[-1][begin : begin + rows, :] = part[...]
        begin += rows


def stack(parts):
    rows = sum(part.shape[0] for part in parts)
    return small(stack_kernel, "stack", [(rows, parts[0].shape[1])], [], *parts)[0]


def backward_kernel(
    n_leaf,
    n_pos,
    mine,
    theirs,
    leaf_solved_hbm,
    inv_leaf_hbm,
    inv_mid_hbm,
    inv_top_hbm,
    inv_group_hbm,
    dense_hbm,
    mid_hbm_parts,
    *refs,
):
    backward_steps(
        n_leaf,
        n_pos,
        mid_hbm_parts,
        refs[:4],
        mine,
        theirs,
        leaf_solved_hbm,
        inv_leaf_hbm,
        inv_mid_hbm,
        inv_top_hbm,
        inv_group_hbm,
        dense_hbm,
        *refs[4:],
    )


def backward_steps(
    n_leaf,
    n_pos,
    mid_parts,
    group_parts,
    mine,
    theirs,
    leaf_solved_hbm,
    inv_leaf_hbm,
    inv_mid_hbm,
    inv_top_hbm,
    inv_group_hbm,
    dense_hbm,
    leaf_hbm,
    group_hbm,
    mid_hbm,
    top_hbm,
    leaf_solved,
    inv_leaf,
    inv_mid,
    inv_top,
    inv_group,
    dense,
    panel_mid,
    panel_group,
    leaf_out,
    group_out,
    mid_out,
    top_out,
    upper,
    residual,
    above,
    sems,
    mid_sems,
    group_sems,
    out_sems,
):
    leaf, pos, core = place()
    pairs = (
        (inv_mid_hbm, inv_mid),
        (inv_top_hbm, inv_top),
        (inv_group_hbm, inv_group),
        (dense_hbm, dense),
        (leaf_solved_hbm, leaf_solved),
        (inv_leaf_hbm, inv_leaf),
    )
    loads = [pltpu.make_async_copy(a, b, sems.at[i]) for i, (a, b) in enumerate(pairs)]
    mid_loads = []
    if mid_parts.ndim == 2:
        mid_loads.append(pltpu.make_async_copy(mid_parts, panel_mid, mid_sems.at[0]))
    else:
        rows = mid_parts.shape[1] // n_leaf
        for i in range(2 * n_pos * n_leaf):
            g, k = divmod(i, n_leaf)
            begin = ((leaf ^ k) * (2 * n_pos) + g) * rows
            span = pl.ds(pl.multiple_of(begin, rows), rows)
            got = mid_parts.at[g, pl.ds(k * rows, rows)]
            mid_loads.append(pltpu.make_async_copy(got, panel_mid.at[span], mid_sems.at[i]))
    group_loads = []
    early, late = group_parts[:2], group_parts[2:]
    cut = early[0].shape[0] // n_pos
    sec = cut + late[0].shape[1]
    for kc in range(2):
        for k in range(n_pos):
            for j, (got, p, shift, rows) in enumerate((
                (early[kc].at[pl.ds(k * cut, cut)], pos ^ k, 0, cut),
                (late[kc].at[k], k, cut, sec - cut),
            )):
                begin = (2 * p + (core ^ kc)) * sec + shift
                span = pl.ds(pl.multiple_of(begin, cut), rows)
                sem = group_sems.at[(kc * n_pos + k) * 2 + j]
                group_loads.append(pltpu.make_async_copy(got, panel_group.at[span], sem))
    for load in loads[:1] + mid_loads + loads[1:3] + group_loads + loads[3:]:
        load.start()
    mid_rows = inv_mid.shape[0]
    top_rows = inv_top.shape[0]
    group_rows = inv_group.shape[0]
    supernodes, block, _ = inv_leaf.shape
    upper_cols = pl.ds(group_rows, mid_rows + top_rows)
    mid_cols = pl.ds(group_rows, mid_rows)
    top_cols = pl.ds(group_rows + mid_rows, top_rows)
    sec = (mid_rows + top_rows) // (2 * n_pos)
    q = sec // n_leaf
    gq = group_rows // (2 * n_pos)
    for kc, got in enumerate((mine, theirs)):
        for kz in range(n_pos):
            for kl in range(n_leaf):
                row = sec * (2 * (pos ^ kz) + (core ^ kc)) + q * (leaf ^ kl)
                begin = (kl * n_pos + kz) * q
                upper[pl.ds(pl.multiple_of(row, q), q), :] = got[begin : begin + q, :]
            row = (group_rows // 2) * (core ^ kc) + gq * (pos ^ kz)
            begin = n_leaf * n_pos * q + kz * gq
            residual[pl.ds(pl.multiple_of(row, gq), gq), :] = got[begin : begin + gq, :]

    loads[0].wait()
    mid_solved = dot(inv_mid[...], upper[0:mid_rows, :]).astype(BF)
    for load in mid_loads:
        load.wait()
    top_residual = upper[mid_rows:, :].astype(F32) - dot(panel_mid[...], mid_solved)
    loads[1].wait()
    top_solved = dot(inv_top[...], top_residual.astype(BF))
    top_t = dot(top_solved.T.astype(BF), inv_top[...])
    above[:, top_cols] = top_t.astype(BF)
    top_out[...] = top_t.T
    stores = [pltpu.make_async_copy(top_out, top_hbm, out_sems.at[0])]
    stores[0].start()
    mid_back = mid_solved.astype(F32).T - dot(above[:, top_cols], panel_mid[...])
    mid_t = dot(mid_back.astype(BF), inv_mid[...])
    above[:, mid_cols] = mid_t.astype(BF)
    mid_out[...] = mid_t.T
    stores.append(pltpu.make_async_copy(mid_out, mid_hbm, out_sems.at[1]))
    stores[1].start()
    loads[2].wait()
    group_solved = dot(inv_group[...], residual[...]).astype(BF).astype(F32).T
    for load in group_loads:
        load.wait()
    group_back = group_solved - dot(above[:, upper_cols], panel_group[...])
    group_t = dot(group_back.astype(BF), inv_group[...])
    above[:, 0:group_rows] = group_t.astype(BF)
    group_out[...] = group_t.T
    stores.append(pltpu.make_async_copy(group_out, group_hbm, out_sems.at[2]))
    stores[2].start()
    for load in loads[3:]:
        load.wait()
    for s in range(supernodes):
        cols = pl.ds(s * block, block)
        terms = dot(above[...], dense[:, cols])
        back = (leaf_solved[cols, :].astype(F32).T - terms).astype(BF)
        leaf_out[cols, :] = dot(back, inv_leaf[s]).T
    stores.append(pltpu.make_async_copy(leaf_out, leaf_hbm, out_sems.at[3]))
    stores[3].start()
    for store in stores:
        store.wait()


def backward(
    mine,
    theirs,
    leaf_solved,
    inv_leaf,
    inv_mid,
    inv_top,
    inv_group,
    dense,
    mid_parts,
    group_parts,
    n_leaf,
    n_pos,
):
    width = mine.shape[-1]
    upper_rows = inv_mid.shape[0] + inv_top.shape[0]
    group_rows = inv_group.shape[0]
    heavy = (leaf_solved, inv_leaf, inv_mid, inv_top, inv_group, dense)
    outs = (
        pltpu.HBM(leaf_solved.shape, F32),
        pltpu.HBM((group_rows, width), F32),
        pltpu.HBM((inv_mid.shape[0], width), F32),
        pltpu.HBM((inv_top.shape[0], width), F32),
    )
    return pl.pallas_call(
        functools.partial(backward_kernel, n_leaf, n_pos),
        out_shape=outs,
        in_specs=[VMEM] * 2 + [HBM] * (len(heavy) + 1 + len(group_parts)),
        out_specs=(HBM,) * 4,
        scratch_shapes=[pltpu.VMEM(a.shape, a.dtype) for a in heavy]
        + [
            pltpu.VMEM((inv_top.shape[0], inv_mid.shape[0]), BF),
            pltpu.VMEM((upper_rows, group_rows), BF),
        ]
        + [pltpu.VMEM(a.shape, a.dtype) for a in outs]
        + [
            pltpu.VMEM((upper_rows, width), BF),
            pltpu.VMEM((group_rows, width), BF),
            pltpu.VMEM((width, dense.shape[0]), BF),
            pltpu.SemaphoreType.DMA((len(heavy),)),
            pltpu.SemaphoreType.DMA((2 * n_pos * n_leaf,)),
            pltpu.SemaphoreType.DMA((4 * n_pos,)),
            pltpu.SemaphoreType.DMA((len(outs),)),
        ],
        compiler_params=pltpu.CompilerParams(vmem_limit_bytes=BIG),
        name="backward",
    )(*in_vmem(mine, theirs), *in_hbm(*heavy, mid_parts, *group_parts))


def swap(x, axis, size, bits):
    return lax.ppermute(x, axis, [(i, i ^ bits) for i in range(size)])


def swaps(x, axis, size, unit=1):
    return [x] + [swap(x, axis, size, unit * k) for k in range(1, size // unit)]


def after(x, *others):
    return lax.optimization_barrier((x, others))[0]


def body(
    n_leaf,
    n_grp,
    rhs_leaf,
    rhs_group,
    rhs_middle,
    rhs_top,
    inv_leaf,
    inv_group,
    inv_middle,
    inv_top,
    leaf_tiles,
    tile_column,
    tile_target,
    tile_count,
    group_panel,
    middle_panel,
):
    n_pos = n_grp // 2
    group_cols = rhs_group.shape[1]
    mid_cols = rhs_middle.shape[0]
    upper_cols = mid_cols + rhs_top.shape[0]
    sec = upper_cols // n_grp
    q = sec // n_leaf
    gq = group_cols // n_grp
    leaf, pos, core = place()
    by_parts = middle_panel.shape[0] % 16 == 0
    pos_groups = [[2 * p + c for p in range(n_pos)] for c in range(2)]
    cut = sec // 2
    with jax.named_scope("gather_group_panel"):
        late = lax.all_gather(group_panel[0, cut:], "grp", axis_index_groups=pos_groups)
        early = swaps(group_panel[0, :cut], "grp", n_grp, 2)
    if by_parts:
        with jax.named_scope("gather_middle_panel"):
            middle = swaps(middle_panel, "leaf", n_leaf)
    keep, send, leaf_solved, dense = leaf_forward(
        rhs_leaf[0],
        inv_leaf[0],
        leaf_tiles[0],
        tile_column,
        tile_target,
        tile_count,
        sec,
        group_cols,
        upper_cols,
    )
    with jax.named_scope("gather_middle_panel"):
        if by_parts:
            middle = stack(middle)
            send, early = after((send, early), middle)
            middle = lax.all_gather(middle, "grp")
        else:
            middle = lax.all_gather(middle_panel, ("leaf", "grp"), axis=0, tiled=True)
    with jax.named_scope("swap_cores"):
        recv = swap(send, "grp", n_grp, 1)
    parts, group = fold(keep, recv, inv_group[0], rhs_group[0], early, late, n_leaf)
    with jax.named_scope("sum_over_leaf"):
        parts = parts[:1] + [swap(parts[k], "leaf", n_leaf, k) for k in range(1, n_leaf)]
    sends = sum_leaf(parts, group, n_pos)
    with jax.named_scope("sum_over_pos"):
        got = sends[:1] + [swap(sends[k], "grp", n_grp, 2 * k) for k in range(1, n_pos)]
    begin = sec * lax.axis_index("grp") + q * leaf
    low = lax.dynamic_slice_in_dim(rhs_middle, jnp.minimum(begin, mid_cols - q), q, 0)
    high = lax.dynamic_slice_in_dim(rhs_top, jnp.maximum(begin - mid_cols, 0), q, 0)
    rhs_mine = jnp.where(begin < mid_cols, low, high)
    group_begin = (group_cols // 2) * core + gq * pos
    group_mine = lax.dynamic_slice_in_dim(rhs_group[0], group_begin, gq, 0)
    residual = sum_pos(rhs_mine, group_mine, got)
    with jax.named_scope("gather_pos"):
        uppers, groups = stack_pos(swaps(residual, "grp", n_grp, 2), q)
    with jax.named_scope("gather_leaf"):
        stacks = swaps(uppers, "leaf", n_leaf)
    with jax.named_scope("swap_group_panel"):
        early = stack(early)
        panels = [early, swap(early, "grp", n_grp, 1), late, swap(late, "grp", n_grp, 1)]
    with jax.named_scope("gather_cores"):
        mine = stack(after(stacks, panels) + [groups])
        theirs = swap(mine, "grp", n_grp, 1)
    leaf_out, group_out, mid_out, top_out = backward(
        mine,
        theirs,
        leaf_solved,
        inv_leaf[0],
        inv_middle,
        inv_top,
        inv_group[0],
        dense,
        middle,
        panels,
        n_leaf,
        n_pos,
    )
    return leaf_out[None], group_out[None], mid_out, top_out


def solution(mesh):
    n_leaf = mesh.shape["leaf"]
    n_grp = mesh.shape["grp"]
    placed = (
        P("leaf", "grp", None),
        P("leaf", None, None),
        P(),
        P(),
        P("leaf", "grp", None, None),
        P("leaf", None, None),
        P(),
        P(),
        P("leaf", "grp", None, None),
        P("leaf", "grp"),
        P("leaf", "grp"),
        P("leaf", "grp"),
        P("leaf", "grp", None),
        P(("leaf", "grp"), None),
    )
    return jax.shard_map(
        functools.partial(body, n_leaf, n_grp),
        mesh=mesh,
        in_specs=placed,
        out_specs=(P("leaf", "grp", None), P("leaf", None, None), P(), P()),
        check_vma=False,
    )
```

```python
import functools

import jax
import jax.numpy as jnp
from jax import lax
from jax.experimental import pallas as pl
from jax.experimental.pallas import tpu as pltpu
from jax.sharding import PartitionSpec as P

BF = jnp.bfloat16
F32 = jnp.float32
MIB = 1024 * 1024
CHUNKS = 16
UNROLL = 4
HBM = pl.BlockSpec(memory_space=pltpu.HBM)
VMEM = pl.BlockSpec(memory_space=pltpu.VMEM)
BIG = 32 * MIB
SMALL = 4 * MIB


def in_hbm(*arrays):
    return [pltpu.with_memory_space_constraint(x, pltpu.HBM) for x in arrays]


def in_vmem(*arrays):
    return [pltpu.with_memory_space_constraint(x, pltpu.VMEM) for x in arrays]


def small(kernel, name, shapes, scratch, *args):
    return pl.pallas_call(
        kernel,
        out_shape=[pltpu.VMEM(shape, BF) for shape in shapes],
        in_specs=[VMEM] * len(args),
        out_specs=[VMEM] * len(shapes),
        scratch_shapes=scratch,
        compiler_params=pltpu.CompilerParams(vmem_limit_bytes=SMALL),
        name=name,
    )(*in_vmem(*args))


def dot(a, b):
    return jnp.dot(a, b, preferred_element_type=F32)


def place():
    g = lax.axis_index("grp")
    return lax.axis_index("leaf"), g >> 1, g & 1


def forward_kernel(
    sec,
    group_cols,
    count_hbm,
    cols_hbm,
    tgts_hbm,
    rhs_hbm,
    inv_hbm,
    tiles_hbm,
    keep,
    send,
    solved,
    dense,
    count,
    cols,
    tgts,
    rhs,
    inv,
    tiles,
    acc,
    stage,
    in_sems,
    tile_sems,
):
    slots, block, _ = tiles.shape
    supernodes = inv.shape[0]
    targets = acc.shape[0]
    chunks = tile_sems.shape[0]
    step = slots // chunks
    _, _, core = place()

    def tile_copy(k):
        span = pl.ds(k * step, step)
        return pltpu.make_async_copy(tiles_hbm.at[span], tiles.at[span], tile_sems.at[k])

    pairs = (
        (count_hbm, count),
        (cols_hbm, cols),
        (tgts_hbm, tgts),
        (rhs_hbm, rhs),
        (inv_hbm, inv),
    )
    loads = [pltpu.make_async_copy(a, b, in_sems.at[i]) for i, (a, b) in enumerate(pairs)]
    for load in loads:
        load.start()
    for k in range(chunks):
        tile_copy(k).start()

    acc[...] = jnp.zeros_like(acc)
    for load in loads:
        load.wait()
    for s in range(supernodes):
        rows = pl.ds(s * block, block)
        solved[rows, :] = dot(inv[s], rhs[rows, :].astype(BF)).astype(BF)

    live = count[0, 0]

    def add(p):
        t = tgts[0, p]
        c = cols[0, p]
        acc[t, c] = acc[t, c] + tiles[p].astype(F32)

    def add_some(i, carry):
        for u in range(UNROLL):
            add(i * UNROLL + u)
        return carry

    def add_one(p, carry):
        add(p)
        return carry

    whole = live // UNROLL
    per = step // UNROLL
    for k in range(chunks):
        tile_copy(k).wait()
        lax.fori_loop(k * per, jnp.clip(whole, k * per, (k + 1) * per), add_some, 0)
    lax.fori_loop(whole * UNROLL, live, add_one, 0)

    span = group_cols
    blocks = span // block
    for i in range(targets // blocks):
        for t in range(i * blocks, (i + 1) * blocks):
            for c in range(supernodes):
                dense[t * block : (t + 1) * block, c * block : (c + 1) * block] = acc[t, c].astype(BF)
        total = dot(dense[i * span : (i + 1) * span, :], solved[...]).astype(BF)
        if i == 0:
            for c in range(2):
                stage[c ^ core, 0 : span // 2, :] = total[c * span // 2 : (c + 1) * span // 2, :]
        else:
            for q in range(0, span, sec):
                section = ((i - 1) * span + q) // sec
                begin = group_cols // 2 + (section // 2) * sec
                stage[(section % 2) ^ core, begin : begin + sec, :] = total[q : q + sec, :]
    keep[...] = stage[0]
    send[...] = stage[1]


def leaf_forward(rhs, inverse, tiles, cols, tgts, count, sec, group_cols, upper_cols):
    slots, block, _ = tiles.shape
    supernodes = inverse.shape[0]
    targets = (group_cols + upper_cols) // block
    width = rhs.shape[-1]
    half = (group_cols + upper_cols) // 2
    return pl.pallas_call(
        functools.partial(forward_kernel, sec, group_cols),
        out_shape=(
            pltpu.VMEM((half, width), BF),
            pltpu.VMEM((half, width), BF),
            pltpu.VMEM((supernodes * block, width), BF),
            pltpu.VMEM((targets * block, supernodes * block), BF),
        ),
        in_specs=[HBM] * 6,
        out_specs=(VMEM,) * 4,
        scratch_shapes=[
            pltpu.SMEM(count.shape, count.dtype),
            pltpu.SMEM(cols.shape, cols.dtype),
            pltpu.SMEM(tgts.shape, tgts.dtype),
            pltpu.VMEM(rhs.shape, rhs.dtype),
            pltpu.VMEM(inverse.shape, inverse.dtype),
            pltpu.VMEM((slots, block, block), BF),
            pltpu.VMEM((targets, supernodes, block, block), F32),
            pltpu.VMEM((2, half, width), BF),
            pltpu.SemaphoreType.DMA((5,)),
            pltpu.SemaphoreType.DMA((CHUNKS,)),
        ],
        compiler_params=pltpu.CompilerParams(vmem_limit_bytes=BIG),
        cost_estimate=pl.CostEstimate(
            flops=2 * targets * block * supernodes * block * width,
            bytes_accessed=2 * tiles.size + 4 * rhs.size,
            transcendentals=0,
        ),
        name="leaf_forward",
    )(count, *in_hbm(cols, tgts, rhs, inverse, tiles))


def total_of(refs):
    total = refs[0][...].astype(F32)
    for ref in refs[1:]:
        total = total + ref[...].astype(F32)
    return total


def pair_sum_kernel(n_leaf, n_pos, keep, recv, *refs):
    groups, parts = refs[:n_pos], refs[n_pos:]
    leaf, pos, _ = place()
    gq = groups[0].shape[0]
    q = parts[0].shape[0] // n_pos

    def both(begin, rows):
        span = pl.ds(pl.multiple_of(begin, rows), rows)
        return (keep[span, :].astype(F32) + recv[span, :].astype(F32)).astype(BF)

    for k in range(n_pos):
        p = pos ^ k
        groups[k][...] = both(p * gq, gq)
        for j in range(n_leaf):
            begin = n_pos * gq + (p * n_leaf + (leaf ^ j)) * q
            parts[j][k * q : (k + 1) * q, :] = both(begin, q)


def pair_sum(keep, recv, n_leaf, n_pos, gq, q):
    width = keep.shape[-1]
    shapes = [(gq, width)] * n_pos + [(n_pos * q, width)] * n_leaf
    kernel = functools.partial(pair_sum_kernel, n_leaf, n_pos)
    outs = small(kernel, "pair_sum", shapes, [], keep, recv)
    return list(outs[:n_pos]), list(outs[n_pos:])


def residual_kernel(rhs, *refs):
    refs[-1][...] = (rhs[...] - total_of(refs[:-1])).astype(BF)


def residual_of(rhs, parts):
    return small(residual_kernel, "residual", [rhs.shape], [], rhs, *parts)[0]


def group_kernel(n_leaf, n_pos, mine, theirs, inv, panel, *refs):
    solved, outs, residual = refs[0], refs[1:-1], refs[-1]
    leaf, pos, core = place()
    rows = inv.shape[0] // (2 * n_pos)
    for kc, got in enumerate((mine, theirs)):
        for k in range(n_pos):
            begin = ((core ^ kc) * n_pos + (pos ^ k)) * rows
            span = pl.ds(pl.multiple_of(begin, rows), rows)
            residual[span, :] = got[k * rows : (k + 1) * rows, :]
    solved[...] = dot(inv[...], residual[...]).astype(BF)
    q = panel.shape[0] // n_leaf
    for j in range(n_leaf):
        span = pl.ds(pl.multiple_of((leaf ^ j) * q, q), q)
        outs[j][...] = dot(panel[span, :], solved[...]).astype(BF)


def group_forward(mine, theirs, inverse, panel, n_leaf, n_pos):
    width = mine.shape[-1]
    shape = (inverse.shape[0], width)
    outs = small(
        functools.partial(group_kernel, n_leaf, n_pos),
        "group_forward",
        [shape] + [(panel.shape[0] // n_leaf, width)] * n_leaf,
        [pltpu.VMEM(shape, BF)],
        mine,
        theirs,
        inverse,
        panel,
    )
    return outs[0], list(outs[1:])


def sum_leaf_kernel(n_leaf, *refs):
    total = total_of(refs[:n_leaf]).astype(BF)
    for k, out in enumerate(refs[n_leaf:]):
        q = out.shape[0]
        out[...] = total[k * q : (k + 1) * q, :]


def sum_leaf(parts, n_pos):
    rows, width = parts[0].shape
    kernel = functools.partial(sum_leaf_kernel, len(parts))
    return list(small(kernel, "sum_leaf", [(rows // n_pos, width)] * n_pos, [], *parts))


def stack_kernel(*refs):
    begin = 0
    for part in refs[:-1]:
        rows = part.shape[0]
        refs[-1][begin : begin + rows, :] = part[...]
        begin += rows


def stack(parts):
    rows = sum(part.shape[0] for part in parts)
    return small(stack_kernel, "stack", [(rows, parts[0].shape[1])], [], *parts)[0]


def weave_kernel(n_leaf, n_pos, own, other, out):
    leaf, pos, core = place()
    rows = own.shape[0] // (n_leaf * n_pos)
    for kc, part in enumerate((own, other)):
        for kl in range(n_leaf):
            for k in range(n_pos):
                block = (leaf ^ kl) * (2 * n_pos) + 2 * (pos ^ k) + (core ^ kc)
                span = pl.ds(pl.multiple_of(block * rows, rows), rows)
                begin = (kl * n_pos + k) * rows
                out[span, :] = part[begin : begin + rows, :]


def weave(own, other, n_leaf, n_pos):
    shape = (2 * own.shape[0], own.shape[1])
    kernel = functools.partial(weave_kernel, n_leaf, n_pos)
    return small(kernel, "weave", [shape], [], own, other)[0]


def backward_kernel(
    n_leaf,
    n_pos,
    mine,
    theirs,
    group_solved_ref,
    leaf_solved,
    dense,
    inv_mid,
    panel_mid,
    inv_top_hbm,
    inv_group_hbm,
    panel_group_hbm,
    inv_leaf_hbm,
    leaf_hbm,
    group_hbm,
    mid_hbm,
    top_hbm,
    inv_top,
    inv_group,
    panel_group,
    inv_leaf,
    leaf_out,
    group_out,
    mid_out,
    top_out,
    upper,
    above,
    sems,
    out_sems,
):
    leaf, pos, core = place()
    pairs = (
        (inv_top_hbm, inv_top),
        (inv_group_hbm, inv_group),
        (panel_group_hbm, panel_group),
        (inv_leaf_hbm, inv_leaf),
    )
    loads = [pltpu.make_async_copy(a, b, sems.at[i]) for i, (a, b) in enumerate(pairs)]
    for load in loads:
        load.start()
    mid_rows = inv_mid.shape[0]
    top_rows = inv_top.shape[0]
    group_rows = inv_group.shape[0]
    supernodes, block, _ = inv_leaf.shape
    upper_cols = pl.ds(group_rows, mid_rows + top_rows)
    mid_cols = pl.ds(group_rows, mid_rows)
    top_cols = pl.ds(group_rows + mid_rows, top_rows)
    sec = (mid_rows + top_rows) // (2 * n_pos)
    q = sec // n_leaf
    for kc, got in enumerate((mine, theirs)):
        for kz in range(n_pos):
            for kl in range(n_leaf):
                row = sec * (2 * (pos ^ kz) + (core ^ kc)) + q * (leaf ^ kl)
                begin = (kl * n_pos + kz) * q
                upper[pl.ds(pl.multiple_of(row, q), q), :] = got[begin : begin + q, :]

    mid_solved = dot(inv_mid[...], upper[0:mid_rows, :]).astype(BF)
    top_residual = upper[mid_rows:, :].astype(F32) - dot(panel_mid[...], mid_solved)
    loads[0].wait()
    top_solved = dot(inv_top[...], top_residual.astype(BF))
    top_t = dot(top_solved.T.astype(BF), inv_top[...])
    above[:, top_cols] = top_t.astype(BF)
    top_out[...] = top_t.T
    stores = [pltpu.make_async_copy(top_out, top_hbm, out_sems.at[0])]
    stores[0].start()
    mid_back = mid_solved.astype(F32).T - dot(above[:, top_cols], panel_mid[...])
    mid_t = dot(mid_back.astype(BF), inv_mid[...])
    above[:, mid_cols] = mid_t.astype(BF)
    mid_out[...] = mid_t.T
    stores.append(pltpu.make_async_copy(mid_out, mid_hbm, out_sems.at[1]))
    stores[1].start()
    for load in loads[1:]:
        load.wait()
    group_solved = group_solved_ref[...].astype(F32).T
    group_back = group_solved - dot(above[:, upper_cols], panel_group[...])
    group_t = dot(group_back.astype(BF), inv_group[...])
    above[:, 0:group_rows] = group_t.astype(BF)
    group_out[...] = group_t.T
    stores.append(pltpu.make_async_copy(group_out, group_hbm, out_sems.at[2]))
    stores[2].start()
    for s in range(supernodes):
        cols = pl.ds(s * block, block)
        terms = dot(above[...], dense[:, cols])
        back = (leaf_solved[cols, :].astype(F32).T - terms).astype(BF)
        leaf_out[cols, :] = dot(back, inv_leaf[s]).T
    stores.append(pltpu.make_async_copy(leaf_out, leaf_hbm, out_sems.at[3]))
    stores[3].start()
    for store in stores:
        store.wait()


def backward(close, far, n_leaf, n_pos):
    mine, _, group_solved, leaf_solved, dense, inv_mid, panel_mid = close
    inv_top, inv_group, _, _ = far
    width = mine.shape[-1]
    outs = (
        leaf_solved.shape,
        group_solved.shape,
        (inv_mid.shape[0], width),
        (inv_top.shape[0], width),
    )
    return pl.pallas_call(
        functools.partial(backward_kernel, n_leaf, n_pos),
        out_shape=[pltpu.HBM(shape, F32) for shape in outs],
        in_specs=[VMEM] * len(close) + [HBM] * len(far),
        out_specs=[HBM] * 4,
        scratch_shapes=[pltpu.VMEM(x.shape, x.dtype) for x in far]
        + [pltpu.VMEM(shape, F32) for shape in outs]
        + [
            pltpu.VMEM((inv_mid.shape[0] + inv_top.shape[0], width), BF),
            pltpu.VMEM((width, dense.shape[0]), BF),
            pltpu.SemaphoreType.DMA((len(far),)),
            pltpu.SemaphoreType.DMA((len(outs),)),
        ],
        compiler_params=pltpu.CompilerParams(vmem_limit_bytes=BIG),
        name="backward",
    )(*in_vmem(*close), *in_hbm(*far))


def swap(x, axis, size, bits):
    return lax.ppermute(x, axis, [(i, i ^ bits) for i in range(size)])


def swaps(x, axis, size, unit=1):
    return [x] + [swap(x, axis, size, unit * k) for k in range(1, size // unit)]


def after(x, *others):
    return lax.optimization_barrier((x, others))[0]


def body(
    n_leaf,
    n_grp,
    rhs_leaf,
    rhs_group,
    rhs_middle,
    rhs_top,
    inv_leaf,
    inv_group,
    inv_middle,
    inv_top,
    leaf_tiles,
    tile_column,
    tile_target,
    tile_count,
    group_panel,
    middle_panel,
):
    n_pos = n_grp // 2
    group_cols = rhs_group.shape[1]
    mid_cols = rhs_middle.shape[0]
    upper_cols = mid_cols + rhs_top.shape[0]
    sec = upper_cols // n_grp
    q = sec // n_leaf
    gq = group_cols // n_grp
    leaf, pos, core = place()
    by_parts = middle_panel.shape[0] % 16 == 0
    with jax.named_scope("gather_group_panel"):
        panel = lax.all_gather(group_panel[0], "grp", axis=0, tiled=True)
    with jax.named_scope("gather_middle_panel"):
        if by_parts:
            middles = swaps(middle_panel, "grp", n_grp, 2)
        else:
            middle = lax.all_gather(middle_panel, ("leaf", "grp"), axis=0, tiled=True)
    keep, send, leaf_solved, dense = leaf_forward(
        rhs_leaf[0],
        inv_leaf[0],
        leaf_tiles[0],
        tile_column,
        tile_target,
        tile_count,
        sec,
        group_cols,
        upper_cols,
    )
    with jax.named_scope("swap_cores"):
        if by_parts:
            send = after(send, middles)
        recv = swap(send, "grp", n_grp, 1)
    groups, parts = pair_sum(keep, recv, n_leaf, n_pos, gq, q)
    with jax.named_scope("sum_group_over_pos"):
        groups = groups[:1] + [swap(groups[k], "grp", n_grp, 2 * k) for k in range(1, n_pos)]
    with jax.named_scope("sum_upper_over_leaf"):
        parts = parts[:1] + [swap(parts[k], "leaf", n_leaf, k) for k in range(1, n_leaf)]
    group_begin = (group_cols // 2) * core + gq * pos
    group_rhs = lax.dynamic_slice_in_dim(rhs_group[0], group_begin, gq, 0)
    residual = residual_of(group_rhs, after(groups, parts))
    with jax.named_scope("sum_upper_over_pos"):
        uppers = sum_leaf(parts, n_pos)
        uppers = uppers[:1] + [swap(uppers[k], "grp", n_grp, 2 * k) for k in range(1, n_pos)]
    with jax.named_scope("gather_group"):
        mine = stack(after(swaps(residual, "grp", n_grp, 2), uppers))
        theirs = swap(mine, "grp", n_grp, 1)
    group_solved, terms = group_forward(mine, theirs, inv_group[0], group_panel[0], n_leaf, n_pos)
    with jax.named_scope("sum_panel_over_leaf"):
        terms = terms[:1] + [swap(terms[k], "leaf", n_leaf, k) for k in range(1, n_leaf)]
    begin = sec * lax.axis_index("grp") + q * leaf
    low = lax.dynamic_slice_in_dim(rhs_middle, jnp.minimum(begin, mid_cols - q), q, 0)
    high = lax.dynamic_slice_in_dim(rhs_top, jnp.maximum(begin - mid_cols, 0), q, 0)
    rhs_mine = jnp.where(begin < mid_cols, low, high)
    residual = residual_of(rhs_mine, uppers + terms)
    with jax.named_scope("gather_middle_panel"):
        if by_parts:
            middles = swaps(stack(after(middles, terms)), "leaf", n_leaf)
    with jax.named_scope("gather_pos"):
        uppers = stack(swaps(residual, "grp", n_grp, 2))
    with jax.named_scope("gather_middle_panel"):
        if by_parts:
            middle, uppers = after((stack(middles), uppers), (middles, panel))
            middle = weave(middle, swap(middle, "grp", n_grp, 1), n_leaf, n_pos)
    with jax.named_scope("gather_leaf"):
        stacks = swaps(uppers, "leaf", n_leaf)
    with jax.named_scope("gather_cores"):
        mine = stack(after(stacks, middle))
        theirs = swap(mine, "grp", n_grp, 1)
    leaf_out, group_out, mid_out, top_out = backward(
        (mine, theirs, group_solved, leaf_solved, dense, inv_middle, middle),
        (inv_top, inv_group[0], panel, inv_leaf[0]),
        n_leaf,
        n_pos,
    )
    return leaf_out[None], group_out[None], mid_out, top_out


def solution(mesh):
    n_leaf = mesh.shape["leaf"]
    n_grp = mesh.shape["grp"]
    placed = (
        P("leaf", "grp", None),
        P("leaf", None, None),
        P(),
        P(),
        P("leaf", "grp", None, None),
        P("leaf", None, None),
        P(),
        P(),
        P("leaf", "grp", None, None),
        P("leaf", "grp"),
        P("leaf", "grp"),
        P("leaf", "grp"),
        P("leaf", "grp", None),
        P(("leaf", "grp"), None),
    )
    return jax.shard_map(
        functools.partial(body, n_leaf, n_grp),
        mesh=mesh,
        in_specs=placed,
        out_specs=(P("leaf", "grp", None), P("leaf", None, None), P(), P()),
        check_vma=False,
    )
```

```python
import functools

import jax
import jax.numpy as jnp
from jax import lax
from jax.experimental import pallas as pl
from jax.experimental.pallas import tpu as pltpu
from jax.sharding import PartitionSpec as P

BF = jnp.bfloat16
F32 = jnp.float32
MIB = 1024 * 1024
CHUNKS = 16
UNROLL = 4
HBM = pl.BlockSpec(memory_space=pltpu.HBM)
VMEM = pl.BlockSpec(memory_space=pltpu.VMEM)
BIG = 40 * MIB
SMALL = 6 * MIB


def in_hbm(*arrays):
    return [pltpu.with_memory_space_constraint(x, pltpu.HBM) for x in arrays]


def in_vmem(*arrays):
    return [pltpu.with_memory_space_constraint(x, pltpu.VMEM) for x in arrays]


def small(kernel, name, shapes, scratch, *args):
    return pl.pallas_call(
        kernel,
        out_shape=[pltpu.VMEM(shape, BF) for shape in shapes],
        in_specs=[VMEM] * len(args),
        out_specs=[VMEM] * len(shapes),
        scratch_shapes=scratch,
        compiler_params=pltpu.CompilerParams(vmem_limit_bytes=SMALL),
        name=name,
    )(*in_vmem(*args))


def dot(a, b):
    return jnp.dot(a, b, preferred_element_type=F32)


def place():
    g = lax.axis_index("grp")
    return lax.axis_index("leaf"), g >> 1, g & 1


def forward_kernel(
    sec,
    group_cols,
    count_hbm,
    cols_hbm,
    tgts_hbm,
    rhs_hbm,
    inv_hbm,
    tiles_hbm,
    keep,
    send,
    solved_hbm,
    dense_hbm,
    count,
    cols,
    tgts,
    rhs,
    inv,
    tiles,
    acc,
    stage,
    solved,
    dense,
    in_sems,
    tile_sems,
    out_sems,
):
    slots, block, _ = tiles.shape
    supernodes = inv.shape[0]
    targets = acc.shape[0]
    chunks = tile_sems.shape[0]
    step = slots // chunks
    _, _, core = place()

    def tile_copy(k):
        span = pl.ds(k * step, step)
        return pltpu.make_async_copy(tiles_hbm.at[span], tiles.at[span], tile_sems.at[k])

    pairs = (
        (count_hbm, count),
        (cols_hbm, cols),
        (tgts_hbm, tgts),
        (rhs_hbm, rhs),
        (inv_hbm, inv),
    )
    loads = [pltpu.make_async_copy(a, b, in_sems.at[i]) for i, (a, b) in enumerate(pairs)]
    for load in loads:
        load.start()
    for k in range(chunks):
        tile_copy(k).start()

    acc[...] = jnp.zeros_like(acc)
    for load in loads:
        load.wait()
    for s in range(supernodes):
        rows = pl.ds(s * block, block)
        solved[rows, :] = dot(inv[s], rhs[rows, :].astype(BF)).astype(BF)
    stores = [pltpu.make_async_copy(solved, solved_hbm, out_sems.at[0])]
    stores[0].start()

    live = count[0, 0]

    def add(p):
        t = tgts[0, p]
        c = cols[0, p]
        acc[t, c] = acc[t, c] + tiles[p].astype(F32)

    def add_some(i, carry):
        for u in range(UNROLL):
            add(i * UNROLL + u)
        return carry

    def add_one(p, carry):
        add(p)
        return carry

    whole = live // UNROLL
    per = step // UNROLL
    for k in range(chunks):
        tile_copy(k).wait()
        lax.fori_loop(k * per, jnp.clip(whole, k * per, (k + 1) * per), add_some, 0)
    lax.fori_loop(whole * UNROLL, live, add_one, 0)

    span = group_cols
    blocks = span // block
    for i in range(targets // blocks):
        for t in range(i * blocks, (i + 1) * blocks):
            for c in range(supernodes):
                dense[t * block : (t + 1) * block, c * block : (c + 1) * block] = acc[t, c].astype(BF)
        rows = pl.ds(i * span, span)
        stores.append(pltpu.make_async_copy(dense.at[rows], dense_hbm.at[rows], out_sems.at[1 + i]))
        stores[-1].start()
        total = dot(dense[rows, :], solved[...]).astype(BF)
        if i == 0:
            stage[0, 0:span, :] = total
            stage[1, 0:span, :] = total
        else:
            for q in range(0, span, sec):
                section = ((i - 1) * span + q) // sec
                begin = group_cols + (section // 2) * sec
                stage[(section % 2) ^ core, begin : begin + sec, :] = total[q : q + sec, :]
    keep[...] = stage[0]
    send[...] = stage[1]
    for store in stores:
        store.wait()


def leaf_forward(rhs, inverse, tiles, cols, tgts, count, sec, group_cols, upper_cols):
    slots, block, _ = tiles.shape
    supernodes = inverse.shape[0]
    targets = (group_cols + upper_cols) // block
    width = rhs.shape[-1]
    half = group_cols + upper_cols // 2
    return pl.pallas_call(
        functools.partial(forward_kernel, sec, group_cols),
        out_shape=(
            pltpu.VMEM((half, width), BF),
            pltpu.VMEM((half, width), BF),
            pltpu.HBM((supernodes * block, width), BF),
            pltpu.HBM((targets * block, supernodes * block), BF),
        ),
        in_specs=[HBM] * 6,
        out_specs=(VMEM, VMEM, HBM, HBM),
        scratch_shapes=[
            pltpu.SMEM(count.shape, count.dtype),
            pltpu.SMEM(cols.shape, cols.dtype),
            pltpu.SMEM(tgts.shape, tgts.dtype),
            pltpu.VMEM(rhs.shape, rhs.dtype),
            pltpu.VMEM(inverse.shape, inverse.dtype),
            pltpu.VMEM((slots, block, block), BF),
            pltpu.VMEM((targets, supernodes, block, block), F32),
            pltpu.VMEM((2, half, width), BF),
            pltpu.VMEM((supernodes * block, width), BF),
            pltpu.VMEM((targets * block, supernodes * block), BF),
            pltpu.SemaphoreType.DMA((5,)),
            pltpu.SemaphoreType.DMA((CHUNKS,)),
            pltpu.SemaphoreType.DMA((1 + targets * block // group_cols,)),
        ],
        compiler_params=pltpu.CompilerParams(vmem_limit_bytes=BIG),
        cost_estimate=pl.CostEstimate(
            flops=2 * targets * block * supernodes * block * width,
            bytes_accessed=2 * tiles.size + 4 * rhs.size,
            transcendentals=0,
        ),
        name="leaf_forward",
    )(count, *in_hbm(cols, tgts, rhs, inverse, tiles))


def total_of(refs):
    total = refs[0][...].astype(F32)
    for ref in refs[1:]:
        total = total + ref[...].astype(F32)
    return total


def fold_kernel(n_leaf, n_pos, keep, recv, inv, rhs, panel_hbm, *refs):
    parts, group, (gsum, stage, panel, sems) = refs[:n_leaf], refs[n_leaf], refs[n_leaf + 1 :]
    loads = [
        pltpu.make_async_copy(panel_hbm.at[p], panel.at[p], sems.at[p]) for p in range(n_pos)
    ]
    for load in loads:
        load.start()
    leaf, pos, core = place()
    group_cols = inv.shape[0]
    sec = panel.shape[1]
    q = sec // n_leaf
    gq = group_cols // (2 * n_pos)
    gsum[...] = keep[0:group_cols, :].astype(F32) + recv[0:group_cols, :].astype(F32)
    residual = rhs[...] * (1.0 / n_pos) - gsum[...]
    solved = dot(inv[...], residual.astype(BF)).astype(BF)
    for load in loads:
        load.wait()
    for k in range(n_pos):
        p = pos ^ k
        rows = pl.ds(pl.multiple_of(group_cols + p * sec, sec), sec)
        terms = dot(panel[p], solved)
        terms = (terms + (keep[rows, :].astype(F32) + recv[rows, :].astype(F32))).astype(BF)
        for j in range(n_leaf):
            stage[j ^ leaf, k * q : (k + 1) * q, :] = terms[j * q : (j + 1) * q, :]
        begin = pl.multiple_of(core * (group_cols // 2) + p * gq, gq)
        group[k * gq : (k + 1) * gq, :] = gsum[pl.ds(begin, gq), :].astype(BF)
    for k in range(n_leaf):
        parts[k][...] = stage[k]


def fold(keep, recv, inverse, rhs, panel, n_leaf):
    width = rhs.shape[-1]
    n_pos, sec, _ = panel.shape
    part = (n_pos * sec // n_leaf, width)
    outs = pl.pallas_call(
        functools.partial(fold_kernel, n_leaf, n_pos),
        out_shape=[pltpu.VMEM(part, BF)] * n_leaf
        + [pltpu.VMEM((inverse.shape[0] // 2, width), BF)],
        in_specs=[VMEM] * 4 + [HBM],
        out_specs=[VMEM] * (n_leaf + 1),
        scratch_shapes=[
            pltpu.VMEM(rhs.shape, F32),
            pltpu.VMEM((n_leaf,) + part, BF),
            pltpu.VMEM(panel.shape, BF),
            pltpu.SemaphoreType.DMA((n_pos,)),
        ],
        compiler_params=pltpu.CompilerParams(vmem_limit_bytes=SMALL),
        name="fold_group",
    )(*in_vmem(keep, recv, inverse, rhs), *in_hbm(panel))
    return list(outs[:n_leaf]), outs[n_leaf]


def sum_leaf_kernel(n_leaf, *refs):
    group, outs = refs[n_leaf], refs[n_leaf + 1 :]
    n_pos = len(outs)
    q = refs[0].shape[0] // n_pos
    gq = group.shape[0] // n_pos
    total = total_of(refs[:n_leaf]).astype(BF)
    for k, out in enumerate(outs):
        out[0:q, :] = total[k * q : (k + 1) * q, :]
        out[q:, :] = group[k * gq : (k + 1) * gq, :]


def sum_leaf(parts, group, n_pos):
    rows = (parts[0].shape[0] + group.shape[0]) // n_pos
    kernel = functools.partial(sum_leaf_kernel, len(parts))
    shapes = [(rows, group.shape[1])] * n_pos
    return list(small(kernel, "sum_leaf", shapes, [], *parts, group))


def sum_pos_kernel(high, group, *refs):
    parts, out = refs[:-1], refs[-1]
    q = high.shape[0]
    total = total_of(parts)
    out[0:q, :] = (high[...] - total[0:q, :]).astype(BF)
    out[q:, :] = (group[...] - total[q:, :]).astype(BF)


def sum_pos(high, group, parts):
    return small(sum_pos_kernel, "sum_pos", [parts[0].shape], [], high, group, *parts)[0]


def stack_pos_kernel(q, *refs):
    parts, (uppers, groups) = refs[:-2], refs[-2:]
    gq = parts[0].shape[0] - q
    for k, part in enumerate(parts):
        uppers[k * q : (k + 1) * q, :] = part[0:q, :]
        groups[k * gq : (k + 1) * gq, :] = part[q:, :]


def stack_pos(parts, q):
    n_pos, (rows, width) = len(parts), parts[0].shape
    shapes = [(n_pos * q, width), (n_pos * (rows - q), width)]
    return small(functools.partial(stack_pos_kernel, q), "stack_pos", shapes, [], *parts)


def stack_kernel(*refs):
    begin = 0
    for part in refs[:-1]:
        rows = part.shape[0]
        refs[-1][begin : begin + rows, :] = part[...]
        begin += rows


def stack(parts):
    rows = sum(part.shape[0] for part in parts)
    return small(stack_kernel, "stack", [(rows, parts[0].shape[1])], [], *parts)[0]


def weave_kernel(n_leaf, n_pos, own, other, out):
    leaf, pos, core = place()
    rows = own.shape[0] // (n_leaf * n_pos)
    for kc, part in enumerate((own, other)):
        for kl in range(n_leaf):
            for k in range(n_pos):
                block = (leaf ^ kl) * (2 * n_pos) + 2 * (pos ^ k) + (core ^ kc)
                span = pl.ds(pl.multiple_of(block * rows, rows), rows)
                begin = (kl * n_pos + k) * rows
                out[span, :] = part[begin : begin + rows, :]


def weave(own, other, n_leaf, n_pos):
    shape = (2 * own.shape[0], own.shape[1])
    kernel = functools.partial(weave_kernel, n_leaf, n_pos)
    return small(kernel, "weave", [shape], [], own, other)[0]


def backward_kernel(
    n_leaf,
    n_pos,
    mine,
    theirs,
    inv_mid,
    panel_mid,
    inv_top_hbm,
    inv_group_hbm,
    panel_own_hbm,
    panel_other_hbm,
    leaf_solved_hbm,
    inv_leaf_hbm,
    dense_hbm,
    leaf_hbm,
    group_hbm,
    mid_hbm,
    top_hbm,
    inv_top,
    inv_group,
    panel_group,
    leaf_solved,
    inv_leaf,
    dense,
    leaf_out,
    group_out,
    mid_out,
    top_out,
    upper,
    residual,
    above,
    sems,
    panel_sems,
    out_sems,
):
    leaf, pos, core = place()
    pairs = (
        (inv_top_hbm, inv_top),
        (inv_group_hbm, inv_group),
        (leaf_solved_hbm, leaf_solved),
        (inv_leaf_hbm, inv_leaf),
        (dense_hbm, dense),
    )
    loads = [pltpu.make_async_copy(a, b, sems.at[i]) for i, (a, b) in enumerate(pairs)]
    for kc, got in enumerate((panel_own_hbm, panel_other_hbm)):
        target = panel_group.at[:, core ^ kc]
        loads.append(pltpu.make_async_copy(got, target, panel_sems.at[kc]))
    for i in (0, 1, 5, 6, 2, 3, 4):
        loads[i].start()
    mid_rows = inv_mid.shape[0]
    top_rows = inv_top.shape[0]
    group_rows = inv_group.shape[0]
    supernodes, block, _ = inv_leaf.shape
    upper_cols = pl.ds(group_rows, mid_rows + top_rows)
    mid_cols = pl.ds(group_rows, mid_rows)
    top_cols = pl.ds(group_rows + mid_rows, top_rows)
    sec = (mid_rows + top_rows) // (2 * n_pos)
    q = sec // n_leaf
    gq = group_rows // (2 * n_pos)
    for kc, got in enumerate((mine, theirs)):
        for kz in range(n_pos):
            for kl in range(n_leaf):
                row = sec * (2 * (pos ^ kz) + (core ^ kc)) + q * (leaf ^ kl)
                begin = (kl * n_pos + kz) * q
                upper[pl.ds(pl.multiple_of(row, q), q), :] = got[begin : begin + q, :]
            row = (group_rows // 2) * (core ^ kc) + gq * (pos ^ kz)
            begin = n_leaf * n_pos * q + kz * gq
            residual[pl.ds(pl.multiple_of(row, gq), gq), :] = got[begin : begin + gq, :]

    mid_solved = dot(inv_mid[...], upper[0:mid_rows, :]).astype(BF)
    top_residual = upper[mid_rows:, :].astype(F32) - dot(panel_mid[...], mid_solved)
    loads[0].wait()
    top_solved = dot(inv_top[...], top_residual.astype(BF))
    top_t = dot(top_solved.T.astype(BF), inv_top[...])
    above[:, top_cols] = top_t.astype(BF)
    top_out[...] = top_t.T
    stores = [pltpu.make_async_copy(top_out, top_hbm, out_sems.at[0])]
    stores[0].start()
    mid_back = mid_solved.astype(F32).T - dot(above[:, top_cols], panel_mid[...])
    mid_t = dot(mid_back.astype(BF), inv_mid[...])
    above[:, mid_cols] = mid_t.astype(BF)
    mid_out[...] = mid_t.T
    stores.append(pltpu.make_async_copy(mid_out, mid_hbm, out_sems.at[1]))
    stores[1].start()
    for load in loads[1:]:
        load.wait()
    group_solved = dot(inv_group[...], residual[...]).astype(BF).astype(F32).T
    panel = panel_group[...].reshape(mid_rows + top_rows, group_rows)
    group_back = group_solved - dot(above[:, upper_cols], panel)
    group_t = dot(group_back.astype(BF), inv_group[...])
    above[:, 0:group_rows] = group_t.astype(BF)
    group_out[...] = group_t.T
    stores.append(pltpu.make_async_copy(group_out, group_hbm, out_sems.at[2]))
    stores[2].start()
    for s in range(supernodes):
        cols = pl.ds(s * block, block)
        terms = dot(above[...], dense[:, cols])
        back = (leaf_solved[cols, :].astype(F32).T - terms).astype(BF)
        leaf_out[cols, :] = dot(back, inv_leaf[s]).T
    stores.append(pltpu.make_async_copy(leaf_out, leaf_hbm, out_sems.at[3]))
    stores[3].start()
    for store in stores:
        store.wait()


def backward(close, far, n_leaf, n_pos):
    mine, _, inv_mid, _ = close
    inv_top, inv_group, panel, _, leaf_solved, inv_leaf, dense = far
    width = mine.shape[-1]
    held = (inv_top.shape, inv_group.shape, (n_pos, 2) + panel.shape[1:])
    held += (leaf_solved.shape, inv_leaf.shape, dense.shape)
    outs = (
        leaf_solved.shape,
        (inv_group.shape[0], width),
        (inv_mid.shape[0], width),
        (inv_top.shape[0], width),
    )
    return pl.pallas_call(
        functools.partial(backward_kernel, n_leaf, n_pos),
        out_shape=[pltpu.HBM(shape, F32) for shape in outs],
        in_specs=[VMEM] * len(close) + [HBM] * len(far),
        out_specs=[HBM] * 4,
        scratch_shapes=[pltpu.VMEM(shape, BF) for shape in held]
        + [pltpu.VMEM(shape, F32) for shape in outs]
        + [
            pltpu.VMEM((inv_mid.shape[0] + inv_top.shape[0], width), BF),
            pltpu.VMEM((inv_group.shape[0], width), BF),
            pltpu.VMEM((width, dense.shape[0]), BF),
            pltpu.SemaphoreType.DMA((5,)),
            pltpu.SemaphoreType.DMA((2,)),
            pltpu.SemaphoreType.DMA((len(outs),)),
        ],
        compiler_params=pltpu.CompilerParams(vmem_limit_bytes=BIG),
        name="backward",
    )(*in_vmem(*close), *in_hbm(*far))


def swap(x, axis, size, bits):
    return lax.ppermute(x, axis, [(i, i ^ bits) for i in range(size)])


def swaps(x, axis, size, unit=1):
    return [x] + [swap(x, axis, size, unit * k) for k in range(1, size // unit)]


def after(x, *others):
    return lax.optimization_barrier((x, others))[0]


def body(
    n_leaf,
    n_grp,
    rhs_leaf,
    rhs_group,
    rhs_middle,
    rhs_top,
    inv_leaf,
    inv_group,
    inv_middle,
    inv_top,
    leaf_tiles,
    tile_column,
    tile_target,
    tile_count,
    group_panel,
    middle_panel,
):
    n_pos = n_grp // 2
    group_cols = rhs_group.shape[1]
    mid_cols = rhs_middle.shape[0]
    upper_cols = mid_cols + rhs_top.shape[0]
    sec = upper_cols // n_grp
    q = sec // n_leaf
    gq = group_cols // n_grp
    leaf, pos, core = place()
    by_parts = middle_panel.shape[0] % 16 == 0
    pos_groups = [[2 * p + c for p in range(n_pos)] for c in range(2)]
    with jax.named_scope("gather_group_panel"):
        panel = lax.all_gather(group_panel[0], "grp", axis_index_groups=pos_groups)
    with jax.named_scope("gather_middle_panel"):
        if by_parts:
            middles = swaps(middle_panel, "grp", n_grp, 2)
        else:
            middle = lax.all_gather(middle_panel, ("leaf", "grp"), axis=0, tiled=True)
    begin = sec * lax.axis_index("grp") + q * leaf
    low = lax.dynamic_slice_in_dim(rhs_middle, jnp.minimum(begin, mid_cols - q), q, 0)
    high = lax.dynamic_slice_in_dim(rhs_top, jnp.maximum(begin - mid_cols, 0), q, 0)
    rhs_mine = jnp.where(begin < mid_cols, low, high)
    group_begin = (group_cols // 2) * core + gq * pos
    group_mine = lax.dynamic_slice_in_dim(rhs_group[0], group_begin, gq, 0)
    keep, send, leaf_solved, dense = leaf_forward(
        rhs_leaf[0],
        inv_leaf[0],
        leaf_tiles[0],
        tile_column,
        tile_target,
        tile_count,
        sec,
        group_cols,
        upper_cols,
    )
    with jax.named_scope("swap_cores"):
        if by_parts:
            send = after(send, middles)
        recv = swap(send, "grp", n_grp, 1)
    with jax.named_scope("gather_middle_panel"):
        if by_parts:
            middles = swaps(stack(after(middles, send)), "leaf", n_leaf)
            recv = after(recv, (middles, rhs_mine, group_mine))
            middle = stack(middles)
    parts, group = fold(keep, recv, inv_group[0], rhs_group[0], panel, n_leaf)
    with jax.named_scope("sum_over_leaf"):
        parts = parts[:1] + [swap(parts[k], "leaf", n_leaf, k) for k in range(1, n_leaf)]
    with jax.named_scope("gather_middle_panel"):
        if by_parts:
            middle = weave(middle, swap(middle, "grp", n_grp, 1), n_leaf, n_pos)
    sends = sum_leaf(after(parts, middle), group, n_pos)
    with jax.named_scope("sum_over_pos"):
        got = sends[:1] + [swap(sends[k], "grp", n_grp, 2 * k) for k in range(1, n_pos)]
    with jax.named_scope("swap_group_panel"):
        panel_other = swap(panel, "grp", n_grp, 1)
    residual = sum_pos(rhs_mine, group_mine, got)
    with jax.named_scope("gather_pos"):
        uppers, groups = stack_pos(swaps(residual, "grp", n_grp, 2), q)
    with jax.named_scope("gather_leaf"):
        stacks = swaps(uppers, "leaf", n_leaf)
    with jax.named_scope("gather_cores"):
        mine = stack(after(stacks, panel_other) + [groups])
        theirs = swap(mine, "grp", n_grp, 1)
    leaf_out, group_out, mid_out, top_out = backward(
        (mine, theirs, inv_middle, middle),
        (inv_top, inv_group[0], panel, panel_other, leaf_solved, inv_leaf[0], dense),
        n_leaf,
        n_pos,
    )
    return leaf_out[None], group_out[None], mid_out, top_out


def solution(mesh):
    n_leaf = mesh.shape["leaf"]
    n_grp = mesh.shape["grp"]
    placed = (
        P("leaf", "grp", None),
        P("leaf", None, None),
        P(),
        P(),
        P("leaf", "grp", None, None),
        P("leaf", None, None),
        P(),
        P(),
        P("leaf", "grp", None, None),
        P("leaf", "grp"),
        P("leaf", "grp"),
        P("leaf", "grp"),
        P("leaf", "grp", None),
        P(("leaf", "grp"), None),
    )
    return jax.shard_map(
        functools.partial(body, n_leaf, n_grp),
        mesh=mesh,
        in_specs=placed,
        out_specs=(P("leaf", "grp", None), P("leaf", None, None), P(), P()),
        check_vma=False,
    )
```

```python
import functools

import jax
import jax.numpy as jnp
from jax import lax
from jax.experimental import pallas as pl
from jax.experimental.pallas import tpu as pltpu
from jax.sharding import PartitionSpec as P

BF = jnp.bfloat16
F32 = jnp.float32
MIB = 1024 * 1024
CHUNKS = 16
UNROLL = 4
HBM = pl.BlockSpec(memory_space=pltpu.HBM)
VMEM = pl.BlockSpec(memory_space=pltpu.VMEM)
BIG = 40 * MIB
SMALL = 8 * MIB


def in_hbm(*arrays):
    return [pltpu.with_memory_space_constraint(x, pltpu.HBM) for x in arrays]


def in_vmem(*arrays):
    return [pltpu.with_memory_space_constraint(x, pltpu.VMEM) for x in arrays]


def small(kernel, name, shapes, scratch, *args):
    return pl.pallas_call(
        kernel,
        out_shape=[pltpu.VMEM(shape, BF) for shape in shapes],
        in_specs=[VMEM] * len(args),
        out_specs=[VMEM] * len(shapes),
        scratch_shapes=scratch,
        compiler_params=pltpu.CompilerParams(vmem_limit_bytes=SMALL),
        name=name,
    )(*in_vmem(*args))


def dot(a, b):
    return jnp.dot(a, b, preferred_element_type=F32)


def place():
    g = lax.axis_index("grp")
    return lax.axis_index("leaf"), g >> 1, g & 1


def forward_kernel(
    sec,
    group_cols,
    count_hbm,
    cols_hbm,
    tgts_hbm,
    rhs_hbm,
    inv_hbm,
    tiles_hbm,
    keep,
    send,
    solved_hbm,
    dense_hbm,
    count,
    cols,
    tgts,
    rhs,
    inv,
    tiles,
    acc,
    stage,
    solved,
    dense,
    in_sems,
    tile_sems,
    out_sems,
):
    slots, block, _ = tiles.shape
    supernodes = inv.shape[0]
    targets = acc.shape[0]
    chunks = tile_sems.shape[0]
    step = slots // chunks
    _, _, core = place()

    def tile_copy(k):
        span = pl.ds(k * step, step)
        return pltpu.make_async_copy(tiles_hbm.at[span], tiles.at[span], tile_sems.at[k])

    pairs = (
        (count_hbm, count),
        (cols_hbm, cols),
        (tgts_hbm, tgts),
        (rhs_hbm, rhs),
        (inv_hbm, inv),
    )
    loads = [pltpu.make_async_copy(a, b, in_sems.at[i]) for i, (a, b) in enumerate(pairs)]
    for load in loads:
        load.start()
    for k in range(chunks):
        tile_copy(k).start()

    acc[...] = jnp.zeros_like(acc)
    for load in loads:
        load.wait()
    for s in range(supernodes):
        rows = pl.ds(s * block, block)
        solved[rows, :] = dot(inv[s], rhs[rows, :].astype(BF)).astype(BF)
    stores = [pltpu.make_async_copy(solved, solved_hbm, out_sems.at[0])]
    stores[0].start()

    live = count[0, 0]

    def add(p):
        t = tgts[0, p]
        c = cols[0, p]
        acc[t, c] = acc[t, c] + tiles[p].astype(F32)

    def add_some(i, carry):
        for u in range(UNROLL):
            add(i * UNROLL + u)
        return carry

    def add_one(p, carry):
        add(p)
        return carry

    whole = live // UNROLL
    per = step // UNROLL
    for k in range(chunks):
        tile_copy(k).wait()
        lax.fori_loop(k * per, jnp.clip(whole, k * per, (k + 1) * per), add_some, 0)
    lax.fori_loop(whole * UNROLL, live, add_one, 0)

    span = group_cols
    blocks = span // block
    for i in range(targets // blocks):
        for t in range(i * blocks, (i + 1) * blocks):
            for c in range(supernodes):
                dense[t * block : (t + 1) * block, c * block : (c + 1) * block] = acc[t, c].astype(BF)
        rows = pl.ds(i * span, span)
        stores.append(pltpu.make_async_copy(dense.at[rows], dense_hbm.at[rows], out_sems.at[1 + i]))
        stores[-1].start()
        total = dot(dense[rows, :], solved[...]).astype(BF)
        if i == 0:
            stage[0, 0:span, :] = total
            stage[1, 0:span, :] = total
        else:
            for q in range(0, span, sec):
                section = ((i - 1) * span + q) // sec
                begin = group_cols + (section // 2) * sec
                stage[(section % 2) ^ core, begin : begin + sec, :] = total[q : q + sec, :]
    keep[...] = stage[0]
    send[...] = stage[1]
    for store in stores:
        store.wait()


def leaf_forward(rhs, inverse, tiles, cols, tgts, count, sec, group_cols, upper_cols):
    slots, block, _ = tiles.shape
    supernodes = inverse.shape[0]
    targets = (group_cols + upper_cols) // block
    width = rhs.shape[-1]
    half = group_cols + upper_cols // 2
    return pl.pallas_call(
        functools.partial(forward_kernel, sec, group_cols),
        out_shape=(
            pltpu.VMEM((half, width), BF),
            pltpu.VMEM((half, width), BF),
            pltpu.HBM((supernodes * block, width), BF),
            pltpu.HBM((targets * block, supernodes * block), BF),
        ),
        in_specs=[HBM] * 6,
        out_specs=(VMEM, VMEM, HBM, HBM),
        scratch_shapes=[
            pltpu.SMEM(count.shape, count.dtype),
            pltpu.SMEM(cols.shape, cols.dtype),
            pltpu.SMEM(tgts.shape, tgts.dtype),
            pltpu.VMEM(rhs.shape, rhs.dtype),
            pltpu.VMEM(inverse.shape, inverse.dtype),
            pltpu.VMEM((slots, block, block), BF),
            pltpu.VMEM((targets, supernodes, block, block), F32),
            pltpu.VMEM((2, half, width), BF),
            pltpu.VMEM((supernodes * block, width), BF),
            pltpu.VMEM((targets * block, supernodes * block), BF),
            pltpu.SemaphoreType.DMA((5,)),
            pltpu.SemaphoreType.DMA((CHUNKS,)),
            pltpu.SemaphoreType.DMA((1 + targets * block // group_cols,)),
        ],
        compiler_params=pltpu.CompilerParams(vmem_limit_bytes=BIG),
        name="leaf_forward",
    )(count, *in_hbm(cols, tgts, rhs, inverse, tiles))


def total_of(refs):
    total = refs[0][...].astype(F32)
    for ref in refs[1:]:
        total = total + ref[...].astype(F32)
    return total


def fold_kernel(n_leaf, n_pos, keep, recv, inv, rhs, panel, *refs):
    parts, group, (gsum, stage) = refs[:n_leaf], refs[n_leaf], refs[n_leaf + 1 :]
    leaf, pos, core = place()
    group_cols = inv.shape[0]
    sec = panel.shape[1]
    q = sec // n_leaf
    gq = group_cols // (2 * n_pos)
    gsum[...] = keep[0:group_cols, :].astype(F32) + recv[0:group_cols, :].astype(F32)
    residual = rhs[...] * (1.0 / n_pos) - gsum[...]
    solved = dot(inv[...], residual.astype(BF)).astype(BF)
    for k in range(n_pos):
        p = pos ^ k
        rows = pl.ds(pl.multiple_of(group_cols + p * sec, sec), sec)
        terms = dot(panel[p], solved)
        terms = (terms + (keep[rows, :].astype(F32) + recv[rows, :].astype(F32))).astype(BF)
        for j in range(n_leaf):
            stage[j ^ leaf, k * q : (k + 1) * q, :] = terms[j * q : (j + 1) * q, :]
        begin = pl.multiple_of(core * (group_cols // 2) + p * gq, gq)
        group[k * gq : (k + 1) * gq, :] = gsum[pl.ds(begin, gq), :].astype(BF)
    for k in range(n_leaf):
        parts[k][...] = stage[k]


def fold(keep, recv, inverse, rhs, panel, n_leaf):
    width = rhs.shape[-1]
    n_pos, sec, _ = panel.shape
    part = (n_pos * sec // n_leaf, width)
    outs = small(
        functools.partial(fold_kernel, n_leaf, n_pos),
        "fold_group",
        [part] * n_leaf + [(inverse.shape[0] // 2, width)],
        [pltpu.VMEM(rhs.shape, F32), pltpu.VMEM((n_leaf,) + part, BF)],
        keep,
        recv,
        inverse,
        rhs,
        panel,
    )
    return list(outs[:n_leaf]), outs[n_leaf]


def sum_leaf_kernel(n_leaf, *refs):
    group, outs = refs[n_leaf], refs[n_leaf + 1 :]
    n_pos = len(outs)
    q = refs[0].shape[0] // n_pos
    gq = group.shape[0] // n_pos
    total = total_of(refs[:n_leaf]).astype(BF)
    for k, out in enumerate(outs):
        out[0:q, :] = total[k * q : (k + 1) * q, :]
        out[q:, :] = group[k * gq : (k + 1) * gq, :]


def sum_leaf(parts, group, n_pos):
    rows = (parts[0].shape[0] + group.shape[0]) // n_pos
    kernel = functools.partial(sum_leaf_kernel, len(parts))
    shapes = [(rows, group.shape[1])] * n_pos
    return list(small(kernel, "sum_leaf", shapes, [], *parts, group))


def sum_pos_kernel(high, group, *refs):
    parts, out = refs[:-1], refs[-1]
    q = high.shape[0]
    total = total_of(parts)
    out[0:q, :] = (high[...] - total[0:q, :]).astype(BF)
    out[q:, :] = (group[...] - total[q:, :]).astype(BF)


def sum_pos(high, group, parts):
    return small(sum_pos_kernel, "sum_pos", [parts[0].shape], [], high, group, *parts)[0]


def stack_pos_kernel(q, *refs):
    parts, (uppers, groups) = refs[:-2], refs[-2:]
    gq = parts[0].shape[0] - q
    for k, part in enumerate(parts):
        uppers[k * q : (k + 1) * q, :] = part[0:q, :]
        groups[k * gq : (k + 1) * gq, :] = part[q:, :]


def stack_pos(parts, q):
    n_pos, (rows, width) = len(parts), parts[0].shape
    shapes = [(n_pos * q, width), (n_pos * (rows - q), width)]
    return small(functools.partial(stack_pos_kernel, q), "stack_pos", shapes, [], *parts)


def stack_kernel(*refs):
    begin = 0
    for part in refs[:-1]:
        rows = part.shape[0]
        refs[-1][begin : begin + rows, :] = part[...]
        begin += rows


def stack(parts):
    rows = sum(part.shape[0] for part in parts)
    return small(stack_kernel, "stack", [(rows, parts[0].shape[1])], [], *parts)[0]


def turn(source, target):
    rows, cols = source.shape
    step = min(256, rows)
    for i in range(0, rows, step):
        for j in range(0, cols, step):
            target[j : j + step, i : i + step] = source[i : i + step, j : j + step].T


def weave_kernel(n_leaf, n_pos, own, other, out, out_t):
    leaf, pos, core = place()
    rows = own.shape[0] // (n_leaf * n_pos)
    for kc, part in enumerate((own, other)):
        for kl in range(n_leaf):
            for k in range(n_pos):
                block = (leaf ^ kl) * (2 * n_pos) + 2 * (pos ^ k) + (core ^ kc)
                span = pl.ds(pl.multiple_of(block * rows, rows), rows)
                begin = (kl * n_pos + k) * rows
                out[span, :] = part[begin : begin + rows, :]
    turn(out, out_t)


def weave(own, other, n_leaf, n_pos):
    shape = (2 * own.shape[0], own.shape[1])
    kernel = functools.partial(weave_kernel, n_leaf, n_pos)
    return small(kernel, "weave", [shape, shape[::-1]], [], own, other)


def weave_group_kernel(own, other, out_t, both, sems):
    _, _, core = place()
    n_pos, sec, cols = own.shape
    loads = []
    for kc, got in enumerate((own, other)):
        for p in range(n_pos):
            begin = pl.multiple_of((2 * p + (core ^ kc)) * sec, sec)
            target = both.at[pl.ds(begin, sec)]
            sem = sems.at[kc * n_pos + p]
            loads.append(pltpu.make_async_copy(got.at[p], target, sem))
    for load in loads:
        load.start()
    for load in loads:
        load.wait()
    turn(both, out_t)


def weave_group(own, other):
    n_pos, sec, cols = own.shape
    rows = 2 * n_pos * sec
    return pl.pallas_call(
        weave_group_kernel,
        out_shape=pltpu.VMEM((cols, rows), BF),
        in_specs=[HBM] * 2,
        out_specs=VMEM,
        scratch_shapes=[
            pltpu.VMEM((rows, cols), BF),
            pltpu.SemaphoreType.DMA((2 * n_pos,)),
        ],
        compiler_params=pltpu.CompilerParams(vmem_limit_bytes=SMALL),
        cost_estimate=pl.CostEstimate(
            flops=0, bytes_accessed=6 * rows * cols, transcendentals=0
        ),
        name="weave_group",
    )(*in_hbm(own, other))


def turned_kernel(source_hbm, target, source, sem):
    load = pltpu.make_async_copy(source_hbm, source, sem)
    load.start()
    load.wait()
    turn(source, target)


def turned(x, name):
    return pl.pallas_call(
        turned_kernel,
        out_shape=pltpu.VMEM(x.shape[::-1], BF),
        in_specs=[HBM],
        out_specs=VMEM,
        scratch_shapes=[pltpu.VMEM(x.shape, BF), pltpu.SemaphoreType.DMA],
        compiler_params=pltpu.CompilerParams(vmem_limit_bytes=BIG // 2),
        cost_estimate=pl.CostEstimate(flops=1, bytes_accessed=1, transcendentals=0),
        name=name,
    )(*in_hbm(x))


def backward_kernel(
    n_leaf,
    n_pos,
    mine,
    theirs,
    inv_mid,
    inv_mid_t,
    inv_top_t,
    inv_group_t,
    panel_mid,
    panel_mid_t,
    panel_group_t,
    dense_t,
    inv_top_hbm,
    inv_group_hbm,
    leaf_solved_hbm,
    inv_leaf_hbm,
    leaf_hbm,
    group_hbm,
    mid_hbm,
    top_hbm,
    inv_top,
    inv_group,
    leaf_solved,
    inv_leaf,
    leaf_out,
    group_out,
    mid_out,
    top_out,
    upper,
    residual,
    above,
    sems,
    out_sems,
):
    leaf, pos, core = place()
    pairs = (
        (inv_top_hbm, inv_top),
        (inv_group_hbm, inv_group),
        (leaf_solved_hbm, leaf_solved),
        (inv_leaf_hbm, inv_leaf),
    )
    loads = [pltpu.make_async_copy(a, b, sems.at[i]) for i, (a, b) in enumerate(pairs)]
    for load in loads:
        load.start()
    mid_rows = inv_mid.shape[0]
    top_rows = inv_top.shape[0]
    group_rows = inv_group.shape[0]
    supernodes, block, _ = inv_leaf.shape
    upper_span = pl.ds(group_rows, mid_rows + top_rows)
    mid_span = pl.ds(group_rows, mid_rows)
    top_span = pl.ds(group_rows + mid_rows, top_rows)
    sec = (mid_rows + top_rows) // (2 * n_pos)
    q = sec // n_leaf
    gq = group_rows // (2 * n_pos)
    for kc, got in enumerate((mine, theirs)):
        for kz in range(n_pos):
            for kl in range(n_leaf):
                row = sec * (2 * (pos ^ kz) + (core ^ kc)) + q * (leaf ^ kl)
                begin = (kl * n_pos + kz) * q
                upper[pl.ds(pl.multiple_of(row, q), q), :] = got[begin : begin + q, :]
            row = (group_rows // 2) * (core ^ kc) + gq * (pos ^ kz)
            begin = n_leaf * n_pos * q + kz * gq
            residual[pl.ds(pl.multiple_of(row, gq), gq), :] = got[begin : begin + gq, :]

    mid_solved = dot(inv_mid[...], upper[0:mid_rows, :]).astype(BF)
    top_residual = upper[mid_rows:, :].astype(F32) - dot(panel_mid[...], mid_solved)
    loads[0].wait()
    top_solved = dot(inv_top[...], top_residual.astype(BF)).astype(BF)
    top_out[...] = dot(inv_top_t[...], top_solved)
    above[top_span, :] = top_out[...].astype(BF)
    stores = [pltpu.make_async_copy(top_out, top_hbm, out_sems.at[0])]
    stores[0].start()
    mid_back = mid_solved.astype(F32) - dot(panel_mid_t[...], above[top_span, :])
    mid_out[...] = dot(inv_mid_t[...], mid_back.astype(BF))
    above[mid_span, :] = mid_out[...].astype(BF)
    stores.append(pltpu.make_async_copy(mid_out, mid_hbm, out_sems.at[1]))
    stores[1].start()
    for load in loads[1:]:
        load.wait()
    group_solved = dot(inv_group[...], residual[...]).astype(BF).astype(F32)
    group_back = group_solved - dot(panel_group_t[...], above[upper_span, :])
    group_out[...] = dot(inv_group_t[...], group_back.astype(BF))
    above[0:group_rows, :] = group_out[...].astype(BF)
    stores.append(pltpu.make_async_copy(group_out, group_hbm, out_sems.at[2]))
    stores[2].start()
    half = supernodes // 2
    for i in range(2):
        rows = pl.ds(i * half * block, half * block)
        terms = dot(dense_t[rows, :], above[...])
        back = (leaf_solved[rows, :].astype(F32) - terms).astype(BF)
        for s in range(half):
            span = pl.ds((i * half + s) * block, block)
            inverse_t = inv_leaf[i * half + s].T
            leaf_out[span, :] = dot(inverse_t, back[s * block : (s + 1) * block, :])
        stores.append(pltpu.make_async_copy(leaf_out.at[rows], leaf_hbm.at[rows], out_sems.at[3 + i]))
        stores[-1].start()
    for store in stores:
        store.wait()


def backward(close, far, n_leaf, n_pos):
    mine, inv_mid, dense_t = close[0], close[2], close[-1]
    inv_top, inv_group, leaf_solved, _ = far
    width = mine.shape[-1]
    outs = (
        leaf_solved.shape,
        (inv_group.shape[0], width),
        (inv_mid.shape[0], width),
        (inv_top.shape[0], width),
    )
    return pl.pallas_call(
        functools.partial(backward_kernel, n_leaf, n_pos),
        out_shape=[pltpu.HBM(shape, F32) for shape in outs],
        in_specs=[VMEM] * len(close) + [HBM] * len(far),
        out_specs=[HBM] * 4,
        scratch_shapes=[pltpu.VMEM(x.shape, BF) for x in far]
        + [pltpu.VMEM(shape, F32) for shape in outs]
        + [
            pltpu.VMEM((inv_mid.shape[0] + inv_top.shape[0], width), BF),
            pltpu.VMEM((inv_group.shape[0], width), BF),
            pltpu.VMEM((dense_t.shape[1], width), BF),
            pltpu.SemaphoreType.DMA((4,)),
            pltpu.SemaphoreType.DMA((5,)),
        ],
        compiler_params=pltpu.CompilerParams(vmem_limit_bytes=BIG // 2),
        name="backward",
    )(*in_vmem(*close), *in_hbm(*far))


def swap(x, axis, size, bits):
    return lax.ppermute(x, axis, [(i, i ^ bits) for i in range(size)])


def swaps(x, axis, size, unit=1):
    return [x] + [swap(x, axis, size, unit * k) for k in range(1, size // unit)]


def after(x, *others):
    return lax.optimization_barrier((x, others))[0]


def body(
    n_leaf,
    n_grp,
    rhs_leaf,
    rhs_group,
    rhs_middle,
    rhs_top,
    inv_leaf,
    inv_group,
    inv_middle,
    inv_top,
    leaf_tiles,
    tile_column,
    tile_target,
    tile_count,
    group_panel,
    middle_panel,
):
    n_pos = n_grp // 2
    group_cols = rhs_group.shape[1]
    mid_cols = rhs_middle.shape[0]
    upper_cols = mid_cols + rhs_top.shape[0]
    sec = upper_cols // n_grp
    q = sec // n_leaf
    gq = group_cols // n_grp
    leaf, pos, core = place()
    by_parts = middle_panel.shape[0] % 16 == 0
    pos_groups = [[2 * p + c for p in range(n_pos)] for c in range(2)]
    with jax.named_scope("gather_group_panel"):
        panel = lax.all_gather(group_panel[0], "grp", axis_index_groups=pos_groups)
    with jax.named_scope("gather_middle_panel"):
        if by_parts:
            middles = swaps(middle_panel, "grp", n_grp, 2)
        else:
            middle = lax.all_gather(middle_panel, ("leaf", "grp"), axis=0, tiled=True)
    begin = sec * lax.axis_index("grp") + q * leaf
    low = lax.dynamic_slice_in_dim(rhs_middle, jnp.minimum(begin, mid_cols - q), q, 0)
    high = lax.dynamic_slice_in_dim(rhs_top, jnp.maximum(begin - mid_cols, 0), q, 0)
    rhs_mine = jnp.where(begin < mid_cols, low, high)
    group_begin = (group_cols // 2) * core + gq * pos
    group_mine = lax.dynamic_slice_in_dim(rhs_group[0], group_begin, gq, 0)
    keep, send, leaf_solved, dense = leaf_forward(
        rhs_leaf[0],
        inv_leaf[0],
        leaf_tiles[0],
        tile_column,
        tile_target,
        tile_count,
        sec,
        group_cols,
        upper_cols,
    )
    with jax.named_scope("swap_cores"):
        if by_parts:
            send = after(send, middles)
        recv = swap(send, "grp", n_grp, 1)
    with jax.named_scope("gather_middle_panel"):
        if by_parts:
            middles = swaps(stack(after(middles, send)), "leaf", n_leaf)
            recv = after(recv, middles)
    turns = (
        turned(inv_middle, "turn_inv_middle"),
        turned(inv_top, "turn_inv_top"),
        turned(inv_group[0], "turn_inv_group"),
        turned(dense, "turn_dense"),
    )
    recv = after(recv, (turns, rhs_mine, group_mine))
    if by_parts:
        middle = stack(after(middles, (turns, rhs_mine, group_mine)))
        middle, panel = lax.optimization_barrier((middle, panel))
    parts, group = fold(keep, recv, inv_group[0], rhs_group[0], panel, n_leaf)
    with jax.named_scope("sum_over_leaf"):
        parts = parts[:1] + [swap(parts[k], "leaf", n_leaf, k) for k in range(1, n_leaf)]
    with jax.named_scope("gather_middle_panel"):
        if by_parts:
            middle, middle_t = weave(middle, swap(middle, "grp", n_grp, 1), n_leaf, n_pos)
        else:
            middle_t = turned(middle, "turn_middle")
    sends = sum_leaf(after(parts, middle), group, n_pos)
    with jax.named_scope("sum_over_pos"):
        got = sends[:1] + [swap(sends[k], "grp", n_grp, 2 * k) for k in range(1, n_pos)]
    with jax.named_scope("swap_group_panel"):
        panel_other = swap(after(panel, group), "grp", n_grp, 1)
    residual = sum_pos(rhs_mine, group_mine, got)
    with jax.named_scope("gather_pos"):
        uppers, groups = stack_pos(swaps(residual, "grp", n_grp, 2), q)
    with jax.named_scope("gather_leaf"):
        stacks = swaps(uppers, "leaf", n_leaf)
    panel_t = weave_group(panel, panel_other)
    with jax.named_scope("gather_cores"):
        mine = stack(after(stacks, panel_t) + [groups])
        theirs = swap(mine, "grp", n_grp, 1)
    leaf_out, group_out, mid_out, top_out = backward(
        (mine, theirs, inv_middle) + turns[:3] + (middle, middle_t, panel_t, turns[3]),
        (inv_top, inv_group[0], leaf_solved, inv_leaf[0]),
        n_leaf,
        n_pos,
    )
    return leaf_out[None], group_out[None], mid_out, top_out


def solution(mesh):
    n_leaf = mesh.shape["leaf"]
    n_grp = mesh.shape["grp"]
    placed = (
        P("leaf", "grp", None),
        P("leaf", None, None),
        P(),
        P(),
        P("leaf", "grp", None, None),
        P("leaf", None, None),
        P(),
        P(),
        P("leaf", "grp", None, None),
        P("leaf", "grp"),
        P("leaf", "grp"),
        P("leaf", "grp"),
        P("leaf", "grp", None),
        P(("leaf", "grp"), None),
    )
    return jax.shard_map(
        functools.partial(body, n_leaf, n_grp),
        mesh=mesh,
        in_specs=placed,
        out_specs=(P("leaf", "grp", None), P("leaf", None, None), P(), P()),
        check_vma=False,
    )
```

```python
import functools

import jax
import jax.numpy as jnp
from jax import lax
from jax.experimental import pallas as pl
from jax.experimental.pallas import tpu as pltpu
from jax.sharding import PartitionSpec as P

BF = jnp.bfloat16
F32 = jnp.float32
MIB = 1024 * 1024
CHUNKS = 16
UNROLL = 4
HBM = pl.BlockSpec(memory_space=pltpu.HBM)
VMEM = pl.BlockSpec(memory_space=pltpu.VMEM)
BIG = 40 * MIB
SMALL = 6 * MIB


def in_hbm(*arrays):
    return [pltpu.with_memory_space_constraint(x, pltpu.HBM) for x in arrays]


def in_vmem(*arrays):
    return [pltpu.with_memory_space_constraint(x, pltpu.VMEM) for x in arrays]


def small(kernel, name, shapes, scratch, *args):
    return pl.pallas_call(
        kernel,
        out_shape=[pltpu.VMEM(shape, BF) for shape in shapes],
        in_specs=[VMEM] * len(args),
        out_specs=[VMEM] * len(shapes),
        scratch_shapes=scratch,
        compiler_params=pltpu.CompilerParams(vmem_limit_bytes=SMALL),
        name=name,
    )(*in_vmem(*args))


def dot(a, b):
    return jnp.dot(a, b, preferred_element_type=F32)


def place():
    g = lax.axis_index("grp")
    return lax.axis_index("leaf"), g >> 1, g & 1


def forward_kernel(
    sec,
    group_cols,
    count_hbm,
    cols_hbm,
    tgts_hbm,
    rhs_hbm,
    inv_hbm,
    tiles_hbm,
    keep,
    send_low,
    send_high,
    solved_hbm,
    dense_hbm,
    count,
    cols,
    tgts,
    rhs,
    inv,
    tiles,
    acc,
    stage,
    solved,
    dense,
    in_sems,
    tile_sems,
    out_sems,
):
    slots, block, _ = tiles.shape
    supernodes = inv.shape[0]
    targets = acc.shape[0]
    chunks = tile_sems.shape[0]
    step = slots // chunks
    _, _, core = place()

    def tile_copy(k):
        span = pl.ds(k * step, step)
        return pltpu.make_async_copy(tiles_hbm.at[span], tiles.at[span], tile_sems.at[k])

    pairs = (
        (count_hbm, count),
        (cols_hbm, cols),
        (tgts_hbm, tgts),
        (rhs_hbm, rhs),
        (inv_hbm, inv),
    )
    loads = [pltpu.make_async_copy(a, b, in_sems.at[i]) for i, (a, b) in enumerate(pairs)]
    for load in loads:
        load.start()
    for k in range(chunks):
        tile_copy(k).start()

    acc[...] = jnp.zeros_like(acc)
    for load in loads:
        load.wait()
    for s in range(supernodes):
        rows = pl.ds(s * block, block)
        solved[rows, :] = dot(inv[s], rhs[rows, :].astype(BF)).astype(BF)
    stores = [pltpu.make_async_copy(solved, solved_hbm, out_sems.at[0])]
    stores[0].start()

    live = count[0, 0]

    def add(p):
        t = tgts[0, p]
        c = cols[0, p]
        acc[t, c] = acc[t, c] + tiles[p].astype(F32)

    def add_some(i, carry):
        for u in range(UNROLL):
            add(i * UNROLL + u)
        return carry

    def add_one(p, carry):
        add(p)
        return carry

    whole = live // UNROLL
    per = step // UNROLL
    for k in range(chunks):
        tile_copy(k).wait()
        lax.fori_loop(k * per, jnp.clip(whole, k * per, (k + 1) * per), add_some, 0)
    lax.fori_loop(whole * UNROLL, live, add_one, 0)

    span = group_cols
    blocks = span // block
    for i in range(targets // blocks):
        for t in range(i * blocks, (i + 1) * blocks):
            for c in range(supernodes):
                dense[t * block : (t + 1) * block, c * block : (c + 1) * block] = acc[t, c].astype(BF)
        rows = pl.ds(i * span, span)
        stores.append(pltpu.make_async_copy(dense.at[rows], dense_hbm.at[rows], out_sems.at[1 + i]))
        stores[-1].start()
        total = dot(dense[rows, :], solved[...]).astype(BF)
        if i == 0:
            stage[0, 0:span, :] = total
            stage[1, 0:span, :] = total
        else:
            for q in range(0, span, sec):
                section = ((i - 1) * span + q) // sec
                begin = group_cols + (section // 2) * sec
                stage[(section % 2) ^ core, begin : begin + sec, :] = total[q : q + sec, :]
    keep[...] = stage[0]
    cut = send_low.shape[0]
    send_low[...] = stage[1, 0:cut, :]
    send_high[...] = stage[1, cut:, :]
    for store in stores:
        store.wait()


def leaf_forward(rhs, inverse, tiles, cols, tgts, count, sec, group_cols, upper_cols):
    slots, block, _ = tiles.shape
    supernodes = inverse.shape[0]
    targets = (group_cols + upper_cols) // block
    width = rhs.shape[-1]
    half = group_cols + upper_cols // 2
    return pl.pallas_call(
        functools.partial(forward_kernel, sec, group_cols),
        out_shape=(
            pltpu.VMEM((half, width), BF),
            pltpu.VMEM((half // 2, width), BF),
            pltpu.VMEM((half // 2, width), BF),
            pltpu.HBM((supernodes * block, width), BF),
            pltpu.HBM((targets * block, supernodes * block), BF),
        ),
        in_specs=[HBM] * 6,
        out_specs=(VMEM, VMEM, VMEM, HBM, HBM),
        scratch_shapes=[
            pltpu.SMEM(count.shape, count.dtype),
            pltpu.SMEM(cols.shape, cols.dtype),
            pltpu.SMEM(tgts.shape, tgts.dtype),
            pltpu.VMEM(rhs.shape, rhs.dtype),
            pltpu.VMEM(inverse.shape, inverse.dtype),
            pltpu.VMEM((slots, block, block), BF),
            pltpu.VMEM((targets, supernodes, block, block), F32),
            pltpu.VMEM((2, half, width), BF),
            pltpu.VMEM((supernodes * block, width), BF),
            pltpu.VMEM((targets * block, supernodes * block), BF),
            pltpu.SemaphoreType.DMA((5,)),
            pltpu.SemaphoreType.DMA((CHUNKS,)),
            pltpu.SemaphoreType.DMA((1 + targets * block // group_cols,)),
        ],
        compiler_params=pltpu.CompilerParams(vmem_limit_bytes=BIG),
        cost_estimate=pl.CostEstimate(
            flops=2 * targets * block * supernodes * block * width,
            bytes_accessed=2 * tiles.size + 4 * rhs.size,
            transcendentals=0,
        ),
        name="leaf_forward",
    )(count, *in_hbm(cols, tgts, rhs, inverse, tiles))


def total_of(refs):
    total = refs[0][...].astype(F32)
    for ref in refs[1:]:
        total = total + ref[...].astype(F32)
    return total


def fold_kernel(n_leaf, n_pos, keep, low, high, inv, rhs, panel, *refs):
    parts, group, (gsum, stage) = refs[:n_leaf], refs[n_leaf], refs[n_leaf + 1 :]
    leaf, _, core = place()
    group_cols = inv.shape[0]
    sec = panel.shape[1]
    q = sec // n_leaf
    cut = low.shape[0]

    def both(begin, rows):
        recv = low[begin : begin + rows, :] if begin < cut else high[begin - cut : begin - cut + rows, :]
        return keep[begin : begin + rows, :].astype(F32) + recv.astype(F32)

    gsum[...] = both(0, group_cols)
    residual = rhs[...] * (1.0 / n_pos) - gsum[...]
    solved = dot(inv[...], residual.astype(BF)).astype(BF)
    for p in range(n_pos):
        terms = (dot(panel[p], solved) + both(group_cols + p * sec, sec)).astype(BF)
        for j in range(n_leaf):
            stage[j ^ leaf, p * q : (p + 1) * q, :] = terms[j * q : (j + 1) * q, :]
    half = group_cols // 2
    group[...] = gsum[pl.ds(pl.multiple_of(core * half, half), half), :].astype(BF)
    for k in range(n_leaf):
        parts[k][...] = stage[k]


def fold(keep, recv, inverse, rhs, panel, n_leaf):
    width = rhs.shape[-1]
    n_pos, sec, _ = panel.shape
    part = (n_pos * sec // n_leaf, width)
    outs = small(
        functools.partial(fold_kernel, n_leaf, n_pos),
        "fold_group",
        [part] * n_leaf + [(inverse.shape[0] // 2, width)],
        [pltpu.VMEM(rhs.shape, F32), pltpu.VMEM((n_leaf,) + part, BF)],
        keep,
        *recv,
        inverse,
        rhs,
        panel,
    )
    return list(outs[:n_leaf]), outs[n_leaf]


def sum_kernel(*refs):
    refs[-1][...] = total_of(refs[:-1]).astype(BF)


def sum_of(*parts):
    return small(sum_kernel, "sum", [parts[0].shape], [], *parts)[0]


def residual_kernel(rhs, *refs):
    refs[-1][...] = (rhs[...] - total_of(refs[:-1])).astype(BF)


def residual_of(rhs, *parts):
    return small(residual_kernel, "residual", [rhs.shape], [], rhs, *parts)[0]


def stack_kernel(*refs):
    begin = 0
    for part in refs[:-1]:
        rows = part.shape[0]
        refs[-1][begin : begin + rows, :] = part[...]
        begin += rows


def stack(parts):
    rows = sum(part.shape[0] for part in parts)
    return small(stack_kernel, "stack", [(rows, parts[0].shape[1])], [], *parts)[0]


def weave_kernel(n_leaf, n_pos, own, other, out):
    leaf, pos, core = place()
    rows = own.shape[0] // (n_leaf * n_pos)
    for kc, part in enumerate((own, other)):
        for kl in range(n_leaf):
            for k in range(n_pos):
                block = (leaf ^ kl) * (2 * n_pos) + 2 * (pos ^ k) + (core ^ kc)
                span = pl.ds(pl.multiple_of(block * rows, rows), rows)
                begin = (kl * n_pos + k) * rows
                out[span, :] = part[begin : begin + rows, :]


def weave(own, other, n_leaf, n_pos):
    shape = (2 * own.shape[0], own.shape[1])
    kernel = functools.partial(weave_kernel, n_leaf, n_pos)
    return small(kernel, "weave", [shape], [], own, other)[0]


def backward_kernel(
    n_leaf,
    n_pos,
    mine,
    theirs,
    inv_mid,
    panel_mid,
    inv_top_hbm,
    inv_group_hbm,
    panel_own_hbm,
    panel_other_hbm,
    leaf_solved_hbm,
    inv_leaf_hbm,
    dense_hbm,
    leaf_hbm,
    group_hbm,
    mid_hbm,
    top_hbm,
    inv_top,
    inv_group,
    panel_group,
    leaf_solved,
    inv_leaf,
    dense,
    leaf_out,
    group_out,
    mid_out,
    top_out,
    upper,
    residual,
    above,
    sems,
    panel_sems,
    out_sems,
):
    leaf, pos, core = place()
    pairs = (
        (inv_top_hbm, inv_top),
        (inv_group_hbm, inv_group),
        (leaf_solved_hbm, leaf_solved),
        (inv_leaf_hbm, inv_leaf),
        (dense_hbm, dense),
    )
    loads = [pltpu.make_async_copy(a, b, sems.at[i]) for i, (a, b) in enumerate(pairs)]
    for kc, got in enumerate((panel_own_hbm, panel_other_hbm)):
        target = panel_group.at[:, core ^ kc]
        loads.append(pltpu.make_async_copy(got, target, panel_sems.at[kc]))
    for i in (0, 1, 5, 6, 2, 3, 4):
        loads[i].start()
    mid_rows = inv_mid.shape[0]
    top_rows = inv_top.shape[0]
    group_rows = inv_group.shape[0]
    supernodes, block, _ = inv_leaf.shape
    upper_cols = pl.ds(group_rows, mid_rows + top_rows)
    mid_cols = pl.ds(group_rows, mid_rows)
    top_cols = pl.ds(group_rows + mid_rows, top_rows)
    sec = (mid_rows + top_rows) // (2 * n_pos)
    q = sec // n_leaf
    half = group_rows // 2
    for kc, got in enumerate((mine, theirs)):
        for p in range(n_pos):
            for kl in range(n_leaf):
                row = sec * (2 * p + (core ^ kc)) + q * (leaf ^ kl)
                begin = (kl * n_pos + p) * q
                upper[pl.ds(pl.multiple_of(row, q), q), :] = got[begin : begin + q, :]
        span = pl.ds(pl.multiple_of(half * (core ^ kc), half), half)
        residual[span, :] = got[n_leaf * n_pos * q :, :]

    mid_solved = dot(inv_mid[...], upper[0:mid_rows, :]).astype(BF)
    top_residual = upper[mid_rows:, :].astype(F32) - dot(panel_mid[...], mid_solved)
    loads[0].wait()
    top_solved = dot(inv_top[...], top_residual.astype(BF))
    top_t = dot(top_solved.T.astype(BF), inv_top[...])
    above[:, top_cols] = top_t.astype(BF)
    top_out[...] = top_t.T
    stores = [pltpu.make_async_copy(top_out, top_hbm, out_sems.at[0])]
    stores[0].start()
    mid_back = mid_solved.astype(F32).T - dot(above[:, top_cols], panel_mid[...])
    mid_t = dot(mid_back.astype(BF), inv_mid[...])
    above[:, mid_cols] = mid_t.astype(BF)
    mid_out[...] = mid_t.T
    stores.append(pltpu.make_async_copy(mid_out, mid_hbm, out_sems.at[1]))
    stores[1].start()
    for load in loads[1:]:
        load.wait()
    group_solved = dot(inv_group[...], residual[...]).astype(BF).astype(F32).T
    panel = panel_group[...].reshape(mid_rows + top_rows, group_rows)
    group_back = group_solved - dot(above[:, upper_cols], panel)
    group_t = dot(group_back.astype(BF), inv_group[...])
    above[:, 0:group_rows] = group_t.astype(BF)
    group_out[...] = group_t.T
    stores.append(pltpu.make_async_copy(group_out, group_hbm, out_sems.at[2]))
    stores[2].start()
    for s in range(supernodes):
        cols = pl.ds(s * block, block)
        terms = dot(above[...], dense[:, cols])
        back = (leaf_solved[cols, :].astype(F32).T - terms).astype(BF)
        leaf_out[cols, :] = dot(back, inv_leaf[s]).T
    stores.append(pltpu.make_async_copy(leaf_out, leaf_hbm, out_sems.at[3]))
    stores[3].start()
    for store in stores:
        store.wait()


def backward(close, far, n_leaf, n_pos):
    mine, _, inv_mid, _ = close
    inv_top, inv_group, panel, _, leaf_solved, inv_leaf, dense = far
    width = mine.shape[-1]
    held = (inv_top.shape, inv_group.shape, (n_pos, 2) + panel.shape[1:])
    held += (leaf_solved.shape, inv_leaf.shape, dense.shape)
    outs = (
        leaf_solved.shape,
        (inv_group.shape[0], width),
        (inv_mid.shape[0], width),
        (inv_top.shape[0], width),
    )
    return pl.pallas_call(
        functools.partial(backward_kernel, n_leaf, n_pos),
        out_shape=[pltpu.HBM(shape, F32) for shape in outs],
        in_specs=[VMEM] * len(close) + [HBM] * len(far),
        out_specs=[HBM] * 4,
        scratch_shapes=[pltpu.VMEM(shape, BF) for shape in held]
        + [pltpu.VMEM(shape, F32) for shape in outs]
        + [
            pltpu.VMEM((inv_mid.shape[0] + inv_top.shape[0], width), BF),
            pltpu.VMEM((inv_group.shape[0], width), BF),
            pltpu.VMEM((width, dense.shape[0]), BF),
            pltpu.SemaphoreType.DMA((5,)),
            pltpu.SemaphoreType.DMA((2,)),
            pltpu.SemaphoreType.DMA((len(outs),)),
        ],
        compiler_params=pltpu.CompilerParams(vmem_limit_bytes=BIG),
        name="backward",
    )(*in_vmem(*close), *in_hbm(*far))


def swap(x, axis, size, bits):
    return lax.ppermute(x, axis, [(i, i ^ bits) for i in range(size)])


def swaps(x, axis, size, unit=1):
    return [x] + [swap(x, axis, size, unit * k) for k in range(1, size // unit)]


def after(x, *others):
    return lax.optimization_barrier((x, others))[0]


def body(
    n_leaf,
    n_grp,
    rhs_leaf,
    rhs_group,
    rhs_middle,
    rhs_top,
    inv_leaf,
    inv_group,
    inv_middle,
    inv_top,
    leaf_tiles,
    tile_column,
    tile_target,
    tile_count,
    group_panel,
    middle_panel,
):
    n_pos = n_grp // 2
    group_cols = rhs_group.shape[1]
    mid_cols = rhs_middle.shape[0]
    upper_cols = mid_cols + rhs_top.shape[0]
    sec = upper_cols // n_grp
    q = sec // n_leaf
    leaf, pos, core = place()
    by_parts = middle_panel.shape[0] % 16 == 0
    pos_groups = [[2 * p + c for p in range(n_pos)] for c in range(2)]
    with jax.named_scope("gather_group_panel"):
        panel = lax.all_gather(group_panel[0], "grp", axis_index_groups=pos_groups)
    with jax.named_scope("gather_middle_panel"):
        if by_parts:
            middles = swaps(middle_panel, "grp", n_grp, 2)
        else:
            middle = lax.all_gather(middle_panel, ("leaf", "grp"), axis=0, tiled=True)
    def mine_of(rhs):
        blocks = rhs.reshape(-1, 2, n_leaf, q, rhs.shape[-1])
        blocks = lax.dynamic_index_in_dim(blocks, core, 1, keepdims=False)
        return lax.dynamic_index_in_dim(blocks, leaf, 1, keepdims=False)

    upper_rhs = jnp.concatenate([mine_of(rhs_middle), mine_of(rhs_top)], axis=0)
    upper_rhs = upper_rhs.reshape(n_pos * q, -1)
    half = group_cols // 2
    group_rhs = lax.dynamic_slice_in_dim(rhs_group[0], half * core, half, 0)
    keep, *send, leaf_solved, dense = leaf_forward(
        rhs_leaf[0],
        inv_leaf[0],
        leaf_tiles[0],
        tile_column,
        tile_target,
        tile_count,
        sec,
        group_cols,
        upper_cols,
    )
    with jax.named_scope("swap_cores"):
        if by_parts:
            send = after(send, middles)
        recv = [swap(x, "grp", n_grp, 1) for x in send]
    recv = after(recv, (upper_rhs, group_rhs))
    with jax.named_scope("gather_middle_panel"):
        if by_parts:
            middles = swaps(stack(after(middles, send)), "leaf", n_leaf)
            middle = stack(after(middles, (upper_rhs, group_rhs, recv)))
            middle, panel = lax.optimization_barrier((middle, panel))
    parts, group = fold(keep, recv, inv_group[0], rhs_group[0], panel, n_leaf)
    with jax.named_scope("sum_over_leaf"):
        parts = parts[:1] + [swap(parts[k], "leaf", n_leaf, k) for k in range(1, n_leaf)]
    steps = [2 << i for i in range((n_pos - 1).bit_length())]
    with jax.named_scope("sum_group_over_pos"):
        for bits in steps[:-1]:
            group = sum_of(group, swap(group, "grp", n_grp, bits))
    with jax.named_scope("gather_middle_panel"):
        if by_parts:
            middle = weave(middle, swap(middle, "grp", n_grp, 1), n_leaf, n_pos)
    upper = sum_of(*after(parts, (middle, group)))
    with jax.named_scope("swap_group_panel"):
        panel_other = swap(after(panel, upper), "grp", n_grp, 1)
    with jax.named_scope("sum_over_pos"):
        for bits in steps[:-1]:
            upper = sum_of(upper, swap(upper, "grp", n_grp, bits))
        upper = residual_of(upper_rhs, upper, swap(upper, "grp", n_grp, steps[-1]))
    with jax.named_scope("gather_leaf"):
        stacks = swaps(upper, "leaf", n_leaf)
    with jax.named_scope("sum_group_over_pos"):
        group = after(group, upper)
        group = residual_of(group_rhs, group, swap(group, "grp", n_grp, steps[-1]))
    with jax.named_scope("gather_cores"):
        mine = stack(after(stacks, panel_other) + [group])
        theirs = swap(mine, "grp", n_grp, 1)
    leaf_out, group_out, mid_out, top_out = backward(
        (mine, theirs, inv_middle, middle),
        (inv_top, inv_group[0], panel, panel_other, leaf_solved, inv_leaf[0], dense),
        n_leaf,
        n_pos,
    )
    return leaf_out[None], group_out[None], mid_out, top_out


def solution(mesh):
    n_leaf = mesh.shape["leaf"]
    n_grp = mesh.shape["grp"]
    placed = (
        P("leaf", "grp", None),
        P("leaf", None, None),
        P(),
        P(),
        P("leaf", "grp", None, None),
        P("leaf", None, None),
        P(),
        P(),
        P("leaf", "grp", None, None),
        P("leaf", "grp"),
        P("leaf", "grp"),
        P("leaf", "grp"),
        P("leaf", "grp", None),
        P(("leaf", "grp"), None),
    )
    return jax.shard_map(
        functools.partial(body, n_leaf, n_grp),
        mesh=mesh,
        in_specs=placed,
        out_specs=(P("leaf", "grp", None), P("leaf", None, None), P(), P()),
        check_vma=False,
    )
```

```python
import functools

import jax
import jax.numpy as jnp
from jax import lax
from jax.experimental import pallas as pl
from jax.experimental.pallas import tpu as pltpu
from jax.sharding import PartitionSpec as P

BF = jnp.bfloat16
F32 = jnp.float32
MIB = 1024 * 1024
CHUNKS = 16
UNROLL = 4
HBM = pl.BlockSpec(memory_space=pltpu.HBM)
VMEM = pl.BlockSpec(memory_space=pltpu.VMEM)
BIG = 40 * MIB
SMALL = 6 * MIB


def in_hbm(*arrays):
    return [pltpu.with_memory_space_constraint(x, pltpu.HBM) for x in arrays]


def in_vmem(*arrays):
    return [pltpu.with_memory_space_constraint(x, pltpu.VMEM) for x in arrays]


def small(kernel, name, shapes, scratch, *args):
    return pl.pallas_call(
        kernel,
        out_shape=[pltpu.VMEM(shape, BF) for shape in shapes],
        in_specs=[VMEM] * len(args),
        out_specs=[VMEM] * len(shapes),
        scratch_shapes=scratch,
        compiler_params=pltpu.CompilerParams(vmem_limit_bytes=SMALL),
        name=name,
    )(*in_vmem(*args))


def dot(a, b):
    return jnp.dot(a, b, preferred_element_type=F32)


def place():
    g = lax.axis_index("grp")
    return lax.axis_index("leaf"), g >> 1, g & 1


def forward_kernel(
    sec,
    group_cols,
    count_hbm,
    cols_hbm,
    tgts_hbm,
    rhs_hbm,
    inv_hbm,
    tiles_hbm,
    inv_group_hbm,
    rhs_group_hbm,
    keep,
    send,
    inv_group,
    rhs_group,
    solved_hbm,
    dense_hbm,
    count,
    cols,
    tgts,
    rhs,
    inv,
    tiles,
    acc,
    stage,
    solved,
    dense,
    in_sems,
    tile_sems,
    out_sems,
    pass_sems,
):
    slots, block, _ = tiles.shape
    supernodes = inv.shape[0]
    targets = acc.shape[0]
    chunks = tile_sems.shape[0]
    step = slots // chunks
    _, _, core = place()

    def tile_copy(k):
        span = pl.ds(k * step, step)
        return pltpu.make_async_copy(tiles_hbm.at[span], tiles.at[span], tile_sems.at[k])

    pairs = (
        (count_hbm, count),
        (cols_hbm, cols),
        (tgts_hbm, tgts),
        (rhs_hbm, rhs),
        (inv_hbm, inv),
    )
    loads = [pltpu.make_async_copy(a, b, in_sems.at[i]) for i, (a, b) in enumerate(pairs)]
    for load in loads:
        load.start()
    for k in range(chunks):
        tile_copy(k).start()
    pairs = ((inv_group_hbm, inv_group), (rhs_group_hbm, rhs_group))
    passes = [pltpu.make_async_copy(a, b, pass_sems.at[i]) for i, (a, b) in enumerate(pairs)]
    for copy in passes:
        copy.start()

    acc[...] = jnp.zeros_like(acc)
    for load in loads:
        load.wait()
    for s in range(supernodes):
        rows = pl.ds(s * block, block)
        solved[rows, :] = dot(inv[s], rhs[rows, :].astype(BF)).astype(BF)
    stores = [pltpu.make_async_copy(solved, solved_hbm, out_sems.at[0])]
    stores[0].start()

    live = count[0, 0]

    def add(p):
        t = tgts[0, p]
        c = cols[0, p]
        acc[t, c] = acc[t, c] + tiles[p].astype(F32)

    def add_some(i, carry):
        for u in range(UNROLL):
            add(i * UNROLL + u)
        return carry

    def add_one(p, carry):
        add(p)
        return carry

    whole = live // UNROLL
    per = step // UNROLL
    for k in range(chunks):
        tile_copy(k).wait()
        lax.fori_loop(k * per, jnp.clip(whole, k * per, (k + 1) * per), add_some, 0)
    lax.fori_loop(whole * UNROLL, live, add_one, 0)

    span = group_cols
    blocks = span // block
    for i in range(targets // blocks):
        for t in range(i * blocks, (i + 1) * blocks):
            for c in range(supernodes):
                dense[t * block : (t + 1) * block, c * block : (c + 1) * block] = acc[t, c].astype(BF)
        rows = pl.ds(i * span, span)
        stores.append(pltpu.make_async_copy(dense.at[rows], dense_hbm.at[rows], out_sems.at[1 + i]))
        stores[-1].start()
        total = dot(dense[rows, :], solved[...]).astype(BF)
        if i == 0:
            stage[0, 0:span, :] = total
            stage[1, 0:span, :] = total
        else:
            for q in range(0, span, sec):
                section = ((i - 1) * span + q) // sec
                begin = group_cols + (section // 2) * sec
                stage[(section % 2) ^ core, begin : begin + sec, :] = total[q : q + sec, :]
    keep[...] = stage[0]
    send[...] = stage[1]
    for copy in passes + stores:
        copy.wait()


def leaf_forward(
    rhs, inverse, tiles, cols, tgts, count, inv_group, rhs_group, sec, upper_cols
):
    group_cols = rhs_group.shape[0]
    slots, block, _ = tiles.shape
    supernodes = inverse.shape[0]
    targets = (group_cols + upper_cols) // block
    width = rhs.shape[-1]
    half = group_cols + upper_cols // 2
    return pl.pallas_call(
        functools.partial(forward_kernel, sec, group_cols),
        out_shape=(
            pltpu.VMEM((half, width), BF),
            pltpu.VMEM((half, width), BF),
            pltpu.VMEM(inv_group.shape, BF),
            pltpu.VMEM(rhs_group.shape, F32),
            pltpu.HBM((supernodes * block, width), BF),
            pltpu.HBM((targets * block, supernodes * block), BF),
        ),
        in_specs=[HBM] * 8,
        out_specs=(VMEM,) * 4 + (HBM,) * 2,
        scratch_shapes=[
            pltpu.SMEM(count.shape, count.dtype),
            pltpu.SMEM(cols.shape, cols.dtype),
            pltpu.SMEM(tgts.shape, tgts.dtype),
            pltpu.VMEM(rhs.shape, rhs.dtype),
            pltpu.VMEM(inverse.shape, inverse.dtype),
            pltpu.VMEM((slots, block, block), BF),
            pltpu.VMEM((targets, supernodes, block, block), F32),
            pltpu.VMEM((2, half, width), BF),
            pltpu.VMEM((supernodes * block, width), BF),
            pltpu.VMEM((targets * block, supernodes * block), BF),
            pltpu.SemaphoreType.DMA((5,)),
            pltpu.SemaphoreType.DMA((CHUNKS,)),
            pltpu.SemaphoreType.DMA((1 + targets * block // group_cols,)),
            pltpu.SemaphoreType.DMA((2,)),
        ],
        compiler_params=pltpu.CompilerParams(vmem_limit_bytes=BIG),
        cost_estimate=pl.CostEstimate(
            flops=2 * targets * block * supernodes * block * width,
            bytes_accessed=2 * tiles.size + 4 * rhs.size,
            transcendentals=0,
        ),
        name="leaf_forward",
    )(count, *in_hbm(cols, tgts, rhs, inverse, tiles, inv_group, rhs_group))


def total_of(refs):
    total = refs[0][...].astype(F32)
    for ref in refs[1:]:
        total = total + ref[...].astype(F32)
    return total


def fold_kernel(n_leaf, n_pos, keep, recv, inv, rhs, panel, *refs):
    parts, group, (gsum, stage) = refs[:n_leaf], refs[n_leaf], refs[n_leaf + 1 :]
    leaf, pos, core = place()
    group_cols = inv.shape[0]
    sec = panel.shape[1]
    q = sec // n_leaf
    gq = group_cols // (2 * n_pos)
    gsum[...] = keep[0:group_cols, :].astype(F32) + recv[0:group_cols, :].astype(F32)
    residual = rhs[...] * (1.0 / n_pos) - gsum[...]
    solved = dot(inv[...], residual.astype(BF)).astype(BF)
    for k in range(n_pos):
        p = pos ^ k
        rows = pl.ds(pl.multiple_of(group_cols + p * sec, sec), sec)
        terms = dot(panel[p], solved)
        terms = (terms + (keep[rows, :].astype(F32) + recv[rows, :].astype(F32))).astype(BF)
        for j in range(n_leaf):
            stage[j ^ leaf, k * q : (k + 1) * q, :] = terms[j * q : (j + 1) * q, :]
        begin = pl.multiple_of(core * (group_cols // 2) + p * gq, gq)
        group[k * gq : (k + 1) * gq, :] = gsum[pl.ds(begin, gq), :].astype(BF)
    for k in range(n_leaf):
        parts[k][...] = stage[k]


def fold(keep, recv, inverse, rhs, panel, n_leaf):
    width = rhs.shape[-1]
    n_pos, sec, _ = panel.shape
    part = (n_pos * sec // n_leaf, width)
    outs = small(
        functools.partial(fold_kernel, n_leaf, n_pos),
        "fold_group",
        [part] * n_leaf + [(inverse.shape[0] // 2, width)],
        [pltpu.VMEM(rhs.shape, F32), pltpu.VMEM((n_leaf,) + part, BF)],
        keep,
        recv,
        inverse,
        rhs,
        panel,
    )
    return list(outs[:n_leaf]), outs[n_leaf]


def sum_leaf_kernel(n_leaf, *refs):
    group, outs = refs[n_leaf], refs[n_leaf + 1 :]
    n_pos = len(outs)
    q = refs[0].shape[0] // n_pos
    gq = group.shape[0] // n_pos
    total = total_of(refs[:n_leaf]).astype(BF)
    for k, out in enumerate(outs):
        out[0:q, :] = total[k * q : (k + 1) * q, :]
        out[q:, :] = group[k * gq : (k + 1) * gq, :]


def sum_leaf(parts, group, n_pos):
    rows = (parts[0].shape[0] + group.shape[0]) // n_pos
    kernel = functools.partial(sum_leaf_kernel, len(parts))
    shapes = [(rows, group.shape[1])] * n_pos
    return list(small(kernel, "sum_leaf", shapes, [], *parts, group))


def sum_pos_kernel(high, group, *refs):
    parts, out = refs[:-1], refs[-1]
    q = high.shape[0]
    total = total_of(parts)
    out[0:q, :] = (high[...] - total[0:q, :]).astype(BF)
    out[q:, :] = (group[...] - total[q:, :]).astype(BF)


def sum_pos(high, group, parts):
    return small(sum_pos_kernel, "sum_pos", [parts[0].shape], [], high, group, *parts)[0]


def stack_pos_kernel(q, *refs):
    parts, (uppers, groups) = refs[:-2], refs[-2:]
    gq = parts[0].shape[0] - q
    for k, part in enumerate(parts):
        uppers[k * q : (k + 1) * q, :] = part[0:q, :]
        groups[k * gq : (k + 1) * gq, :] = part[q:, :]


def stack_pos(parts, q):
    n_pos, (rows, width) = len(parts), parts[0].shape
    shapes = [(n_pos * q, width), (n_pos * (rows - q), width)]
    return small(functools.partial(stack_pos_kernel, q), "stack_pos", shapes, [], *parts)


def stack_kernel(*refs):
    begin = 0
    for part in refs[:-1]:
        rows = part.shape[0]
        refs[-1][begin : begin + rows, :] = part[...]
        begin += rows


def stack(parts):
    rows = sum(part.shape[0] for part in parts)
    return small(stack_kernel, "stack", [(rows, parts[0].shape[1])], [], *parts)[0]


def weave_kernel(n_leaf, n_pos, own, other, out):
    leaf, pos, core = place()
    rows = own.shape[0] // (n_leaf * n_pos)
    for kc, part in enumerate((own, other)):
        for kl in range(n_leaf):
            for k in range(n_pos):
                block = (leaf ^ kl) * (2 * n_pos) + 2 * (pos ^ k) + (core ^ kc)
                span = pl.ds(pl.multiple_of(block * rows, rows), rows)
                begin = (kl * n_pos + k) * rows
                out[span, :] = part[begin : begin + rows, :]


def weave(own, other, n_leaf, n_pos):
    shape = (2 * own.shape[0], own.shape[1])
    kernel = functools.partial(weave_kernel, n_leaf, n_pos)
    return small(kernel, "weave", [shape], [], own, other)[0]


def lower_dot(lower, x):
    n = lower.shape[0]
    step = n // 4
    parts = []
    for i in range(0, n, step):
        parts.append(dot(lower[i : i + step, 0 : i + step], x[0 : i + step, :]))
    return jnp.concatenate(parts, axis=0)


def dot_lower(x, lower):
    n = lower.shape[0]
    step = n // 4
    parts = []
    for i in range(0, n, step):
        parts.append(dot(x[:, i:], lower[i:, i : i + step]))
    return jnp.concatenate(parts, axis=1)


def backward_kernel(
    n_leaf,
    n_pos,
    mine,
    theirs,
    inv_mid,
    panel_mid,
    inv_top_hbm,
    inv_group_hbm,
    panel_own_hbm,
    panel_other_hbm,
    leaf_solved_hbm,
    inv_leaf_hbm,
    dense_hbm,
    leaf_hbm,
    group_hbm,
    mid_hbm,
    top_hbm,
    inv_top,
    inv_group,
    panel_group,
    leaf_solved,
    inv_leaf,
    dense,
    leaf_out,
    group_out,
    mid_out,
    top_out,
    upper,
    residual,
    above,
    sems,
    panel_sems,
    out_sems,
):
    leaf, pos, core = place()
    pairs = (
        (inv_top_hbm, inv_top),
        (inv_group_hbm, inv_group),
        (leaf_solved_hbm, leaf_solved),
        (inv_leaf_hbm, inv_leaf),
        (dense_hbm, dense),
    )
    loads = [pltpu.make_async_copy(a, b, sems.at[i]) for i, (a, b) in enumerate(pairs)]
    for kc, got in enumerate((panel_own_hbm, panel_other_hbm)):
        target = panel_group.at[:, core ^ kc]
        loads.append(pltpu.make_async_copy(got, target, panel_sems.at[kc]))
    for i in (0, 1, 5, 6, 2, 3, 4):
        loads[i].start()
    mid_rows = inv_mid.shape[0]
    top_rows = inv_top.shape[0]
    group_rows = inv_group.shape[0]
    supernodes, block, _ = inv_leaf.shape
    upper_cols = pl.ds(group_rows, mid_rows + top_rows)
    mid_cols = pl.ds(group_rows, mid_rows)
    top_cols = pl.ds(group_rows + mid_rows, top_rows)
    sec = (mid_rows + top_rows) // (2 * n_pos)
    q = sec // n_leaf
    gq = group_rows // (2 * n_pos)
    for kc, got in enumerate((mine, theirs)):
        for kz in range(n_pos):
            for kl in range(n_leaf):
                row = sec * (2 * (pos ^ kz) + (core ^ kc)) + q * (leaf ^ kl)
                begin = (kl * n_pos + kz) * q
                upper[pl.ds(pl.multiple_of(row, q), q), :] = got[begin : begin + q, :]
            row = (group_rows // 2) * (core ^ kc) + gq * (pos ^ kz)
            begin = n_leaf * n_pos * q + kz * gq
            residual[pl.ds(pl.multiple_of(row, gq), gq), :] = got[begin : begin + gq, :]

    mid_solved = lower_dot(inv_mid, upper[0:mid_rows, :]).astype(BF)
    top_residual = upper[mid_rows:, :].astype(F32) - dot(panel_mid[...], mid_solved)
    loads[0].wait()
    top_solved = lower_dot(inv_top, top_residual.astype(BF))
    top_t = dot_lower(top_solved.T.astype(BF), inv_top)
    above[:, top_cols] = top_t.astype(BF)
    top_out[...] = top_t.T
    stores = [pltpu.make_async_copy(top_out, top_hbm, out_sems.at[0])]
    stores[0].start()
    mid_back = mid_solved.astype(F32).T - dot(above[:, top_cols], panel_mid[...])
    mid_t = dot_lower(mid_back.astype(BF), inv_mid)
    above[:, mid_cols] = mid_t.astype(BF)
    mid_out[...] = mid_t.T
    stores.append(pltpu.make_async_copy(mid_out, mid_hbm, out_sems.at[1]))
    stores[1].start()
    for load in loads[1:]:
        load.wait()
    group_solved = dot(inv_group[...], residual[...]).astype(BF).astype(F32).T
    panel = panel_group[...].reshape(mid_rows + top_rows, group_rows)
    group_back = group_solved - dot(above[:, upper_cols], panel)
    group_t = dot(group_back.astype(BF), inv_group[...])
    above[:, 0:group_rows] = group_t.astype(BF)
    group_out[...] = group_t.T
    stores.append(pltpu.make_async_copy(group_out, group_hbm, out_sems.at[2]))
    stores[2].start()
    for s in range(supernodes):
        cols = pl.ds(s * block, block)
        terms = dot(above[...], dense[:, cols])
        back = (leaf_solved[cols, :].astype(F32).T - terms).astype(BF)
        leaf_out[cols, :] = dot(back, inv_leaf[s]).T
    stores.append(pltpu.make_async_copy(leaf_out, leaf_hbm, out_sems.at[3]))
    stores[3].start()
    for store in stores:
        store.wait()


def backward(close, far, n_leaf, n_pos):
    mine, _, inv_mid, _ = close
    inv_top, inv_group, panel, _, leaf_solved, inv_leaf, dense = far
    width = mine.shape[-1]
    held = (inv_top.shape, inv_group.shape, (n_pos, 2) + panel.shape[1:])
    held += (leaf_solved.shape, inv_leaf.shape, dense.shape)
    outs = (
        leaf_solved.shape,
        (inv_group.shape[0], width),
        (inv_mid.shape[0], width),
        (inv_top.shape[0], width),
    )
    return pl.pallas_call(
        functools.partial(backward_kernel, n_leaf, n_pos),
        out_shape=[pltpu.HBM(shape, F32) for shape in outs],
        in_specs=[VMEM] * len(close) + [HBM] * len(far),
        out_specs=[HBM] * 4,
        scratch_shapes=[pltpu.VMEM(shape, BF) for shape in held]
        + [pltpu.VMEM(shape, F32) for shape in outs]
        + [
            pltpu.VMEM((inv_mid.shape[0] + inv_top.shape[0], width), BF),
            pltpu.VMEM((inv_group.shape[0], width), BF),
            pltpu.VMEM((width, dense.shape[0]), BF),
            pltpu.SemaphoreType.DMA((5,)),
            pltpu.SemaphoreType.DMA((2,)),
            pltpu.SemaphoreType.DMA((len(outs),)),
        ],
        compiler_params=pltpu.CompilerParams(vmem_limit_bytes=BIG),
        name="backward",
    )(*in_vmem(*close), *in_hbm(*far))


def swap(x, axis, size, bits):
    return lax.ppermute(x, axis, [(i, i ^ bits) for i in range(size)])


def swaps(x, axis, size, unit=1):
    return [x] + [swap(x, axis, size, unit * k) for k in range(1, size // unit)]


def after(x, *others):
    return lax.optimization_barrier((x, others))[0]


def body(
    n_leaf,
    n_grp,
    rhs_leaf,
    rhs_group,
    rhs_middle,
    rhs_top,
    inv_leaf,
    inv_group,
    inv_middle,
    inv_top,
    leaf_tiles,
    tile_column,
    tile_target,
    tile_count,
    group_panel,
    middle_panel,
):
    n_pos = n_grp // 2
    group_cols = rhs_group.shape[1]
    mid_cols = rhs_middle.shape[0]
    upper_cols = mid_cols + rhs_top.shape[0]
    sec = upper_cols // n_grp
    q = sec // n_leaf
    gq = group_cols // n_grp
    leaf, pos, core = place()
    by_parts = middle_panel.shape[0] % 16 == 0
    pos_groups = [[2 * p + c for p in range(n_pos)] for c in range(2)]
    with jax.named_scope("gather_group_panel"):
        panel = lax.all_gather(group_panel[0], "grp", axis_index_groups=pos_groups)
    with jax.named_scope("gather_middle_panel"):
        if by_parts:
            middles = swaps(middle_panel, "grp", n_grp, 2)
        else:
            middle = lax.all_gather(middle_panel, ("leaf", "grp"), axis=0, tiled=True)
    begin = sec * lax.axis_index("grp") + q * leaf
    low = lax.dynamic_slice_in_dim(rhs_middle, jnp.minimum(begin, mid_cols - q), q, 0)
    high = lax.dynamic_slice_in_dim(rhs_top, jnp.maximum(begin - mid_cols, 0), q, 0)
    rhs_mine = jnp.where(begin < mid_cols, low, high)
    group_begin = (group_cols // 2) * core + gq * pos
    group_mine = lax.dynamic_slice_in_dim(rhs_group[0], group_begin, gq, 0)
    keep, send, inv_here, rhs_here, leaf_solved, dense = leaf_forward(
        rhs_leaf[0],
        inv_leaf[0],
        leaf_tiles[0],
        tile_column,
        tile_target,
        tile_count,
        inv_group[0],
        rhs_group[0],
        sec,
        upper_cols,
    )
    with jax.named_scope("swap_cores"):
        if by_parts:
            send = after(send, middles)
        recv = swap(send, "grp", n_grp, 1)
    with jax.named_scope("gather_middle_panel"):
        if by_parts:
            middles = swaps(stack(after(middles, send)), "leaf", n_leaf)
            recv = after(recv, middles)
            middle = stack(after(middles, (rhs_mine, group_mine)))
    parts, group = fold(keep, recv, inv_here, rhs_here, panel, n_leaf)
    with jax.named_scope("sum_over_leaf"):
        parts = parts[:1] + [swap(parts[k], "leaf", n_leaf, k) for k in range(1, n_leaf)]
    with jax.named_scope("gather_middle_panel"):
        if by_parts:
            middle = weave(middle, swap(middle, "grp", n_grp, 1), n_leaf, n_pos)
    sends = sum_leaf(after(parts, middle), group, n_pos)
    with jax.named_scope("sum_over_pos"):
        got = sends[:1] + [swap(sends[k], "grp", n_grp, 2 * k) for k in range(1, n_pos)]
    with jax.named_scope("swap_group_panel"):
        panel_other = swap(panel, "grp", n_grp, 1)
    residual = sum_pos(rhs_mine, group_mine, got)
    with jax.named_scope("gather_pos"):
        uppers, groups = stack_pos(swaps(residual, "grp", n_grp, 2), q)
    with jax.named_scope("gather_leaf"):
        stacks = swaps(uppers, "leaf", n_leaf)
    with jax.named_scope("gather_cores"):
        mine = stack(after(stacks, panel_other) + [groups])
        theirs = swap(mine, "grp", n_grp, 1)
    leaf_out, group_out, mid_out, top_out = backward(
        (mine, theirs, inv_middle, middle),
        (inv_top, inv_group[0], panel, panel_other, leaf_solved, inv_leaf[0], dense),
        n_leaf,
        n_pos,
    )
    return leaf_out[None], group_out[None], mid_out, top_out


def solution(mesh):
    n_leaf = mesh.shape["leaf"]
    n_grp = mesh.shape["grp"]
    placed = (
        P("leaf", "grp", None),
        P("leaf", None, None),
        P(),
        P(),
        P("leaf", "grp", None, None),
        P("leaf", None, None),
        P(),
        P(),
        P("leaf", "grp", None, None),
        P("leaf", "grp"),
        P("leaf", "grp"),
        P("leaf", "grp"),
        P("leaf", "grp", None),
        P(("leaf", "grp"), None),
    )
    return jax.shard_map(
        functools.partial(body, n_leaf, n_grp),
        mesh=mesh,
        in_specs=placed,
        out_specs=(P("leaf", "grp", None), P("leaf", None, None), P(), P()),
        check_vma=False,
    )
```

```python
import functools

import jax
import jax.numpy as jnp
from jax import lax
from jax.experimental import pallas as pl
from jax.experimental.pallas import tpu as pltpu
from jax.sharding import PartitionSpec as P

BF = jnp.bfloat16
F32 = jnp.float32
MIB = 1024 * 1024
CHUNKS = 16
UNROLL = 4
HBM = pl.BlockSpec(memory_space=pltpu.HBM)
VMEM = pl.BlockSpec(memory_space=pltpu.VMEM)
BIG = 40 * MIB
SMALL = 6 * MIB


def in_hbm(*arrays):
    return [pltpu.with_memory_space_constraint(x, pltpu.HBM) for x in arrays]


def in_vmem(*arrays):
    return [pltpu.with_memory_space_constraint(x, pltpu.VMEM) for x in arrays]


def small(kernel, name, shapes, scratch, *args):
    return pl.pallas_call(
        kernel,
        out_shape=[pltpu.VMEM(shape, BF) for shape in shapes],
        in_specs=[VMEM] * len(args),
        out_specs=[VMEM] * len(shapes),
        scratch_shapes=scratch,
        compiler_params=pltpu.CompilerParams(vmem_limit_bytes=SMALL),
        name=name,
    )(*in_vmem(*args))


def dot(a, b):
    return jnp.dot(a, b, preferred_element_type=F32)


def place():
    g = lax.axis_index("grp")
    return lax.axis_index("leaf"), g >> 1, g & 1


def forward_kernel(
    n_pos,
    sec,
    group_cols,
    count_hbm,
    cols_hbm,
    tgts_hbm,
    rhs_hbm,
    inv_hbm,
    tiles_hbm,
    inv_group_hbm,
    rhs_group_hbm,
    keep,
    send_low,
    send_high,
    inv_group,
    solved_hbm,
    dense_hbm,
    count,
    cols,
    tgts,
    rhs,
    inv,
    tiles,
    acc,
    stage,
    solved,
    dense,
    rhs_group,
    in_sems,
    tile_sems,
    out_sems,
    pass_sems,
):
    slots, block, _ = tiles.shape
    supernodes = inv.shape[0]
    targets = acc.shape[0]
    chunks = tile_sems.shape[0]
    step = slots // chunks
    _, _, core = place()

    def tile_copy(k):
        span = pl.ds(k * step, step)
        return pltpu.make_async_copy(tiles_hbm.at[span], tiles.at[span], tile_sems.at[k])

    pairs = (
        (count_hbm, count),
        (cols_hbm, cols),
        (tgts_hbm, tgts),
        (rhs_hbm, rhs),
        (inv_hbm, inv),
    )
    loads = [pltpu.make_async_copy(a, b, in_sems.at[i]) for i, (a, b) in enumerate(pairs)]
    for load in loads:
        load.start()
    for k in range(chunks):
        tile_copy(k).start()
    pairs = ((inv_group_hbm, inv_group), (rhs_group_hbm, rhs_group))
    passes = [pltpu.make_async_copy(a, b, pass_sems.at[i]) for i, (a, b) in enumerate(pairs)]
    for copy in passes:
        copy.start()

    acc[...] = jnp.zeros_like(acc)
    for load in loads:
        load.wait()
    for s in range(supernodes):
        rows = pl.ds(s * block, block)
        solved[rows, :] = dot(inv[s], rhs[rows, :].astype(BF)).astype(BF)
    stores = [pltpu.make_async_copy(solved, solved_hbm, out_sems.at[0])]
    stores[0].start()

    live = count[0, 0]

    def add(p):
        t = tgts[0, p]
        c = cols[0, p]
        acc[t, c] = acc[t, c] + tiles[p].astype(F32)

    def add_some(i, carry):
        for u in range(UNROLL):
            add(i * UNROLL + u)
        return carry

    def add_one(p, carry):
        add(p)
        return carry

    whole = live // UNROLL
    per = step // UNROLL
    for k in range(chunks):
        tile_copy(k).wait()
        lax.fori_loop(k * per, jnp.clip(whole, k * per, (k + 1) * per), add_some, 0)
    lax.fori_loop(whole * UNROLL, live, add_one, 0)

    span = group_cols
    blocks = span // block
    for i in range(targets // blocks):
        for t in range(i * blocks, (i + 1) * blocks):
            for c in range(supernodes):
                dense[t * block : (t + 1) * block, c * block : (c + 1) * block] = acc[t, c].astype(BF)
        rows = pl.ds(i * span, span)
        stores.append(pltpu.make_async_copy(dense.at[rows], dense_hbm.at[rows], out_sems.at[1 + i]))
        stores[-1].start()
        total = dot(dense[rows, :], solved[...])
        if i == 0:
            passes[1].wait()
            share = jnp.where(core == 0, 1.0 / n_pos, 0.0)
            total = (total - rhs_group[...] * share).astype(BF)
            stage[0, 0:span, :] = total
            stage[1, 0:span, :] = total
        else:
            total = total.astype(BF)
            for q in range(0, span, sec):
                section = ((i - 1) * span + q) // sec
                begin = group_cols + (section // 2) * sec
                stage[(section % 2) ^ core, begin : begin + sec, :] = total[q : q + sec, :]
    keep[...] = stage[0]
    cut = send_low.shape[0]
    send_low[...] = stage[1, 0:cut, :]
    send_high[...] = stage[1, cut:, :]
    for copy in passes[:1] + stores:
        copy.wait()


def leaf_forward(
    rhs, inverse, tiles, cols, tgts, count, inv_group, rhs_group, sec, upper_cols
):
    group_cols = rhs_group.shape[0]
    slots, block, _ = tiles.shape
    supernodes = inverse.shape[0]
    targets = (group_cols + upper_cols) // block
    width = rhs.shape[-1]
    half = group_cols + upper_cols // 2
    return pl.pallas_call(
        functools.partial(forward_kernel, upper_cols // (2 * sec), sec, group_cols),
        out_shape=(
            pltpu.VMEM((half, width), BF),
            pltpu.VMEM((half // 2, width), BF),
            pltpu.VMEM((half // 2, width), BF),
            pltpu.VMEM(inv_group.shape, BF),
            pltpu.HBM((supernodes * block, width), BF),
            pltpu.HBM((targets * block, supernodes * block), BF),
        ),
        in_specs=[HBM] * 8,
        out_specs=(VMEM,) * 4 + (HBM,) * 2,
        scratch_shapes=[
            pltpu.SMEM(count.shape, count.dtype),
            pltpu.SMEM(cols.shape, cols.dtype),
            pltpu.SMEM(tgts.shape, tgts.dtype),
            pltpu.VMEM(rhs.shape, rhs.dtype),
            pltpu.VMEM(inverse.shape, inverse.dtype),
            pltpu.VMEM((slots, block, block), BF),
            pltpu.VMEM((targets, supernodes, block, block), F32),
            pltpu.VMEM((2, half, width), BF),
            pltpu.VMEM((supernodes * block, width), BF),
            pltpu.VMEM((targets * block, supernodes * block), BF),
            pltpu.VMEM(rhs_group.shape, F32),
            pltpu.SemaphoreType.DMA((5,)),
            pltpu.SemaphoreType.DMA((CHUNKS,)),
            pltpu.SemaphoreType.DMA((1 + targets * block // group_cols,)),
            pltpu.SemaphoreType.DMA((2,)),
        ],
        compiler_params=pltpu.CompilerParams(vmem_limit_bytes=BIG),
        cost_estimate=pl.CostEstimate(
            flops=2 * targets * block * supernodes * block * width,
            bytes_accessed=2 * tiles.size + 4 * rhs.size,
            transcendentals=0,
        ),
        name="leaf_forward",
    )(count, *in_hbm(cols, tgts, rhs, inverse, tiles, inv_group, rhs_group))


def total_of(refs):
    total = refs[0][...].astype(F32)
    for ref in refs[1:]:
        total = total + ref[...].astype(F32)
    return total


def fold_kernel(n_leaf, n_pos, keep, low, high, inv, panel, *refs):
    parts, group, (gsum, base, stage) = refs[:n_leaf], refs[n_leaf], refs[n_leaf + 1 :]
    leaf, pos, core = place()
    group_cols = inv.shape[0]
    sec = panel.shape[1]
    q = sec // n_leaf
    gq = group_cols // (2 * n_pos)
    cut = low.shape[0]
    gsum[...] = keep[0:group_cols, :].astype(F32) + low[0:group_cols, :].astype(F32)
    base[0 : cut - group_cols, :] = keep[group_cols:cut, :].astype(F32) + low[group_cols:, :].astype(F32)
    base[cut - group_cols :, :] = keep[cut:, :].astype(F32) + high[...].astype(F32)
    solved = dot(inv[...], (-gsum[...]).astype(BF)).astype(BF)
    for k in range(n_pos):
        p = pos ^ k
        rows = pl.ds(pl.multiple_of(p * sec, sec), sec)
        terms = (dot(panel[p], solved) + base[rows, :]).astype(BF)
        for j in range(n_leaf):
            stage[j ^ leaf, k * q : (k + 1) * q, :] = terms[j * q : (j + 1) * q, :]
        begin = pl.multiple_of(core * (group_cols // 2) + p * gq, gq)
        group[k * gq : (k + 1) * gq, :] = gsum[pl.ds(begin, gq), :].astype(BF)
    for k in range(n_leaf):
        parts[k][...] = stage[k]


def fold(keep, recv, inverse, panel, n_leaf):
    width = keep.shape[-1]
    n_pos, sec, _ = panel.shape
    part = (n_pos * sec // n_leaf, width)
    outs = small(
        functools.partial(fold_kernel, n_leaf, n_pos),
        "fold_group",
        [part] * n_leaf + [(inverse.shape[0] // 2, width)],
        [
            pltpu.VMEM((inverse.shape[0], width), F32),
            pltpu.VMEM((n_pos * sec, width), F32),
            pltpu.VMEM((n_leaf,) + part, BF),
        ],
        keep,
        *recv,
        inverse,
        panel,
    )
    return list(outs[:n_leaf]), outs[n_leaf]


def sum_leaf_kernel(n_leaf, *refs):
    group, outs = refs[n_leaf], refs[n_leaf + 1 :]
    n_pos = len(outs)
    q = refs[0].shape[0] // n_pos
    gq = group.shape[0] // n_pos
    total = total_of(refs[:n_leaf]).astype(BF)
    for k, out in enumerate(outs):
        out[0:q, :] = total[k * q : (k + 1) * q, :]
        out[q:, :] = group[k * gq : (k + 1) * gq, :]


def sum_leaf(parts, group, n_pos):
    rows = (parts[0].shape[0] + group.shape[0]) // n_pos
    kernel = functools.partial(sum_leaf_kernel, len(parts))
    shapes = [(rows, group.shape[1])] * n_pos
    return list(small(kernel, "sum_leaf", shapes, [], *parts, group))


def sum_pos_kernel(high, *refs):
    parts, out = refs[:-1], refs[-1]
    q = high.shape[0]
    total = total_of(parts)
    out[0:q, :] = (high[...] - total[0:q, :]).astype(BF)
    out[q:, :] = (-total[q:, :]).astype(BF)


def sum_pos(high, parts):
    return small(sum_pos_kernel, "sum_pos", [parts[0].shape], [], high, *parts)[0]


def stack_pos_kernel(q, *refs):
    parts, (uppers, groups) = refs[:-2], refs[-2:]
    gq = parts[0].shape[0] - q
    for k, part in enumerate(parts):
        uppers[k * q : (k + 1) * q, :] = part[0:q, :]
        groups[k * gq : (k + 1) * gq, :] = part[q:, :]


def stack_pos(parts, q):
    n_pos, (rows, width) = len(parts), parts[0].shape
    shapes = [(n_pos * q, width), (n_pos * (rows - q), width)]
    return small(functools.partial(stack_pos_kernel, q), "stack_pos", shapes, [], *parts)


def stack_kernel(*refs):
    begin = 0
    for part in refs[:-1]:
        rows = part.shape[0]
        refs[-1][begin : begin + rows, :] = part[...]
        begin += rows


def stack(parts):
    rows = sum(part.shape[0] for part in parts)
    return small(stack_kernel, "stack", [(rows, parts[0].shape[1])], [], *parts)[0]


def weave_kernel(n_leaf, n_pos, own, other, out):
    leaf, pos, core = place()
    rows = own.shape[0] // (n_leaf * n_pos)
    for kc, part in enumerate((own, other)):
        for kl in range(n_leaf):
            for k in range(n_pos):
                block = (leaf ^ kl) * (2 * n_pos) + 2 * (pos ^ k) + (core ^ kc)
                span = pl.ds(pl.multiple_of(block * rows, rows), rows)
                begin = (kl * n_pos + k) * rows
                out[span, :] = part[begin : begin + rows, :]


def weave(own, other, n_leaf, n_pos):
    shape = (2 * own.shape[0], own.shape[1])
    kernel = functools.partial(weave_kernel, n_leaf, n_pos)
    return small(kernel, "weave", [shape], [], own, other)[0]


def lower_dot(lower, x):
    n = lower.shape[0]
    step = n // 4
    parts = []
    for i in range(0, n, step):
        parts.append(dot(lower[i : i + step, 0 : i + step], x[0 : i + step, :]))
    return jnp.concatenate(parts, axis=0)


def dot_lower(x, lower):
    n = lower.shape[0]
    step = n // 4
    parts = []
    for i in range(0, n, step):
        parts.append(dot(x[:, i:], lower[i:, i : i + step]))
    return jnp.concatenate(parts, axis=1)


def backward_kernel(
    n_leaf,
    n_pos,
    mine,
    theirs,
    inv_mid,
    panel_mid,
    inv_top_hbm,
    inv_group_hbm,
    panel_own_hbm,
    panel_other_hbm,
    leaf_solved_hbm,
    inv_leaf_hbm,
    dense_hbm,
    leaf_hbm,
    group_hbm,
    mid_hbm,
    top_hbm,
    inv_top,
    inv_group,
    panel_group,
    leaf_solved,
    inv_leaf,
    dense,
    leaf_out,
    group_out,
    mid_out,
    top_out,
    upper,
    residual,
    above,
    sems,
    panel_sems,
    out_sems,
):
    leaf, pos, core = place()
    pairs = (
        (inv_top_hbm, inv_top),
        (inv_group_hbm, inv_group),
        (leaf_solved_hbm, leaf_solved),
        (inv_leaf_hbm, inv_leaf),
        (dense_hbm, dense),
    )
    loads = [pltpu.make_async_copy(a, b, sems.at[i]) for i, (a, b) in enumerate(pairs)]
    for kc, got in enumerate((panel_own_hbm, panel_other_hbm)):
        target = panel_group.at[:, core ^ kc]
        loads.append(pltpu.make_async_copy(got, target, panel_sems.at[kc]))
    for i in (0, 1, 5, 6, 2, 3, 4):
        loads[i].start()
    mid_rows = inv_mid.shape[0]
    top_rows = inv_top.shape[0]
    group_rows = inv_group.shape[0]
    supernodes, block, _ = inv_leaf.shape
    upper_cols = pl.ds(group_rows, mid_rows + top_rows)
    mid_cols = pl.ds(group_rows, mid_rows)
    top_cols = pl.ds(group_rows + mid_rows, top_rows)
    sec = (mid_rows + top_rows) // (2 * n_pos)
    q = sec // n_leaf
    gq = group_rows // (2 * n_pos)
    for kc, got in enumerate((mine, theirs)):
        for kz in range(n_pos):
            for kl in range(n_leaf):
                row = sec * (2 * (pos ^ kz) + (core ^ kc)) + q * (leaf ^ kl)
                begin = (kl * n_pos + kz) * q
                upper[pl.ds(pl.multiple_of(row, q), q), :] = got[begin : begin + q, :]
            row = (group_rows // 2) * (core ^ kc) + gq * (pos ^ kz)
            begin = n_leaf * n_pos * q + kz * gq
            residual[pl.ds(pl.multiple_of(row, gq), gq), :] = got[begin : begin + gq, :]

    mid_solved = lower_dot(inv_mid, upper[0:mid_rows, :]).astype(BF)
    top_residual = upper[mid_rows:, :].astype(F32) - dot(panel_mid[...], mid_solved)
    loads[0].wait()
    top_solved = lower_dot(inv_top, top_residual.astype(BF))
    top_t = dot_lower(top_solved.T.astype(BF), inv_top)
    above[:, top_cols] = top_t.astype(BF)
    top_out[...] = top_t.T
    stores = [pltpu.make_async_copy(top_out, top_hbm, out_sems.at[0])]
    stores[0].start()
    mid_back = mid_solved.astype(F32).T - dot(above[:, top_cols], panel_mid[...])
    mid_t = dot_lower(mid_back.astype(BF), inv_mid)
    above[:, mid_cols] = mid_t.astype(BF)
    mid_out[...] = mid_t.T
    stores.append(pltpu.make_async_copy(mid_out, mid_hbm, out_sems.at[1]))
    stores[1].start()
    for load in loads[1:]:
        load.wait()
    group_solved = dot(inv_group[...], residual[...]).astype(BF).astype(F32).T
    panel = panel_group[...].reshape(mid_rows + top_rows, group_rows)
    group_back = group_solved - dot(above[:, upper_cols], panel)
    group_t = dot(group_back.astype(BF), inv_group[...])
    above[:, 0:group_rows] = group_t.astype(BF)
    group_out[...] = group_t.T
    stores.append(pltpu.make_async_copy(group_out, group_hbm, out_sems.at[2]))
    stores[2].start()
    for s in range(supernodes):
        cols = pl.ds(s * block, block)
        terms = dot(above[...], dense[:, cols])
        back = (leaf_solved[cols, :].astype(F32).T - terms).astype(BF)
        leaf_out[cols, :] = dot(back, inv_leaf[s]).T
    stores.append(pltpu.make_async_copy(leaf_out, leaf_hbm, out_sems.at[3]))
    stores[3].start()
    for store in stores:
        store.wait()


def backward(close, far, n_leaf, n_pos):
    mine, _, inv_mid, _ = close
    inv_top, inv_group, panel, _, leaf_solved, inv_leaf, dense = far
    width = mine.shape[-1]
    held = (inv_top.shape, inv_group.shape, (n_pos, 2) + panel.shape[1:])
    held += (leaf_solved.shape, inv_leaf.shape, dense.shape)
    outs = (
        leaf_solved.shape,
        (inv_group.shape[0], width),
        (inv_mid.shape[0], width),
        (inv_top.shape[0], width),
    )
    return pl.pallas_call(
        functools.partial(backward_kernel, n_leaf, n_pos),
        out_shape=[pltpu.HBM(shape, F32) for shape in outs],
        in_specs=[VMEM] * len(close) + [HBM] * len(far),
        out_specs=[HBM] * 4,
        scratch_shapes=[pltpu.VMEM(shape, BF) for shape in held]
        + [pltpu.VMEM(shape, F32) for shape in outs]
        + [
            pltpu.VMEM((inv_mid.shape[0] + inv_top.shape[0], width), BF),
            pltpu.VMEM((inv_group.shape[0], width), BF),
            pltpu.VMEM((width, dense.shape[0]), BF),
            pltpu.SemaphoreType.DMA((5,)),
            pltpu.SemaphoreType.DMA((2,)),
            pltpu.SemaphoreType.DMA((len(outs),)),
        ],
        compiler_params=pltpu.CompilerParams(vmem_limit_bytes=BIG),
        name="backward",
    )(*in_vmem(*close), *in_hbm(*far))


def swap(x, axis, size, bits):
    return lax.ppermute(x, axis, [(i, i ^ bits) for i in range(size)])


def swaps(x, axis, size, unit=1):
    return [x] + [swap(x, axis, size, unit * k) for k in range(1, size // unit)]


def after(x, *others):
    return lax.optimization_barrier((x, others))[0]


def body(
    n_leaf,
    n_grp,
    rhs_leaf,
    rhs_group,
    rhs_middle,
    rhs_top,
    inv_leaf,
    inv_group,
    inv_middle,
    inv_top,
    leaf_tiles,
    tile_column,
    tile_target,
    tile_count,
    group_panel,
    middle_panel,
):
    n_pos = n_grp // 2
    group_cols = rhs_group.shape[1]
    mid_cols = rhs_middle.shape[0]
    upper_cols = mid_cols + rhs_top.shape[0]
    sec = upper_cols // n_grp
    q = sec // n_leaf
    gq = group_cols // n_grp
    leaf, pos, core = place()
    by_parts = middle_panel.shape[0] % 16 == 0
    pos_groups = [[2 * p + c for p in range(n_pos)] for c in range(2)]
    with jax.named_scope("gather_group_panel"):
        panel = lax.all_gather(group_panel[0], "grp", axis_index_groups=pos_groups)
    with jax.named_scope("gather_middle_panel"):
        if by_parts:
            middles = swaps(middle_panel, "grp", n_grp, 2)
        else:
            middle = lax.all_gather(middle_panel, ("leaf", "grp"), axis=0, tiled=True)
    begin = sec * lax.axis_index("grp") + q * leaf
    low = lax.dynamic_slice_in_dim(rhs_middle, jnp.minimum(begin, mid_cols - q), q, 0)
    high = lax.dynamic_slice_in_dim(rhs_top, jnp.maximum(begin - mid_cols, 0), q, 0)
    rhs_mine = jnp.where(begin < mid_cols, low, high)
    keep, *send, inv_here, leaf_solved, dense = leaf_forward(
        rhs_leaf[0],
        inv_leaf[0],
        leaf_tiles[0],
        tile_column,
        tile_target,
        tile_count,
        inv_group[0],
        rhs_group[0],
        sec,
        upper_cols,
    )
    with jax.named_scope("swap_cores"):
        if by_parts:
            send = after(send, middles)
        recv = [swap(x, "grp", n_grp, 1) for x in send]
    with jax.named_scope("gather_middle_panel"):
        if by_parts:
            middles = swaps(stack(after(middles, send)), "leaf", n_leaf)
            recv = after(recv, middles)
            middle = stack(after(middles, rhs_mine))
    parts, group = fold(keep, recv, inv_here, panel, n_leaf)
    with jax.named_scope("sum_over_leaf"):
        parts = parts[:1] + [swap(parts[k], "leaf", n_leaf, k) for k in range(1, n_leaf)]
    with jax.named_scope("gather_middle_panel"):
        if by_parts:
            other = swap(after(middle, group), "grp", n_grp, 1)
            middle = weave(middle, other, n_leaf, n_pos)
    sends = sum_leaf(parts, group, n_pos)
    with jax.named_scope("sum_over_pos"):
        got = sends[:1] + [swap(sends[k], "grp", n_grp, 2 * k) for k in range(1, n_pos)]
    with jax.named_scope("swap_group_panel"):
        panel_other = swap(after(panel, sends), "grp", n_grp, 1)
    residual = sum_pos(rhs_mine, got)
    with jax.named_scope("gather_pos"):
        uppers, groups = stack_pos(swaps(residual, "grp", n_grp, 2), q)
    with jax.named_scope("gather_leaf"):
        stacks = swaps(uppers, "leaf", n_leaf)
    with jax.named_scope("gather_cores"):
        mine = stack(after(stacks, (panel_other, middle)) + [groups])
        theirs = swap(mine, "grp", n_grp, 1)
    leaf_out, group_out, mid_out, top_out = backward(
        (mine, theirs, inv_middle, middle),
        (inv_top, inv_group[0], panel, panel_other, leaf_solved, inv_leaf[0], dense),
        n_leaf,
        n_pos,
    )
    return leaf_out[None], group_out[None], mid_out, top_out


def solution(mesh):
    n_leaf = mesh.shape["leaf"]
    n_grp = mesh.shape["grp"]
    placed = (
        P("leaf", "grp", None),
        P("leaf", None, None),
        P(),
        P(),
        P("leaf", "grp", None, None),
        P("leaf", None, None),
        P(),
        P(),
        P("leaf", "grp", None, None),
        P("leaf", "grp"),
        P("leaf", "grp"),
        P("leaf", "grp"),
        P("leaf", "grp", None),
        P(("leaf", "grp"), None),
    )
    return jax.shard_map(
        functools.partial(body, n_leaf, n_grp),
        mesh=mesh,
        in_specs=placed,
        out_specs=(P("leaf", "grp", None), P("leaf", None, None), P(), P()),
        check_vma=False,
    )
```

```python
import functools

import jax
import jax.numpy as jnp
from jax import lax
from jax.experimental import pallas as pl
from jax.experimental.pallas import tpu as pltpu
from jax.sharding import PartitionSpec as P

BF = jnp.bfloat16
F32 = jnp.float32
MIB = 1024 * 1024
CHUNKS = 16
UNROLL = 4
HBM = pl.BlockSpec(memory_space=pltpu.HBM)
VMEM = pl.BlockSpec(memory_space=pltpu.VMEM)
BIG = 40 * MIB
SMALL = 6 * MIB


def in_hbm(*arrays):
    return [pltpu.with_memory_space_constraint(x, pltpu.HBM) for x in arrays]


def in_vmem(*arrays):
    return [pltpu.with_memory_space_constraint(x, pltpu.VMEM) for x in arrays]


def small(kernel, name, shapes, scratch, *args):
    return pl.pallas_call(
        kernel,
        out_shape=[pltpu.VMEM(shape, BF) for shape in shapes],
        in_specs=[VMEM] * len(args),
        out_specs=[VMEM] * len(shapes),
        scratch_shapes=scratch,
        compiler_params=pltpu.CompilerParams(vmem_limit_bytes=SMALL),
        name=name,
    )(*in_vmem(*args))


def dot(a, b):
    return jnp.dot(a, b, preferred_element_type=F32)


def place():
    g = lax.axis_index("grp")
    return lax.axis_index("leaf"), g >> 1, g & 1


def forward_kernel(
    n_pos,
    sec,
    group_cols,
    count_hbm,
    cols_hbm,
    tgts_hbm,
    rhs_hbm,
    inv_hbm,
    tiles_hbm,
    inv_group_hbm,
    rhs_group_hbm,
    keep,
    send_low,
    send_high,
    inv_group,
    solved_hbm,
    dense_hbm,
    count,
    cols,
    tgts,
    rhs,
    inv,
    tiles,
    acc,
    stage,
    solved,
    dense,
    rhs_group,
    in_sems,
    tile_sems,
    out_sems,
    pass_sems,
):
    slots, block, _ = tiles.shape
    supernodes = inv.shape[0]
    targets = acc.shape[0]
    chunks = tile_sems.shape[0]
    step = slots // chunks
    _, _, core = place()

    def tile_copy(k):
        span = pl.ds(k * step, step)
        return pltpu.make_async_copy(tiles_hbm.at[span], tiles.at[span], tile_sems.at[k])

    pairs = (
        (count_hbm, count),
        (cols_hbm, cols),
        (tgts_hbm, tgts),
        (rhs_hbm, rhs),
        (inv_hbm, inv),
    )
    loads = [pltpu.make_async_copy(a, b, in_sems.at[i]) for i, (a, b) in enumerate(pairs)]
    for load in loads:
        load.start()
    for k in range(chunks):
        tile_copy(k).start()
    pairs = ((inv_group_hbm, inv_group), (rhs_group_hbm, rhs_group))
    passes = [pltpu.make_async_copy(a, b, pass_sems.at[i]) for i, (a, b) in enumerate(pairs)]
    for copy in passes:
        copy.start()

    acc[...] = jnp.zeros_like(acc)
    for load in loads:
        load.wait()
    for s in range(supernodes):
        rows = pl.ds(s * block, block)
        solved[rows, :] = dot(inv[s], rhs[rows, :].astype(BF)).astype(BF)
    stores = [pltpu.make_async_copy(solved, solved_hbm, out_sems.at[0])]
    stores[0].start()

    live = count[0, 0]

    def add(p):
        t = tgts[0, p]
        c = cols[0, p]
        acc[t, c] = acc[t, c] + tiles[p].astype(F32)

    def add_some(i, carry):
        for u in range(UNROLL):
            add(i * UNROLL + u)
        return carry

    def add_one(p, carry):
        add(p)
        return carry

    whole = live // UNROLL
    per = step // UNROLL
    for k in range(chunks):
        tile_copy(k).wait()
        lax.fori_loop(k * per, jnp.clip(whole, k * per, (k + 1) * per), add_some, 0)
    lax.fori_loop(whole * UNROLL, live, add_one, 0)

    span = group_cols
    blocks = span // block
    for i in range(targets // blocks):
        for t in range(i * blocks, (i + 1) * blocks):
            for c in range(supernodes):
                dense[t * block : (t + 1) * block, c * block : (c + 1) * block] = acc[t, c].astype(BF)
        rows = pl.ds(i * span, span)
        stores.append(pltpu.make_async_copy(dense.at[rows], dense_hbm.at[rows], out_sems.at[1 + i]))
        stores[-1].start()
        total = dot(dense[rows, :], solved[...])
        if i == 0:
            passes[1].wait()
            share = jnp.where(core == 0, 1.0 / n_pos, 0.0)
            total = (total - rhs_group[...] * share).astype(BF)
            stage[0, 0:span, :] = total
            stage[1, 0:span, :] = total
        else:
            total = total.astype(BF)
            for q in range(0, span, sec):
                section = ((i - 1) * span + q) // sec
                begin = group_cols + (section // 2) * sec
                stage[(section % 2) ^ core, begin : begin + sec, :] = total[q : q + sec, :]
    keep[...] = stage[0]
    cut = send_low.shape[0]
    send_low[...] = stage[1, 0:cut, :]
    send_high[...] = stage[1, cut:, :]
    for copy in passes[:1] + stores:
        copy.wait()


def leaf_forward(
    rhs, inverse, tiles, cols, tgts, count, inv_group, rhs_group, sec, upper_cols
):
    group_cols = rhs_group.shape[0]
    slots, block, _ = tiles.shape
    supernodes = inverse.shape[0]
    targets = (group_cols + upper_cols) // block
    width = rhs.shape[-1]
    half = group_cols + upper_cols // 2
    return pl.pallas_call(
        functools.partial(forward_kernel, upper_cols // (2 * sec), sec, group_cols),
        out_shape=(
            pltpu.VMEM((half, width), BF),
            pltpu.VMEM((half // 2, width), BF),
            pltpu.VMEM((half // 2, width), BF),
            pltpu.VMEM(inv_group.shape, BF),
            pltpu.HBM((supernodes * block, width), BF),
            pltpu.HBM((targets * block, supernodes * block), BF),
        ),
        in_specs=[HBM] * 8,
        out_specs=(VMEM,) * 4 + (HBM,) * 2,
        scratch_shapes=[
            pltpu.SMEM(count.shape, count.dtype),
            pltpu.SMEM(cols.shape, cols.dtype),
            pltpu.SMEM(tgts.shape, tgts.dtype),
            pltpu.VMEM(rhs.shape, rhs.dtype),
            pltpu.VMEM(inverse.shape, inverse.dtype),
            pltpu.VMEM((slots, block, block), BF),
            pltpu.VMEM((targets, supernodes, block, block), F32),
            pltpu.VMEM((2, half, width), BF),
            pltpu.VMEM((supernodes * block, width), BF),
            pltpu.VMEM((targets * block, supernodes * block), BF),
            pltpu.VMEM(rhs_group.shape, F32),
            pltpu.SemaphoreType.DMA((5,)),
            pltpu.SemaphoreType.DMA((CHUNKS,)),
            pltpu.SemaphoreType.DMA((1 + targets * block // group_cols,)),
            pltpu.SemaphoreType.DMA((2,)),
        ],
        compiler_params=pltpu.CompilerParams(vmem_limit_bytes=BIG),
        cost_estimate=pl.CostEstimate(
            flops=2 * targets * block * supernodes * block * width,
            bytes_accessed=2 * tiles.size + 4 * rhs.size,
            transcendentals=0,
        ),
        name="leaf_forward",
    )(count, *in_hbm(cols, tgts, rhs, inverse, tiles, inv_group, rhs_group))


def total_of(refs):
    total = refs[0][...].astype(F32)
    for ref in refs[1:]:
        total = total + ref[...].astype(F32)
    return total


def fold_kernel(n_leaf, n_pos, keep, low, high, inv, late, *refs):
    early, refs = refs[:n_pos], refs[n_pos:]
    parts, group, (gsum, base, stage) = refs[:n_leaf], refs[n_leaf], refs[n_leaf + 1 :]
    leaf, pos, core = place()
    group_cols = inv.shape[0]
    first = early[0].shape[0]
    sec = first + late.shape[1]
    q = sec // n_leaf
    gq = group_cols // (2 * n_pos)
    cut = low.shape[0]
    gsum[...] = keep[0:group_cols, :].astype(F32) + low[0:group_cols, :].astype(F32)
    base[0 : cut - group_cols, :] = keep[group_cols:cut, :].astype(F32) + low[group_cols:, :].astype(F32)
    base[cut - group_cols :, :] = keep[cut:, :].astype(F32) + high[...].astype(F32)
    solved = dot(inv[...], (-gsum[...]).astype(BF)).astype(BF)
    for k in range(n_pos):
        p = pos ^ k
        for begin, panel in ((0, early[k]), (first, late.at[2 * p + core])):
            span = panel.shape[0]
            rows = pl.ds(pl.multiple_of(p * sec + begin, first), span)
            terms = (dot(panel[...], solved) + base[rows, :]).astype(BF)
            for j in range(begin // q, (begin + span) // q):
                stage[j ^ leaf, k * q : (k + 1) * q, :] = terms[j * q - begin : (j + 1) * q - begin, :]
        begin = pl.multiple_of(core * (group_cols // 2) + p * gq, gq)
        group[k * gq : (k + 1) * gq, :] = gsum[pl.ds(begin, gq), :].astype(BF)
    for k in range(n_leaf):
        parts[k][...] = stage[k]


def fold(keep, recv, inverse, early, late, n_leaf):
    width = keep.shape[-1]
    n_pos = len(early)
    sec = early[0].shape[0] + late.shape[1]
    part = (n_pos * sec // n_leaf, width)
    outs = small(
        functools.partial(fold_kernel, n_leaf, n_pos),
        "fold_group",
        [part] * n_leaf + [(inverse.shape[0] // 2, width)],
        [
            pltpu.VMEM((inverse.shape[0], width), F32),
            pltpu.VMEM((n_pos * sec, width), F32),
            pltpu.VMEM((n_leaf,) + part, BF),
        ],
        keep,
        *recv,
        inverse,
        late,
        *early,
    )
    return list(outs[:n_leaf]), outs[n_leaf]


def sum_leaf_kernel(n_leaf, *refs):
    group, outs = refs[n_leaf], refs[n_leaf + 1 :]
    n_pos = len(outs)
    q = refs[0].shape[0] // n_pos
    gq = group.shape[0] // n_pos
    total = total_of(refs[:n_leaf]).astype(BF)
    for k, out in enumerate(outs):
        out[0:q, :] = total[k * q : (k + 1) * q, :]
        out[q:, :] = group[k * gq : (k + 1) * gq, :]


def sum_leaf(parts, group, n_pos):
    rows = (parts[0].shape[0] + group.shape[0]) // n_pos
    kernel = functools.partial(sum_leaf_kernel, len(parts))
    shapes = [(rows, group.shape[1])] * n_pos
    return list(small(kernel, "sum_leaf", shapes, [], *parts, group))


def sum_pos_kernel(high, *refs):
    parts, out = refs[:-1], refs[-1]
    q = high.shape[0]
    total = total_of(parts)
    out[0:q, :] = (high[...] - total[0:q, :]).astype(BF)
    out[q:, :] = (-total[q:, :]).astype(BF)


def sum_pos(high, parts):
    return small(sum_pos_kernel, "sum_pos", [parts[0].shape], [], high, *parts)[0]


def stack_pos_kernel(q, *refs):
    parts, (uppers, groups) = refs[:-2], refs[-2:]
    gq = parts[0].shape[0] - q
    for k, part in enumerate(parts):
        uppers[k * q : (k + 1) * q, :] = part[0:q, :]
        groups[k * gq : (k + 1) * gq, :] = part[q:, :]


def stack_pos(parts, q):
    n_pos, (rows, width) = len(parts), parts[0].shape
    shapes = [(n_pos * q, width), (n_pos * (rows - q), width)]
    return small(functools.partial(stack_pos_kernel, q), "stack_pos", shapes, [], *parts)


def stack_kernel(*refs):
    begin = 0
    for part in refs[:-1]:
        rows = part.shape[0]
        refs[-1][begin : begin + rows, :] = part[...]
        begin += rows


def stack(parts):
    rows = sum(part.shape[0] for part in parts)
    return small(stack_kernel, "stack", [(rows, parts[0].shape[1])], [], *parts)[0]


def weave_kernel(n_leaf, gathered, out, sems):
    leaf, _, _ = place()
    n_grp = gathered.shape[0]
    rows = gathered.shape[1] // n_leaf
    loads = []
    for g in range(n_grp):
        for k in range(n_leaf):
            begin = pl.multiple_of(((leaf ^ k) * n_grp + g) * rows, rows)
            got = gathered.at[g, pl.ds(k * rows, rows)]
            target = out.at[pl.ds(begin, rows)]
            loads.append(pltpu.make_async_copy(got, target, sems.at[g * n_leaf + k]))
    for load in loads:
        load.start()
    for load in loads:
        load.wait()


def weave(gathered, n_leaf):
    n_grp, rows, cols = gathered.shape
    return pl.pallas_call(
        functools.partial(weave_kernel, n_leaf),
        out_shape=pltpu.VMEM((n_grp * rows, cols), BF),
        in_specs=[HBM],
        out_specs=VMEM,
        scratch_shapes=[pltpu.SemaphoreType.DMA((n_grp * n_leaf,))],
        compiler_params=pltpu.CompilerParams(vmem_limit_bytes=SMALL),
        name="weave",
    )(*in_hbm(gathered))


def lower_dot(lower, x):
    n = lower.shape[0]
    step = n // 4
    parts = []
    for i in range(0, n, step):
        parts.append(dot(lower[i : i + step, 0 : i + step], x[0 : i + step, :]))
    return jnp.concatenate(parts, axis=0)


def dot_lower(x, lower):
    n = lower.shape[0]
    step = n // 4
    parts = []
    for i in range(0, n, step):
        parts.append(dot(x[:, i:], lower[i:, i : i + step]))
    return jnp.concatenate(parts, axis=1)


def backward_kernel(
    n_leaf,
    n_pos,
    mine,
    theirs,
    inv_mid,
    panel_mid,
    inv_top_hbm,
    inv_group_hbm,
    panel_own_hbm,
    panel_other_hbm,
    panel_late_hbm,
    leaf_solved_hbm,
    inv_leaf_hbm,
    dense_hbm,
    leaf_hbm,
    group_hbm,
    mid_hbm,
    top_hbm,
    inv_top,
    inv_group,
    panel_group,
    leaf_solved,
    inv_leaf,
    dense,
    leaf_out,
    group_out,
    mid_out,
    top_out,
    upper,
    residual,
    above,
    sems,
    panel_sems,
    out_sems,
):
    leaf, pos, core = place()
    pairs = (
        (inv_top_hbm, inv_top),
        (inv_group_hbm, inv_group),
        (leaf_solved_hbm, leaf_solved),
        (inv_leaf_hbm, inv_leaf),
        (dense_hbm, dense),
    )
    loads = [pltpu.make_async_copy(a, b, sems.at[i]) for i, (a, b) in enumerate(pairs)]
    first = panel_own_hbm.shape[0] // n_pos
    panel_loads = []
    for kc, got in enumerate((panel_own_hbm, panel_other_hbm)):
        for k in range(n_pos):
            target = panel_group.at[pos ^ k, core ^ kc, pl.ds(0, first)]
            sem = panel_sems.at[kc * n_pos + k]
            rows = pl.ds(k * first, first)
            panel_loads.append(pltpu.make_async_copy(got.at[rows], target, sem))
    for p in range(n_pos):
        for c in range(2):
            got = panel_late_hbm.at[2 * p + c]
            target = panel_group.at[p, c, pl.ds(first, got.shape[0])]
            sem = panel_sems.at[2 * n_pos + 2 * p + c]
            panel_loads.append(pltpu.make_async_copy(got, target, sem))
    for load in loads[:2] + panel_loads + loads[2:]:
        load.start()
    loads = loads + panel_loads
    mid_rows = inv_mid.shape[0]
    top_rows = inv_top.shape[0]
    group_rows = inv_group.shape[0]
    supernodes, block, _ = inv_leaf.shape
    upper_cols = pl.ds(group_rows, mid_rows + top_rows)
    mid_cols = pl.ds(group_rows, mid_rows)
    top_cols = pl.ds(group_rows + mid_rows, top_rows)
    sec = (mid_rows + top_rows) // (2 * n_pos)
    q = sec // n_leaf
    gq = group_rows // (2 * n_pos)
    for kc, got in enumerate((mine, theirs)):
        for kz in range(n_pos):
            for kl in range(n_leaf):
                row = sec * (2 * (pos ^ kz) + (core ^ kc)) + q * (leaf ^ kl)
                begin = (kl * n_pos + kz) * q
                upper[pl.ds(pl.multiple_of(row, q), q), :] = got[begin : begin + q, :]
            row = (group_rows // 2) * (core ^ kc) + gq * (pos ^ kz)
            begin = n_leaf * n_pos * q + kz * gq
            residual[pl.ds(pl.multiple_of(row, gq), gq), :] = got[begin : begin + gq, :]

    mid_solved = lower_dot(inv_mid, upper[0:mid_rows, :]).astype(BF)
    top_residual = upper[mid_rows:, :].astype(F32) - dot(panel_mid[...], mid_solved)
    loads[0].wait()
    top_solved = lower_dot(inv_top, top_residual.astype(BF))
    top_t = dot_lower(top_solved.T.astype(BF), inv_top)
    above[:, top_cols] = top_t.astype(BF)
    top_out[...] = top_t.T
    stores = [pltpu.make_async_copy(top_out, top_hbm, out_sems.at[0])]
    stores[0].start()
    mid_back = mid_solved.astype(F32).T - dot(above[:, top_cols], panel_mid[...])
    mid_t = dot_lower(mid_back.astype(BF), inv_mid)
    above[:, mid_cols] = mid_t.astype(BF)
    mid_out[...] = mid_t.T
    stores.append(pltpu.make_async_copy(mid_out, mid_hbm, out_sems.at[1]))
    stores[1].start()
    for load in loads[1:]:
        load.wait()
    group_solved = dot(inv_group[...], residual[...]).astype(BF).astype(F32).T
    panel = panel_group[...].reshape(mid_rows + top_rows, group_rows)
    group_back = group_solved - dot(above[:, upper_cols], panel)
    group_t = dot(group_back.astype(BF), inv_group[...])
    above[:, 0:group_rows] = group_t.astype(BF)
    group_out[...] = group_t.T
    stores.append(pltpu.make_async_copy(group_out, group_hbm, out_sems.at[2]))
    stores[2].start()
    for s in range(supernodes):
        cols = pl.ds(s * block, block)
        terms = dot(above[...], dense[:, cols])
        back = (leaf_solved[cols, :].astype(F32).T - terms).astype(BF)
        leaf_out[cols, :] = dot(back, inv_leaf[s]).T
    stores.append(pltpu.make_async_copy(leaf_out, leaf_hbm, out_sems.at[3]))
    stores[3].start()
    for store in stores:
        store.wait()


def backward(close, far, n_leaf, n_pos):
    mine, _, inv_mid, _ = close
    inv_top, inv_group, panel, _, late, leaf_solved, inv_leaf, dense = far
    sec = panel.shape[0] // n_pos + late.shape[1]
    width = mine.shape[-1]
    held = (inv_top.shape, inv_group.shape, (n_pos, 2, sec, late.shape[2]))
    held += (leaf_solved.shape, inv_leaf.shape, dense.shape)
    outs = (
        leaf_solved.shape,
        (inv_group.shape[0], width),
        (inv_mid.shape[0], width),
        (inv_top.shape[0], width),
    )
    return pl.pallas_call(
        functools.partial(backward_kernel, n_leaf, n_pos),
        out_shape=[pltpu.HBM(shape, F32) for shape in outs],
        in_specs=[VMEM] * len(close) + [HBM] * len(far),
        out_specs=[HBM] * 4,
        scratch_shapes=[pltpu.VMEM(shape, BF) for shape in held]
        + [pltpu.VMEM(shape, F32) for shape in outs]
        + [
            pltpu.VMEM((inv_mid.shape[0] + inv_top.shape[0], width), BF),
            pltpu.VMEM((inv_group.shape[0], width), BF),
            pltpu.VMEM((width, dense.shape[0]), BF),
            pltpu.SemaphoreType.DMA((5,)),
            pltpu.SemaphoreType.DMA((4 * n_pos,)),
            pltpu.SemaphoreType.DMA((len(outs),)),
        ],
        compiler_params=pltpu.CompilerParams(vmem_limit_bytes=BIG),
        name="backward",
    )(*in_vmem(*close), *in_hbm(*far))


def swap(x, axis, size, bits):
    return lax.ppermute(x, axis, [(i, i ^ bits) for i in range(size)])


def swaps(x, axis, size, unit=1):
    return [x] + [swap(x, axis, size, unit * k) for k in range(1, size // unit)]


def after(x, *others):
    return lax.optimization_barrier((x, others))[0]


def body(
    n_leaf,
    n_grp,
    rhs_leaf,
    rhs_group,
    rhs_middle,
    rhs_top,
    inv_leaf,
    inv_group,
    inv_middle,
    inv_top,
    leaf_tiles,
    tile_column,
    tile_target,
    tile_count,
    group_panel,
    middle_panel,
):
    n_pos = n_grp // 2
    group_cols = rhs_group.shape[1]
    mid_cols = rhs_middle.shape[0]
    upper_cols = mid_cols + rhs_top.shape[0]
    sec = upper_cols // n_grp
    q = sec // n_leaf
    gq = group_cols // n_grp
    leaf, pos, core = place()
    by_parts = middle_panel.shape[0] % 16 == 0
    first = sec // 2
    with jax.named_scope("gather_group_panel"):
        late = lax.all_gather(group_panel[0, first:], "grp")
        early = swaps(group_panel[0, :first], "grp", n_grp, 2)
    with jax.named_scope("gather_middle_panel"):
        if by_parts:
            middles = swaps(middle_panel, "leaf", n_leaf)
        else:
            middle = lax.all_gather(middle_panel, ("leaf", "grp"), axis=0, tiled=True)
    begin = sec * lax.axis_index("grp") + q * leaf
    low = lax.dynamic_slice_in_dim(rhs_middle, jnp.minimum(begin, mid_cols - q), q, 0)
    high = lax.dynamic_slice_in_dim(rhs_top, jnp.maximum(begin - mid_cols, 0), q, 0)
    rhs_mine = jnp.where(begin < mid_cols, low, high)
    keep, *send, inv_here, leaf_solved, dense = leaf_forward(
        rhs_leaf[0],
        inv_leaf[0],
        leaf_tiles[0],
        tile_column,
        tile_target,
        tile_count,
        inv_group[0],
        rhs_group[0],
        sec,
        upper_cols,
    )
    with jax.named_scope("swap_cores"):
        recv = [swap(x, "grp", n_grp, 1) for x in send]
    with jax.named_scope("gather_middle_panel"):
        if by_parts:
            middle = stack(after(middles, (keep, early)))
            middle = lax.all_gather(middle, "grp")
    parts, group = fold(keep, recv, inv_here, after(early, rhs_mine), late, n_leaf)
    with jax.named_scope("sum_over_leaf"):
        parts = parts[:1] + [swap(parts[k], "leaf", n_leaf, k) for k in range(1, n_leaf)]
    sends = sum_leaf(parts, group, n_pos)
    with jax.named_scope("sum_over_pos"):
        got = sends[:1] + [swap(sends[k], "grp", n_grp, 2 * k) for k in range(1, n_pos)]
    with jax.named_scope("swap_group_panel"):
        early = stack(after(early, sends))
        early_other = swap(early, "grp", n_grp, 1)
    residual = sum_pos(rhs_mine, got)
    with jax.named_scope("gather_pos"):
        uppers, groups = stack_pos(swaps(residual, "grp", n_grp, 2), q)
    with jax.named_scope("gather_leaf"):
        stacks = swaps(uppers, "leaf", n_leaf)
    with jax.named_scope("gather_cores"):
        if by_parts:
            middle = weave(middle, n_leaf)
        mine = stack(after(stacks, (early_other, middle)) + [groups])
        theirs = swap(mine, "grp", n_grp, 1)
    leaf_out, group_out, mid_out, top_out = backward(
        (mine, theirs, inv_middle, middle),
        (inv_top, inv_group[0], early, early_other, late, leaf_solved, inv_leaf[0], dense),
        n_leaf,
        n_pos,
    )
    return leaf_out[None], group_out[None], mid_out, top_out


def solution(mesh):
    n_leaf = mesh.shape["leaf"]
    n_grp = mesh.shape["grp"]
    placed = (
        P("leaf", "grp", None),
        P("leaf", None, None),
        P(),
        P(),
        P("leaf", "grp", None, None),
        P("leaf", None, None),
        P(),
        P(),
        P("leaf", "grp", None, None),
        P("leaf", "grp"),
        P("leaf", "grp"),
        P("leaf", "grp"),
        P("leaf", "grp", None),
        P(("leaf", "grp"), None),
    )
    return jax.shard_map(
        functools.partial(body, n_leaf, n_grp),
        mesh=mesh,
        in_specs=placed,
        out_specs=(P("leaf", "grp", None), P("leaf", None, None), P(), P()),
        check_vma=False,
    )
```

```python
import functools

import jax
import jax.numpy as jnp
from jax import lax
from jax.experimental import pallas as pl
from jax.experimental.pallas import tpu as pltpu
from jax.sharding import PartitionSpec as P

BF = jnp.bfloat16
F32 = jnp.float32
MIB = 1024 * 1024
CHUNKS = 16
UNROLL = 4
HBM = pl.BlockSpec(memory_space=pltpu.HBM)
VMEM = pl.BlockSpec(memory_space=pltpu.VMEM)
BIG = 40 * MIB
SMALL = 6 * MIB


def in_hbm(*arrays):
    return [pltpu.with_memory_space_constraint(x, pltpu.HBM) for x in arrays]


def in_vmem(*arrays):
    return [pltpu.with_memory_space_constraint(x, pltpu.VMEM) for x in arrays]


def small(kernel, name, shapes, scratch, *args):
    return pl.pallas_call(
        kernel,
        out_shape=[pltpu.VMEM(shape, BF) for shape in shapes],
        in_specs=[VMEM] * len(args),
        out_specs=[VMEM] * len(shapes),
        scratch_shapes=scratch,
        compiler_params=pltpu.CompilerParams(vmem_limit_bytes=SMALL),
        name=name,
    )(*in_vmem(*args))


def dot(a, b):
    return jnp.dot(a, b, preferred_element_type=F32)


def place():
    g = lax.axis_index("grp")
    return lax.axis_index("leaf"), g >> 1, g & 1


def forward_kernel(
    n_pos,
    sec,
    group_cols,
    count_hbm,
    cols_hbm,
    tgts_hbm,
    rhs_hbm,
    inv_hbm,
    tiles_hbm,
    inv_group_hbm,
    rhs_group_hbm,
    keep,
    send_low,
    send_high,
    inv_group,
    solved_hbm,
    dense_hbm,
    count,
    cols,
    tgts,
    rhs,
    inv,
    tiles,
    acc,
    stage,
    solved,
    dense,
    rhs_group,
    in_sems,
    tile_sems,
    out_sems,
    pass_sems,
):
    slots, block, _ = tiles.shape
    supernodes = inv.shape[0]
    targets = acc.shape[0]
    chunks = tile_sems.shape[0]
    step = slots // chunks
    _, _, core = place()

    def tile_copy(k):
        span = pl.ds(k * step, step)
        return pltpu.make_async_copy(tiles_hbm.at[span], tiles.at[span], tile_sems.at[k])

    pairs = (
        (count_hbm, count),
        (cols_hbm, cols),
        (tgts_hbm, tgts),
        (rhs_hbm, rhs),
        (inv_hbm, inv),
    )
    loads = [pltpu.make_async_copy(a, b, in_sems.at[i]) for i, (a, b) in enumerate(pairs)]
    for load in loads:
        load.start()
    for k in range(chunks):
        tile_copy(k).start()
    pairs = ((inv_group_hbm, inv_group), (rhs_group_hbm, rhs_group))
    passes = [pltpu.make_async_copy(a, b, pass_sems.at[i]) for i, (a, b) in enumerate(pairs)]
    for copy in passes:
        copy.start()

    acc[...] = jnp.zeros_like(acc)
    for load in loads:
        load.wait()
    for s in range(supernodes):
        rows = pl.ds(s * block, block)
        solved[rows, :] = dot(inv[s], rhs[rows, :].astype(BF)).astype(BF)
    stores = [pltpu.make_async_copy(solved, solved_hbm, out_sems.at[0])]
    stores[0].start()

    live = count[0, 0]

    def add(p):
        t = tgts[0, p]
        c = cols[0, p]
        acc[t, c] = acc[t, c] + tiles[p].astype(F32)

    def add_some(i, carry):
        for u in range(UNROLL):
            add(i * UNROLL + u)
        return carry

    def add_one(p, carry):
        add(p)
        return carry

    whole = live // UNROLL
    per = step // UNROLL
    for k in range(chunks):
        tile_copy(k).wait()
        lax.fori_loop(k * per, jnp.clip(whole, k * per, (k + 1) * per), add_some, 0)
    lax.fori_loop(whole * UNROLL, live, add_one, 0)

    span = group_cols
    blocks = span // block
    for i in range(targets // blocks):
        for t in range(i * blocks, (i + 1) * blocks):
            for c in range(supernodes):
                dense[t * block : (t + 1) * block, c * block : (c + 1) * block] = acc[t, c].astype(BF)
        rows = pl.ds(i * span, span)
        stores.append(pltpu.make_async_copy(dense.at[rows], dense_hbm.at[rows], out_sems.at[1 + i]))
        stores[-1].start()
        total = dot(dense[rows, :], solved[...])
        if i == 0:
            passes[1].wait()
            share = jnp.where(core == 0, 1.0 / n_pos, 0.0)
            total = (total - rhs_group[...] * share).astype(BF)
            stage[0, 0:span, :] = total
            stage[1, 0:span, :] = total
        else:
            total = total.astype(BF)
            for q in range(0, span, sec):
                section = ((i - 1) * span + q) // sec
                begin = group_cols + (section // 2) * sec
                stage[(section % 2) ^ core, begin : begin + sec, :] = total[q : q + sec, :]
    keep[...] = stage[0]
    cut = send_low.shape[0]
    send_low[...] = stage[1, 0:cut, :]
    send_high[...] = stage[1, cut:, :]
    for copy in passes[:1] + stores:
        copy.wait()


def leaf_forward(
    rhs, inverse, tiles, cols, tgts, count, inv_group, rhs_group, sec, upper_cols
):
    group_cols = rhs_group.shape[0]
    slots, block, _ = tiles.shape
    supernodes = inverse.shape[0]
    targets = (group_cols + upper_cols) // block
    width = rhs.shape[-1]
    half = group_cols + upper_cols // 2
    return pl.pallas_call(
        functools.partial(forward_kernel, upper_cols // (2 * sec), sec, group_cols),
        out_shape=(
            pltpu.VMEM((half, width), BF),
            pltpu.VMEM((half // 2, width), BF),
            pltpu.VMEM((half // 2, width), BF),
            pltpu.VMEM(inv_group.shape, BF),
            pltpu.HBM((supernodes * block, width), BF),
            pltpu.HBM((targets * block, supernodes * block), BF),
        ),
        in_specs=[HBM] * 8,
        out_specs=(VMEM,) * 4 + (HBM,) * 2,
        scratch_shapes=[
            pltpu.SMEM(count.shape, count.dtype),
            pltpu.SMEM(cols.shape, cols.dtype),
            pltpu.SMEM(tgts.shape, tgts.dtype),
            pltpu.VMEM(rhs.shape, rhs.dtype),
            pltpu.VMEM(inverse.shape, inverse.dtype),
            pltpu.VMEM((slots, block, block), BF),
            pltpu.VMEM((targets, supernodes, block, block), F32),
            pltpu.VMEM((2, half, width), BF),
            pltpu.VMEM((supernodes * block, width), BF),
            pltpu.VMEM((targets * block, supernodes * block), BF),
            pltpu.VMEM(rhs_group.shape, F32),
            pltpu.SemaphoreType.DMA((5,)),
            pltpu.SemaphoreType.DMA((CHUNKS,)),
            pltpu.SemaphoreType.DMA((1 + targets * block // group_cols,)),
            pltpu.SemaphoreType.DMA((2,)),
        ],
        compiler_params=pltpu.CompilerParams(vmem_limit_bytes=BIG),
        cost_estimate=pl.CostEstimate(
            flops=2 * targets * block * supernodes * block * width,
            bytes_accessed=2 * tiles.size + 4 * rhs.size,
            transcendentals=0,
        ),
        name="leaf_forward",
    )(count, *in_hbm(cols, tgts, rhs, inverse, tiles, inv_group, rhs_group))


def total_of(refs):
    total = refs[0][...].astype(F32)
    for ref in refs[1:]:
        total = total + ref[...].astype(F32)
    return total


def fold_kernel(n_leaf, n_pos, keep, low, high, inv, panel, *refs):
    parts, group, (gsum, base, stage) = refs[:n_leaf], refs[n_leaf], refs[n_leaf + 1 :]
    leaf, pos, core = place()
    group_cols = inv.shape[0]
    sec = panel.shape[1]
    q = sec // n_leaf
    gq = group_cols // (2 * n_pos)
    cut = low.shape[0]
    gsum[...] = keep[0:group_cols, :].astype(F32) + low[0:group_cols, :].astype(F32)
    base[0 : cut - group_cols, :] = keep[group_cols:cut, :].astype(F32) + low[group_cols:, :].astype(F32)
    base[cut - group_cols :, :] = keep[cut:, :].astype(F32) + high[...].astype(F32)
    solved = dot(inv[...], (-gsum[...]).astype(BF)).astype(BF)
    for k in range(n_pos):
        p = pos ^ k
        rows = pl.ds(pl.multiple_of(p * sec, sec), sec)
        terms = (dot(panel[p], solved) + base[rows, :]).astype(BF)
        for j in range(n_leaf):
            stage[j ^ leaf, k * q : (k + 1) * q, :] = terms[j * q : (j + 1) * q, :]
        begin = pl.multiple_of(core * (group_cols // 2) + p * gq, gq)
        group[k * gq : (k + 1) * gq, :] = gsum[pl.ds(begin, gq), :].astype(BF)
    for k in range(n_leaf):
        parts[k][...] = stage[k]


def fold(keep, recv, inverse, panel, n_leaf):
    width = keep.shape[-1]
    n_pos, sec, _ = panel.shape
    part = (n_pos * sec // n_leaf, width)
    outs = small(
        functools.partial(fold_kernel, n_leaf, n_pos),
        "fold_group",
        [part] * n_leaf + [(inverse.shape[0] // 2, width)],
        [
            pltpu.VMEM((inverse.shape[0], width), F32),
            pltpu.VMEM((n_pos * sec, width), F32),
            pltpu.VMEM((n_leaf,) + part, BF),
        ],
        keep,
        *recv,
        inverse,
        panel,
    )
    return list(outs[:n_leaf]), outs[n_leaf]


def sum_leaf_kernel(n_leaf, *refs):
    group, outs = refs[n_leaf], refs[n_leaf + 1 :]
    n_pos = len(outs)
    q = refs[0].shape[0] // n_pos
    gq = group.shape[0] // n_pos
    total = total_of(refs[:n_leaf]).astype(BF)
    for k, out in enumerate(outs):
        out[0:q, :] = total[k * q : (k + 1) * q, :]
        out[q:, :] = group[k * gq : (k + 1) * gq, :]


def sum_leaf(parts, group, n_pos):
    rows = (parts[0].shape[0] + group.shape[0]) // n_pos
    kernel = functools.partial(sum_leaf_kernel, len(parts))
    shapes = [(rows, group.shape[1])] * n_pos
    return list(small(kernel, "sum_leaf", shapes, [], *parts, group))


def sum_pos_kernel(high, *refs):
    parts, out = refs[:-1], refs[-1]
    q = high.shape[0]
    total = total_of(parts)
    out[0:q, :] = (high[...] - total[0:q, :]).astype(BF)
    out[q:, :] = (-total[q:, :]).astype(BF)


def sum_pos(high, parts):
    return small(sum_pos_kernel, "sum_pos", [parts[0].shape], [], high, *parts)[0]


def stack_pos_kernel(q, *refs):
    parts, (uppers, groups) = refs[:-2], refs[-2:]
    gq = parts[0].shape[0] - q
    for k, part in enumerate(parts):
        uppers[k * q : (k + 1) * q, :] = part[0:q, :]
        groups[k * gq : (k + 1) * gq, :] = part[q:, :]


def stack_pos(parts, q):
    n_pos, (rows, width) = len(parts), parts[0].shape
    shapes = [(n_pos * q, width), (n_pos * (rows - q), width)]
    return small(functools.partial(stack_pos_kernel, q), "stack_pos", shapes, [], *parts)


def stack_kernel(*refs):
    begin = 0
    for part in refs[:-1]:
        rows = part.shape[0]
        refs[-1][begin : begin + rows, :] = part[...]
        begin += rows


def stack(parts):
    rows = sum(part.shape[0] for part in parts)
    return small(stack_kernel, "stack", [(rows, parts[0].shape[1])], [], *parts)[0]


def weave_kernel(n_leaf, n_pos, own, other, out):
    leaf, pos, core = place()
    rows = own.shape[0] // (n_leaf * n_pos)
    for kc, part in enumerate((own, other)):
        for kl in range(n_leaf):
            for k in range(n_pos):
                block = (leaf ^ kl) * (2 * n_pos) + 2 * (pos ^ k) + (core ^ kc)
                span = pl.ds(pl.multiple_of(block * rows, rows), rows)
                begin = (kl * n_pos + k) * rows
                out[span, :] = part[begin : begin + rows, :]


def weave(own, other, n_leaf, n_pos):
    shape = (2 * own.shape[0], own.shape[1])
    kernel = functools.partial(weave_kernel, n_leaf, n_pos)
    return small(kernel, "weave", [shape], [], own, other)[0]


def lower_dot(lower, x):
    n = lower.shape[0]
    step = min(n, max(n // 4, 256))
    parts = []
    for i in range(0, n, step):
        parts.append(dot(lower[i : i + step, 0 : i + step], x[0 : i + step, :]))
    return jnp.concatenate(parts, axis=0)


def dot_lower(x, lower):
    n = lower.shape[0]
    step = min(n, max(n // 4, 256))
    parts = []
    for i in range(0, n, step):
        parts.append(dot(x[:, i:], lower[i:, i : i + step]))
    return jnp.concatenate(parts, axis=1)


def backward_kernel(
    n_leaf,
    n_pos,
    mine,
    theirs,
    inv_mid,
    panel_mid,
    inv_top_hbm,
    inv_group_hbm,
    panel_own_hbm,
    panel_other_hbm,
    leaf_solved_hbm,
    inv_leaf_hbm,
    dense_hbm,
    leaf_hbm,
    group_hbm,
    mid_hbm,
    top_hbm,
    inv_top,
    inv_group,
    panel_group,
    leaf_solved,
    inv_leaf,
    dense,
    leaf_out,
    group_out,
    mid_out,
    top_out,
    upper,
    residual,
    above,
    sems,
    panel_sems,
    out_sems,
):
    leaf, pos, core = place()
    pairs = (
        (inv_top_hbm, inv_top),
        (inv_group_hbm, inv_group),
        (leaf_solved_hbm, leaf_solved),
        (inv_leaf_hbm, inv_leaf),
        (dense_hbm, dense),
    )
    loads = [pltpu.make_async_copy(a, b, sems.at[i]) for i, (a, b) in enumerate(pairs)]
    for kc, got in enumerate((panel_own_hbm, panel_other_hbm)):
        target = panel_group.at[:, core ^ kc]
        loads.append(pltpu.make_async_copy(got, target, panel_sems.at[kc]))
    for i in (0, 1, 5, 6, 2, 3, 4):
        loads[i].start()
    mid_rows = inv_mid.shape[0]
    top_rows = inv_top.shape[0]
    group_rows = inv_group.shape[0]
    supernodes, block, _ = inv_leaf.shape
    upper_cols = pl.ds(group_rows, mid_rows + top_rows)
    mid_cols = pl.ds(group_rows, mid_rows)
    top_cols = pl.ds(group_rows + mid_rows, top_rows)
    sec = (mid_rows + top_rows) // (2 * n_pos)
    q = sec // n_leaf
    gq = group_rows // (2 * n_pos)
    for kc, got in enumerate((mine, theirs)):
        for kz in range(n_pos):
            for kl in range(n_leaf):
                row = sec * (2 * (pos ^ kz) + (core ^ kc)) + q * (leaf ^ kl)
                begin = (kl * n_pos + kz) * q
                upper[pl.ds(pl.multiple_of(row, q), q), :] = got[begin : begin + q, :]
            row = (group_rows // 2) * (core ^ kc) + gq * (pos ^ kz)
            begin = n_leaf * n_pos * q + kz * gq
            residual[pl.ds(pl.multiple_of(row, gq), gq), :] = got[begin : begin + gq, :]

    mid_solved = lower_dot(inv_mid, upper[0:mid_rows, :]).astype(BF)
    top_residual = upper[mid_rows:, :].astype(F32) - dot(panel_mid[...], mid_solved)
    loads[0].wait()
    top_solved = lower_dot(inv_top, top_residual.astype(BF))
    top_t = dot_lower(top_solved.T.astype(BF), inv_top)
    above[:, top_cols] = top_t.astype(BF)
    top_out[...] = top_t.T
    stores = [pltpu.make_async_copy(top_out, top_hbm, out_sems.at[0])]
    stores[0].start()
    mid_back = mid_solved.astype(F32).T - dot(above[:, top_cols], panel_mid[...])
    mid_t = dot_lower(mid_back.astype(BF), inv_mid)
    above[:, mid_cols] = mid_t.astype(BF)
    mid_out[...] = mid_t.T
    stores.append(pltpu.make_async_copy(mid_out, mid_hbm, out_sems.at[1]))
    stores[1].start()
    for load in loads[1:]:
        load.wait()
    group_solved = lower_dot(inv_group, residual).astype(BF).astype(F32).T
    panel = panel_group[...].reshape(mid_rows + top_rows, group_rows)
    group_back = group_solved - dot(above[:, upper_cols], panel)
    group_t = dot_lower(group_back.astype(BF), inv_group)
    above[:, 0:group_rows] = group_t.astype(BF)
    group_out[...] = group_t.T
    stores.append(pltpu.make_async_copy(group_out, group_hbm, out_sems.at[2]))
    stores[2].start()
    pair = 2 * block
    for i in range(supernodes // 2):
        cols = pl.ds(i * pair, pair)
        terms = dot(above[...], dense[:, cols])
        back = (leaf_solved[cols, :].astype(F32).T - terms).astype(BF)
        for j in range(2):
            span = pl.ds(i * pair + j * block, block)
            out = dot(back[:, j * block : (j + 1) * block], inv_leaf[2 * i + j])
            leaf_out[span, :] = out.T
        sem = out_sems.at[3 + i]
        stores.append(pltpu.make_async_copy(leaf_out.at[cols], leaf_hbm.at[cols], sem))
        stores[-1].start()
    for store in stores:
        store.wait()


def backward(close, far, n_leaf, n_pos):
    mine, _, inv_mid, _ = close
    inv_top, inv_group, panel, _, leaf_solved, inv_leaf, dense = far
    width = mine.shape[-1]
    held = (inv_top.shape, inv_group.shape, (n_pos, 2) + panel.shape[1:])
    held += (leaf_solved.shape, inv_leaf.shape, dense.shape)
    outs = (
        leaf_solved.shape,
        (inv_group.shape[0], width),
        (inv_mid.shape[0], width),
        (inv_top.shape[0], width),
    )
    return pl.pallas_call(
        functools.partial(backward_kernel, n_leaf, n_pos),
        out_shape=[pltpu.HBM(shape, F32) for shape in outs],
        in_specs=[VMEM] * len(close) + [HBM] * len(far),
        out_specs=[HBM] * 4,
        scratch_shapes=[pltpu.VMEM(shape, BF) for shape in held]
        + [pltpu.VMEM(shape, F32) for shape in outs]
        + [
            pltpu.VMEM((inv_mid.shape[0] + inv_top.shape[0], width), BF),
            pltpu.VMEM((inv_group.shape[0], width), BF),
            pltpu.VMEM((width, dense.shape[0]), BF),
            pltpu.SemaphoreType.DMA((5,)),
            pltpu.SemaphoreType.DMA((2,)),
            pltpu.SemaphoreType.DMA((3 + leaf_solved.shape[0] // (2 * inv_leaf.shape[1]),)),
        ],
        compiler_params=pltpu.CompilerParams(vmem_limit_bytes=BIG),
        name="backward",
    )(*in_vmem(*close), *in_hbm(*far))


def swap(x, axis, size, bits):
    return lax.ppermute(x, axis, [(i, i ^ bits) for i in range(size)])


def swaps(x, axis, size, unit=1):
    return [x] + [swap(x, axis, size, unit * k) for k in range(1, size // unit)]


def after(x, *others):
    return lax.optimization_barrier((x, others))[0]


def body(
    n_leaf,
    n_grp,
    rhs_leaf,
    rhs_group,
    rhs_middle,
    rhs_top,
    inv_leaf,
    inv_group,
    inv_middle,
    inv_top,
    leaf_tiles,
    tile_column,
    tile_target,
    tile_count,
    group_panel,
    middle_panel,
):
    n_pos = n_grp // 2
    group_cols = rhs_group.shape[1]
    mid_cols = rhs_middle.shape[0]
    upper_cols = mid_cols + rhs_top.shape[0]
    sec = upper_cols // n_grp
    q = sec // n_leaf
    gq = group_cols // n_grp
    leaf, pos, core = place()
    by_parts = middle_panel.shape[0] % 16 == 0
    pos_groups = [[2 * p + c for p in range(n_pos)] for c in range(2)]
    with jax.named_scope("gather_group_panel"):
        panel = lax.all_gather(group_panel[0], "grp", axis_index_groups=pos_groups)
    with jax.named_scope("gather_middle_panel"):
        if by_parts:
            middles = swaps(middle_panel, "grp", n_grp, 2)
        else:
            middle = lax.all_gather(middle_panel, ("leaf", "grp"), axis=0, tiled=True)
    begin = sec * lax.axis_index("grp") + q * leaf
    low = lax.dynamic_slice_in_dim(rhs_middle, jnp.minimum(begin, mid_cols - q), q, 0)
    high = lax.dynamic_slice_in_dim(rhs_top, jnp.maximum(begin - mid_cols, 0), q, 0)
    rhs_mine = jnp.where(begin < mid_cols, low, high)
    keep, *send, inv_here, leaf_solved, dense = leaf_forward(
        rhs_leaf[0],
        inv_leaf[0],
        leaf_tiles[0],
        tile_column,
        tile_target,
        tile_count,
        inv_group[0],
        rhs_group[0],
        sec,
        upper_cols,
    )
    with jax.named_scope("swap_cores"):
        if by_parts:
            send = after(send, middles)
        recv = [swap(x, "grp", n_grp, 1) for x in send]
    with jax.named_scope("gather_middle_panel"):
        if by_parts:
            middles = swaps(stack(after(middles, send)), "leaf", n_leaf)
            recv = after(recv, middles)
            middle = stack(after(middles, rhs_mine))
    parts, group = fold(keep, recv, inv_here, panel, n_leaf)
    with jax.named_scope("sum_over_leaf"):
        parts = parts[:1] + [swap(parts[k], "leaf", n_leaf, k) for k in range(1, n_leaf)]
    with jax.named_scope("gather_middle_panel"):
        if by_parts:
            other = swap(after(middle, group), "grp", n_grp, 1)
            middle = weave(middle, other, n_leaf, n_pos)
    sends = sum_leaf(parts, group, n_pos)
    with jax.named_scope("sum_over_pos"):
        got = sends[:1] + [swap(sends[k], "grp", n_grp, 2 * k) for k in range(1, n_pos)]
    with jax.named_scope("swap_group_panel"):
        panel_other = swap(after(panel, sends), "grp", n_grp, 1)
    residual = sum_pos(rhs_mine, got)
    with jax.named_scope("gather_pos"):
        uppers, groups = stack_pos(swaps(residual, "grp", n_grp, 2), q)
    with jax.named_scope("gather_leaf"):
        stacks = swaps(uppers, "leaf", n_leaf)
    with jax.named_scope("gather_cores"):
        mine = stack(after(stacks, (panel_other, middle)) + [groups])
        theirs = swap(mine, "grp", n_grp, 1)
    leaf_out, group_out, mid_out, top_out = backward(
        (mine, theirs, inv_middle, middle),
        (inv_top, inv_group[0], panel, panel_other, leaf_solved, inv_leaf[0], dense),
        n_leaf,
        n_pos,
    )
    return leaf_out[None], group_out[None], mid_out, top_out


def solution(mesh):
    n_leaf = mesh.shape["leaf"]
    n_grp = mesh.shape["grp"]
    placed = (
        P("leaf", "grp", None),
        P("leaf", None, None),
        P(),
        P(),
        P("leaf", "grp", None, None),
        P("leaf", None, None),
        P(),
        P(),
        P("leaf", "grp", None, None),
        P("leaf", "grp"),
        P("leaf", "grp"),
        P("leaf", "grp"),
        P("leaf", "grp", None),
        P(("leaf", "grp"), None),
    )
    return jax.shard_map(
        functools.partial(body, n_leaf, n_grp),
        mesh=mesh,
        in_specs=placed,
        out_specs=(P("leaf", "grp", None), P("leaf", None, None), P(), P()),
        check_vma=False,
    )
```

```python
import functools

import jax
import jax.numpy as jnp
from jax import lax
from jax.experimental import pallas as pl
from jax.experimental.pallas import tpu as pltpu
from jax.sharding import PartitionSpec as P

BF = jnp.bfloat16
F32 = jnp.float32
MIB = 1024 * 1024
CHUNKS = 16
UNROLL = 4
HBM = pl.BlockSpec(memory_space=pltpu.HBM)
VMEM = pl.BlockSpec(memory_space=pltpu.VMEM)
BIG = 40 * MIB
SMALL = 6 * MIB


def in_hbm(*arrays):
    return [pltpu.with_memory_space_constraint(x, pltpu.HBM) for x in arrays]


def in_vmem(*arrays):
    return [pltpu.with_memory_space_constraint(x, pltpu.VMEM) for x in arrays]


def small(kernel, name, shapes, scratch, *args):
    return pl.pallas_call(
        kernel,
        out_shape=[pltpu.VMEM(shape, BF) for shape in shapes],
        in_specs=[VMEM] * len(args),
        out_specs=[VMEM] * len(shapes),
        scratch_shapes=scratch,
        compiler_params=pltpu.CompilerParams(vmem_limit_bytes=SMALL),
        name=name,
    )(*in_vmem(*args))


def dot(a, b):
    return jnp.dot(a, b, preferred_element_type=F32)


def place():
    g = lax.axis_index("grp")
    return lax.axis_index("leaf"), g >> 1, g & 1


def forward_kernel(
    n_pos,
    sec,
    group_cols,
    count_hbm,
    cols_hbm,
    tgts_hbm,
    rhs_hbm,
    inv_hbm,
    tiles_hbm,
    inv_group_hbm,
    rhs_group_hbm,
    keep,
    send_low,
    send_high,
    inv_group,
    solved_hbm,
    dense_hbm,
    count,
    cols,
    tgts,
    rhs,
    inv,
    tiles,
    acc,
    stage,
    solved,
    dense,
    rhs_group,
    in_sems,
    tile_sems,
    out_sems,
    pass_sems,
):
    slots, block, _ = tiles.shape
    supernodes = inv.shape[0]
    targets = acc.shape[0]
    chunks = tile_sems.shape[0]
    step = slots // chunks
    _, _, core = place()

    def tile_copy(k):
        span = pl.ds(k * step, step)
        return pltpu.make_async_copy(tiles_hbm.at[span], tiles.at[span], tile_sems.at[k])

    pairs = (
        (count_hbm, count),
        (cols_hbm, cols),
        (tgts_hbm, tgts),
        (rhs_hbm, rhs),
        (inv_hbm, inv),
    )
    loads = [pltpu.make_async_copy(a, b, in_sems.at[i]) for i, (a, b) in enumerate(pairs)]
    for load in loads:
        load.start()
    for k in range(chunks):
        tile_copy(k).start()
    pairs = ((inv_group_hbm, inv_group), (rhs_group_hbm, rhs_group))
    passes = [pltpu.make_async_copy(a, b, pass_sems.at[i]) for i, (a, b) in enumerate(pairs)]
    for copy in passes:
        copy.start()

    acc[...] = jnp.zeros_like(acc)
    for load in loads:
        load.wait()
    for s in range(supernodes):
        rows = pl.ds(s * block, block)
        solved[rows, :] = dot(inv[s], rhs[rows, :].astype(BF)).astype(BF)
    stores = [pltpu.make_async_copy(solved, solved_hbm, out_sems.at[0])]
    stores[0].start()

    live = count[0, 0]

    def add(p):
        t = tgts[0, p]
        c = cols[0, p]
        acc[t, c] = acc[t, c] + tiles[p].astype(F32)

    def add_some(i, carry):
        for u in range(UNROLL):
            add(i * UNROLL + u)
        return carry

    def add_one(p, carry):
        add(p)
        return carry

    whole = live // UNROLL
    per = step // UNROLL
    for k in range(chunks):
        tile_copy(k).wait()
        lax.fori_loop(k * per, jnp.clip(whole, k * per, (k + 1) * per), add_some, 0)
    lax.fori_loop(whole * UNROLL, live, add_one, 0)

    span = group_cols
    blocks = span // block
    for i in range(targets // blocks):
        for t in range(i * blocks, (i + 1) * blocks):
            for c in range(supernodes):
                dense[t * block : (t + 1) * block, c * block : (c + 1) * block] = acc[t, c].astype(BF)
        rows = pl.ds(i * span, span)
        stores.append(pltpu.make_async_copy(dense.at[rows], dense_hbm.at[rows], out_sems.at[1 + i]))
        stores[-1].start()
        total = dot(dense[rows, :], solved[...])
        if i == 0:
            passes[1].wait()
            share = jnp.where(core == 0, 1.0 / n_pos, 0.0)
            total = (total - rhs_group[...] * share).astype(BF)
            stage[0, 0:span, :] = total
            stage[1, 0:span, :] = total
        else:
            total = total.astype(BF)
            for q in range(0, span, sec):
                section = ((i - 1) * span + q) // sec
                begin = group_cols + (section // 2) * sec
                stage[(section % 2) ^ core, begin : begin + sec, :] = total[q : q + sec, :]
    keep[...] = stage[0]
    cut = send_low.shape[0]
    send_low[...] = stage[1, 0:cut, :]
    send_high[...] = stage[1, cut:, :]
    for copy in passes[:1] + stores:
        copy.wait()


def leaf_forward(
    rhs, inverse, tiles, cols, tgts, count, inv_group, rhs_group, sec, upper_cols
):
    group_cols = rhs_group.shape[0]
    slots, block, _ = tiles.shape
    supernodes = inverse.shape[0]
    targets = (group_cols + upper_cols) // block
    width = rhs.shape[-1]
    half = group_cols + upper_cols // 2
    return pl.pallas_call(
        functools.partial(forward_kernel, upper_cols // (2 * sec), sec, group_cols),
        out_shape=(
            pltpu.VMEM((half, width), BF),
            pltpu.VMEM((half // 2, width), BF),
            pltpu.VMEM((half // 2, width), BF),
            pltpu.VMEM(inv_group.shape, BF),
            pltpu.HBM((supernodes * block, width), BF),
            pltpu.HBM((targets * block, supernodes * block), BF),
        ),
        in_specs=[HBM] * 8,
        out_specs=(VMEM,) * 4 + (HBM,) * 2,
        scratch_shapes=[
            pltpu.SMEM(count.shape, count.dtype),
            pltpu.SMEM(cols.shape, cols.dtype),
            pltpu.SMEM(tgts.shape, tgts.dtype),
            pltpu.VMEM(rhs.shape, rhs.dtype),
            pltpu.VMEM(inverse.shape, inverse.dtype),
            pltpu.VMEM((slots, block, block), BF),
            pltpu.VMEM((targets, supernodes, block, block), F32),
            pltpu.VMEM((2, half, width), BF),
            pltpu.VMEM((supernodes * block, width), BF),
            pltpu.VMEM((targets * block, supernodes * block), BF),
            pltpu.VMEM(rhs_group.shape, F32),
            pltpu.SemaphoreType.DMA((5,)),
            pltpu.SemaphoreType.DMA((CHUNKS,)),
            pltpu.SemaphoreType.DMA((1 + targets * block // group_cols,)),
            pltpu.SemaphoreType.DMA((2,)),
        ],
        compiler_params=pltpu.CompilerParams(vmem_limit_bytes=BIG),
        cost_estimate=pl.CostEstimate(
            flops=2 * targets * block * supernodes * block * width,
            bytes_accessed=2 * tiles.size + 4 * rhs.size,
            transcendentals=0,
        ),
        name="leaf_forward",
    )(count, *in_hbm(cols, tgts, rhs, inverse, tiles, inv_group, rhs_group))


def total_of(refs):
    total = refs[0][...].astype(F32)
    for ref in refs[1:]:
        total = total + ref[...].astype(F32)
    return total


def fold_kernel(n_leaf, n_pos, keep, low, high, inv, panel_hbm, *refs):
    parts, group, (gsum, base, stage, panel, sems) = refs[:n_leaf], refs[n_leaf], refs[n_leaf + 1 :]
    leaf, pos, core = place()
    loads = [
        pltpu.make_async_copy(panel_hbm.at[pos ^ k], panel.at[k], sems.at[k]) for k in range(n_pos)
    ]
    for load in loads:
        load.start()
    group_cols = inv.shape[0]
    sec = panel.shape[1]
    q = sec // n_leaf
    gq = group_cols // (2 * n_pos)
    cut = low.shape[0]
    gsum[...] = keep[0:group_cols, :].astype(F32) + low[0:group_cols, :].astype(F32)
    base[0 : cut - group_cols, :] = keep[group_cols:cut, :].astype(F32) + low[group_cols:, :].astype(F32)
    base[cut - group_cols :, :] = keep[cut:, :].astype(F32) + high[...].astype(F32)
    solved = dot(inv[...], (-gsum[...]).astype(BF)).astype(BF)
    for k in range(n_pos):
        p = pos ^ k
        rows = pl.ds(pl.multiple_of(p * sec, sec), sec)
        loads[k].wait()
        terms = (dot(panel[k], solved) + base[rows, :]).astype(BF)
        for j in range(n_leaf):
            stage[j ^ leaf, k * q : (k + 1) * q, :] = terms[j * q : (j + 1) * q, :]
        begin = pl.multiple_of(core * (group_cols // 2) + p * gq, gq)
        group[k * gq : (k + 1) * gq, :] = gsum[pl.ds(begin, gq), :].astype(BF)
    for k in range(n_leaf):
        parts[k][...] = stage[k]


def fold(keep, recv, inverse, panel, n_leaf):
    width = keep.shape[-1]
    n_pos, sec, _ = panel.shape
    part = (n_pos * sec // n_leaf, width)
    outs = pl.pallas_call(
        functools.partial(fold_kernel, n_leaf, n_pos),
        out_shape=[pltpu.VMEM(part, BF)] * n_leaf
        + [pltpu.VMEM((inverse.shape[0] // 2, width), BF)],
        in_specs=[VMEM] * 4 + [HBM],
        out_specs=[VMEM] * (n_leaf + 1),
        scratch_shapes=[
            pltpu.VMEM((inverse.shape[0], width), F32),
            pltpu.VMEM((n_pos * sec, width), F32),
            pltpu.VMEM((n_leaf,) + part, BF),
            pltpu.VMEM(panel.shape, BF),
            pltpu.SemaphoreType.DMA((n_pos,)),
        ],
        compiler_params=pltpu.CompilerParams(vmem_limit_bytes=SMALL),
        name="fold_group",
    )(*in_vmem(keep, *recv, inverse), *in_hbm(panel))
    return list(outs[:n_leaf]), outs[n_leaf]


def sum_leaf_kernel(n_leaf, *refs):
    group, outs = refs[n_leaf], refs[n_leaf + 1 :]
    n_pos = len(outs)
    q = refs[0].shape[0] // n_pos
    gq = group.shape[0] // n_pos
    total = total_of(refs[:n_leaf]).astype(BF)
    for k, out in enumerate(outs):
        out[0:q, :] = total[k * q : (k + 1) * q, :]
        out[q:, :] = group[k * gq : (k + 1) * gq, :]


def sum_leaf(parts, group, n_pos):
    rows = (parts[0].shape[0] + group.shape[0]) // n_pos
    kernel = functools.partial(sum_leaf_kernel, len(parts))
    shapes = [(rows, group.shape[1])] * n_pos
    return list(small(kernel, "sum_leaf", shapes, [], *parts, group))


def sum_pos_kernel(high, *refs):
    parts, out = refs[:-1], refs[-1]
    q = high.shape[0]
    total = total_of(parts)
    out[0:q, :] = (high[...] - total[0:q, :]).astype(BF)
    out[q:, :] = (-total[q:, :]).astype(BF)


def sum_pos(high, parts):
    return small(sum_pos_kernel, "sum_pos", [parts[0].shape], [], high, *parts)[0]


def stack_pos_kernel(q, *refs):
    parts, (uppers, groups) = refs[:-2], refs[-2:]
    gq = parts[0].shape[0] - q
    for k, part in enumerate(parts):
        uppers[k * q : (k + 1) * q, :] = part[0:q, :]
        groups[k * gq : (k + 1) * gq, :] = part[q:, :]


def stack_pos(parts, q):
    n_pos, (rows, width) = len(parts), parts[0].shape
    shapes = [(n_pos * q, width), (n_pos * (rows - q), width)]
    return small(functools.partial(stack_pos_kernel, q), "stack_pos", shapes, [], *parts)


def stack_kernel(*refs):
    begin = 0
    for part in refs[:-1]:
        rows = part.shape[0]
        refs[-1][begin : begin + rows, :] = part[...]
        begin += rows


def stack(parts):
    rows = sum(part.shape[0] for part in parts)
    return small(stack_kernel, "stack", [(rows, parts[0].shape[1])], [], *parts)[0]


def weave_kernel(n_leaf, n_pos, own, other, out):
    leaf, pos, core = place()
    rows = own.shape[0] // (n_leaf * n_pos)
    for kc, part in enumerate((own, other)):
        for kl in range(n_leaf):
            for k in range(n_pos):
                block = (leaf ^ kl) * (2 * n_pos) + 2 * (pos ^ k) + (core ^ kc)
                span = pl.ds(pl.multiple_of(block * rows, rows), rows)
                begin = (kl * n_pos + k) * rows
                out[span, :] = part[begin : begin + rows, :]


def weave(own, other, n_leaf, n_pos):
    shape = (2 * own.shape[0], own.shape[1])
    kernel = functools.partial(weave_kernel, n_leaf, n_pos)
    return small(kernel, "weave", [shape], [], own, other)[0]


def lower_dot(lower, x):
    n = lower.shape[0]
    step = min(n, max(n // 4, 256))
    parts = []
    for i in range(0, n, step):
        parts.append(dot(lower[i : i + step, 0 : i + step], x[0 : i + step, :]))
    return jnp.concatenate(parts, axis=0)


def dot_lower(x, lower):
    n = lower.shape[0]
    step = min(n, max(n // 4, 256))
    parts = []
    for i in range(0, n, step):
        parts.append(dot(x[:, i:], lower[i:, i : i + step]))
    return jnp.concatenate(parts, axis=1)


def backward_kernel(
    n_leaf,
    n_pos,
    mine,
    theirs,
    inv_mid,
    panel_mid,
    inv_top_hbm,
    inv_group_hbm,
    panel_own_hbm,
    panel_other_hbm,
    leaf_solved_hbm,
    inv_leaf_hbm,
    dense_hbm,
    leaf_hbm,
    group_hbm,
    mid_hbm,
    top_hbm,
    inv_top,
    inv_group,
    panel_group,
    leaf_solved,
    inv_leaf,
    dense,
    leaf_out,
    group_out,
    mid_out,
    top_out,
    upper,
    residual,
    above,
    sems,
    panel_sems,
    out_sems,
):
    leaf, pos, core = place()
    pairs = (
        (inv_top_hbm, inv_top),
        (inv_group_hbm, inv_group),
        (leaf_solved_hbm, leaf_solved),
        (inv_leaf_hbm, inv_leaf),
        (dense_hbm, dense),
    )
    loads = [pltpu.make_async_copy(a, b, sems.at[i]) for i, (a, b) in enumerate(pairs)]
    for kc, got in enumerate((panel_own_hbm, panel_other_hbm)):
        target = panel_group.at[:, core ^ kc]
        loads.append(pltpu.make_async_copy(got, target, panel_sems.at[kc]))
    for i in (0, 1, 5, 6, 2, 3, 4):
        loads[i].start()
    mid_rows = inv_mid.shape[0]
    top_rows = inv_top.shape[0]
    group_rows = inv_group.shape[0]
    supernodes, block, _ = inv_leaf.shape
    upper_cols = pl.ds(group_rows, mid_rows + top_rows)
    mid_cols = pl.ds(group_rows, mid_rows)
    top_cols = pl.ds(group_rows + mid_rows, top_rows)
    sec = (mid_rows + top_rows) // (2 * n_pos)
    q = sec // n_leaf
    gq = group_rows // (2 * n_pos)
    for kc, got in enumerate((mine, theirs)):
        for kz in range(n_pos):
            for kl in range(n_leaf):
                row = sec * (2 * (pos ^ kz) + (core ^ kc)) + q * (leaf ^ kl)
                begin = (kl * n_pos + kz) * q
                upper[pl.ds(pl.multiple_of(row, q), q), :] = got[begin : begin + q, :]
            row = (group_rows // 2) * (core ^ kc) + gq * (pos ^ kz)
            begin = n_leaf * n_pos * q + kz * gq
            residual[pl.ds(pl.multiple_of(row, gq), gq), :] = got[begin : begin + gq, :]

    mid_solved = lower_dot(inv_mid, upper[0:mid_rows, :]).astype(BF)
    top_residual = upper[mid_rows:, :].astype(F32) - dot(panel_mid[...], mid_solved)
    loads[0].wait()
    top_solved = lower_dot(inv_top, top_residual.astype(BF))
    top_t = dot_lower(top_solved.T.astype(BF), inv_top)
    above[:, top_cols] = top_t.astype(BF)
    top_out[...] = top_t.T
    stores = [pltpu.make_async_copy(top_out, top_hbm, out_sems.at[0])]
    stores[0].start()
    mid_back = mid_solved.astype(F32).T - dot(above[:, top_cols], panel_mid[...])
    mid_t = dot_lower(mid_back.astype(BF), inv_mid)
    above[:, mid_cols] = mid_t.astype(BF)
    mid_out[...] = mid_t.T
    stores.append(pltpu.make_async_copy(mid_out, mid_hbm, out_sems.at[1]))
    stores[1].start()
    for load in loads[1:]:
        load.wait()
    group_solved = lower_dot(inv_group, residual).astype(BF).astype(F32).T
    panel = panel_group[...].reshape(mid_rows + top_rows, group_rows)
    group_back = group_solved - dot(above[:, upper_cols], panel)
    group_t = dot_lower(group_back.astype(BF), inv_group)
    above[:, 0:group_rows] = group_t.astype(BF)
    group_out[...] = group_t.T
    stores.append(pltpu.make_async_copy(group_out, group_hbm, out_sems.at[2]))
    stores[2].start()
    pair = 2 * block
    for i in range(supernodes // 2):
        cols = pl.ds(i * pair, pair)
        terms = dot(above[...], dense[:, cols])
        back = (leaf_solved[cols, :].astype(F32).T - terms).astype(BF)
        for j in range(2):
            span = pl.ds(i * pair + j * block, block)
            out = dot(back[:, j * block : (j + 1) * block], inv_leaf[2 * i + j])
            leaf_out[span, :] = out.T
        sem = out_sems.at[3 + i]
        stores.append(pltpu.make_async_copy(leaf_out.at[cols], leaf_hbm.at[cols], sem))
        stores[-1].start()
    for store in stores:
        store.wait()


def backward(close, far, n_leaf, n_pos):
    mine, _, inv_mid, _ = close
    inv_top, inv_group, panel, _, leaf_solved, inv_leaf, dense = far
    width = mine.shape[-1]
    held = (inv_top.shape, inv_group.shape, (n_pos, 2) + panel.shape[1:])
    held += (leaf_solved.shape, inv_leaf.shape, dense.shape)
    outs = (
        leaf_solved.shape,
        (inv_group.shape[0], width),
        (inv_mid.shape[0], width),
        (inv_top.shape[0], width),
    )
    return pl.pallas_call(
        functools.partial(backward_kernel, n_leaf, n_pos),
        out_shape=[pltpu.HBM(shape, F32) for shape in outs],
        in_specs=[VMEM] * len(close) + [HBM] * len(far),
        out_specs=[HBM] * 4,
        scratch_shapes=[pltpu.VMEM(shape, BF) for shape in held]
        + [pltpu.VMEM(shape, F32) for shape in outs]
        + [
            pltpu.VMEM((inv_mid.shape[0] + inv_top.shape[0], width), BF),
            pltpu.VMEM((inv_group.shape[0], width), BF),
            pltpu.VMEM((width, dense.shape[0]), BF),
            pltpu.SemaphoreType.DMA((5,)),
            pltpu.SemaphoreType.DMA((2,)),
            pltpu.SemaphoreType.DMA((3 + leaf_solved.shape[0] // (2 * inv_leaf.shape[1]),)),
        ],
        compiler_params=pltpu.CompilerParams(vmem_limit_bytes=BIG),
        name="backward",
    )(*in_vmem(*close), *in_hbm(*far))


def swap(x, axis, size, bits):
    return lax.ppermute(x, axis, [(i, i ^ bits) for i in range(size)])


def swaps(x, axis, size, unit=1):
    return [x] + [swap(x, axis, size, unit * k) for k in range(1, size // unit)]


def after(x, *others):
    return lax.optimization_barrier((x, others))[0]


def body(
    n_leaf,
    n_grp,
    rhs_leaf,
    rhs_group,
    rhs_middle,
    rhs_top,
    inv_leaf,
    inv_group,
    inv_middle,
    inv_top,
    leaf_tiles,
    tile_column,
    tile_target,
    tile_count,
    group_panel,
    middle_panel,
):
    n_pos = n_grp // 2
    group_cols = rhs_group.shape[1]
    mid_cols = rhs_middle.shape[0]
    upper_cols = mid_cols + rhs_top.shape[0]
    sec = upper_cols // n_grp
    q = sec // n_leaf
    gq = group_cols // n_grp
    leaf, pos, core = place()
    by_parts = middle_panel.shape[0] % 16 == 0
    pos_groups = [[2 * p + c for p in range(n_pos)] for c in range(2)]
    with jax.named_scope("gather_group_panel"):
        panel = lax.all_gather(group_panel[0], "grp", axis_index_groups=pos_groups)
    with jax.named_scope("gather_middle_panel"):
        if by_parts:
            middles = swaps(middle_panel, "grp", n_grp, 2)
        else:
            middle = lax.all_gather(middle_panel, ("leaf", "grp"), axis=0, tiled=True)
    begin = sec * lax.axis_index("grp") + q * leaf
    low = lax.dynamic_slice_in_dim(rhs_middle, jnp.minimum(begin, mid_cols - q), q, 0)
    high = lax.dynamic_slice_in_dim(rhs_top, jnp.maximum(begin - mid_cols, 0), q, 0)
    rhs_mine = jnp.where(begin < mid_cols, low, high)
    keep, *send, inv_here, leaf_solved, dense = leaf_forward(
        rhs_leaf[0],
        inv_leaf[0],
        leaf_tiles[0],
        tile_column,
        tile_target,
        tile_count,
        inv_group[0],
        rhs_group[0],
        sec,
        upper_cols,
    )
    with jax.named_scope("swap_cores"):
        if by_parts:
            send = after(send, middles)
        recv = [swap(x, "grp", n_grp, 1) for x in send]
    with jax.named_scope("gather_middle_panel"):
        if by_parts:
            middles = swaps(stack(after(middles, send)), "leaf", n_leaf)
            recv = after(recv, middles)
            middle = stack(after(middles, rhs_mine))
    parts, group = fold(keep, recv, inv_here, panel, n_leaf)
    with jax.named_scope("sum_over_leaf"):
        parts = parts[:1] + [swap(parts[k], "leaf", n_leaf, k) for k in range(1, n_leaf)]
    with jax.named_scope("gather_middle_panel"):
        if by_parts:
            other = swap(after(middle, group), "grp", n_grp, 1)
            middle = weave(middle, other, n_leaf, n_pos)
    sends = sum_leaf(parts, group, n_pos)
    with jax.named_scope("sum_over_pos"):
        got = sends[:1] + [swap(sends[k], "grp", n_grp, 2 * k) for k in range(1, n_pos)]
    with jax.named_scope("swap_group_panel"):
        panel_other = swap(after(panel, sends), "grp", n_grp, 1)
    residual = sum_pos(rhs_mine, got)
    with jax.named_scope("gather_pos"):
        uppers, groups = stack_pos(swaps(residual, "grp", n_grp, 2), q)
    with jax.named_scope("gather_leaf"):
        stacks = swaps(uppers, "leaf", n_leaf)
    with jax.named_scope("gather_cores"):
        mine = stack(after(stacks, (panel_other, middle)) + [groups])
        theirs = swap(mine, "grp", n_grp, 1)
    leaf_out, group_out, mid_out, top_out = backward(
        (mine, theirs, inv_middle, middle),
        (inv_top, inv_group[0], panel, panel_other, leaf_solved, inv_leaf[0], dense),
        n_leaf,
        n_pos,
    )
    return leaf_out[None], group_out[None], mid_out, top_out


def solution(mesh):
    n_leaf = mesh.shape["leaf"]
    n_grp = mesh.shape["grp"]
    placed = (
        P("leaf", "grp", None),
        P("leaf", None, None),
        P(),
        P(),
        P("leaf", "grp", None, None),
        P("leaf", None, None),
        P(),
        P(),
        P("leaf", "grp", None, None),
        P("leaf", "grp"),
        P("leaf", "grp"),
        P("leaf", "grp"),
        P("leaf", "grp", None),
        P(("leaf", "grp"), None),
    )
    return jax.shard_map(
        functools.partial(body, n_leaf, n_grp),
        mesh=mesh,
        in_specs=placed,
        out_specs=(P("leaf", "grp", None), P("leaf", None, None), P(), P()),
        check_vma=False,
    )
```

```python
import functools

import jax
import jax.numpy as jnp
from jax import lax
from jax.experimental import pallas as pl
from jax.experimental.pallas import tpu as pltpu
from jax.sharding import PartitionSpec as P

BF = jnp.bfloat16
F32 = jnp.float32
MIB = 1024 * 1024
CHUNKS = 16
UNROLL = 4
HBM = pl.BlockSpec(memory_space=pltpu.HBM)
VMEM = pl.BlockSpec(memory_space=pltpu.VMEM)
BIG = 40 * MIB
SMALL = 6 * MIB


def in_hbm(*arrays):
    return [pltpu.with_memory_space_constraint(x, pltpu.HBM) for x in arrays]


def in_vmem(*arrays):
    return [pltpu.with_memory_space_constraint(x, pltpu.VMEM) for x in arrays]


def small(kernel, name, shapes, scratch, *args):
    return pl.pallas_call(
        kernel,
        out_shape=[pltpu.VMEM(shape, BF) for shape in shapes],
        in_specs=[VMEM] * len(args),
        out_specs=[VMEM] * len(shapes),
        scratch_shapes=scratch,
        compiler_params=pltpu.CompilerParams(vmem_limit_bytes=SMALL),
        name=name,
    )(*in_vmem(*args))


def dot(a, b):
    return jnp.dot(a, b, preferred_element_type=F32)


def place():
    g = lax.axis_index("grp")
    return lax.axis_index("leaf"), g >> 1, g & 1


def forward_kernel(
    n_pos,
    sec,
    group_cols,
    count_hbm,
    cols_hbm,
    tgts_hbm,
    rhs_hbm,
    inv_hbm,
    tiles_hbm,
    inv_group_hbm,
    rhs_group_hbm,
    keep,
    send_low,
    send_high,
    inv_group,
    solved_hbm,
    dense_hbm,
    count,
    cols,
    tgts,
    rhs,
    inv,
    tiles,
    acc,
    stage,
    solved,
    dense,
    rhs_group,
    in_sems,
    tile_sems,
    out_sems,
    pass_sems,
):
    slots, block, _ = tiles.shape
    supernodes = inv.shape[0]
    targets = acc.shape[0]
    chunks = tile_sems.shape[0]
    step = slots // chunks
    _, _, core = place()

    def tile_copy(k):
        span = pl.ds(k * step, step)
        return pltpu.make_async_copy(tiles_hbm.at[span], tiles.at[span], tile_sems.at[k])

    pairs = (
        (count_hbm, count),
        (cols_hbm, cols),
        (tgts_hbm, tgts),
        (rhs_hbm, rhs),
        (inv_hbm, inv),
    )
    loads = [pltpu.make_async_copy(a, b, in_sems.at[i]) for i, (a, b) in enumerate(pairs)]
    for load in loads:
        load.start()
    for k in range(chunks):
        tile_copy(k).start()
    pairs = ((inv_group_hbm, inv_group), (rhs_group_hbm, rhs_group))
    passes = [pltpu.make_async_copy(a, b, pass_sems.at[i]) for i, (a, b) in enumerate(pairs)]
    for copy in passes:
        copy.start()

    acc[...] = jnp.zeros_like(acc)
    for load in loads:
        load.wait()
    for s in range(supernodes):
        rows = pl.ds(s * block, block)
        solved[rows, :] = dot(inv[s], rhs[rows, :].astype(BF)).astype(BF)
    stores = [pltpu.make_async_copy(solved, solved_hbm, out_sems.at[0])]
    stores[0].start()

    live = count[0, 0]

    def add(p):
        t = tgts[0, p]
        c = cols[0, p]
        acc[t, c] = acc[t, c] + tiles[p].astype(F32)

    def add_some(i, carry):
        for u in range(UNROLL):
            add(i * UNROLL + u)
        return carry

    def add_one(p, carry):
        add(p)
        return carry

    whole = live // UNROLL
    per = step // UNROLL
    for k in range(chunks):
        tile_copy(k).wait()
        lax.fori_loop(k * per, jnp.clip(whole, k * per, (k + 1) * per), add_some, 0)
    lax.fori_loop(whole * UNROLL, live, add_one, 0)

    span = group_cols
    blocks = span // block
    for i in range(targets // blocks):
        for t in range(i * blocks, (i + 1) * blocks):
            for c in range(supernodes):
                dense[t * block : (t + 1) * block, c * block : (c + 1) * block] = acc[t, c].astype(BF)
        rows = pl.ds(i * span, span)
        stores.append(pltpu.make_async_copy(dense.at[rows], dense_hbm.at[rows], out_sems.at[1 + i]))
        stores[-1].start()
        total = dot(dense[rows, :], solved[...])
        if i == 0:
            passes[1].wait()
            share = jnp.where(core == 0, 1.0 / n_pos, 0.0)
            total = (total - rhs_group[...] * share).astype(BF)
            stage[0, 0:span, :] = total
            stage[1, 0:span, :] = total
        else:
            total = total.astype(BF)
            for q in range(0, span, sec):
                section = ((i - 1) * span + q) // sec
                begin = group_cols + (section // 2) * sec
                stage[(section % 2) ^ core, begin : begin + sec, :] = total[q : q + sec, :]
    keep[...] = stage[0]
    cut = send_low.shape[0]
    send_low[...] = stage[1, 0:cut, :]
    send_high[...] = stage[1, cut:, :]
    for copy in passes[:1] + stores:
        copy.wait()


def leaf_forward(
    rhs, inverse, tiles, cols, tgts, count, inv_group, rhs_group, sec, upper_cols
):
    group_cols = rhs_group.shape[0]
    slots, block, _ = tiles.shape
    supernodes = inverse.shape[0]
    targets = (group_cols + upper_cols) // block
    width = rhs.shape[-1]
    half = group_cols + upper_cols // 2
    return pl.pallas_call(
        functools.partial(forward_kernel, upper_cols // (2 * sec), sec, group_cols),
        out_shape=(
            pltpu.VMEM((half, width), BF),
            pltpu.VMEM((half // 2, width), BF),
            pltpu.VMEM((half // 2, width), BF),
            pltpu.VMEM(inv_group.shape, BF),
            pltpu.HBM((supernodes * block, width), BF),
            pltpu.HBM((targets * block, supernodes * block), BF),
        ),
        in_specs=[HBM] * 8,
        out_specs=(VMEM,) * 4 + (HBM,) * 2,
        scratch_shapes=[
            pltpu.SMEM(count.shape, count.dtype),
            pltpu.SMEM(cols.shape, cols.dtype),
            pltpu.SMEM(tgts.shape, tgts.dtype),
            pltpu.VMEM(rhs.shape, rhs.dtype),
            pltpu.VMEM(inverse.shape, inverse.dtype),
            pltpu.VMEM((slots, block, block), BF),
            pltpu.VMEM((targets, supernodes, block, block), F32),
            pltpu.VMEM((2, half, width), BF),
            pltpu.VMEM((supernodes * block, width), BF),
            pltpu.VMEM((targets * block, supernodes * block), BF),
            pltpu.VMEM(rhs_group.shape, F32),
            pltpu.SemaphoreType.DMA((5,)),
            pltpu.SemaphoreType.DMA((CHUNKS,)),
            pltpu.SemaphoreType.DMA((1 + targets * block // group_cols,)),
            pltpu.SemaphoreType.DMA((2,)),
        ],
        compiler_params=pltpu.CompilerParams(vmem_limit_bytes=BIG),
        cost_estimate=pl.CostEstimate(
            flops=2 * targets * block * supernodes * block * width,
            bytes_accessed=2 * tiles.size + 4 * rhs.size,
            transcendentals=0,
        ),
        name="leaf_forward",
    )(count, *in_hbm(cols, tgts, rhs, inverse, tiles, inv_group, rhs_group))


def total_of(refs):
    total = refs[0][...].astype(F32)
    for ref in refs[1:]:
        total = total + ref[...].astype(F32)
    return total


def fold_kernel(n_leaf, n_pos, keep, low, high, inv, panel_hbm, *refs):
    parts, group, (gsum, base, stage, panel, sems) = refs[:n_leaf], refs[n_leaf], refs[n_leaf + 1 :]
    leaf, pos, core = place()
    loads = [
        pltpu.make_async_copy(panel_hbm.at[pos ^ k], panel.at[k], sems.at[k]) for k in range(n_pos)
    ]
    for load in loads:
        load.start()
    group_cols = inv.shape[0]
    sec = panel.shape[1]
    q = sec // n_leaf
    gq = group_cols // (2 * n_pos)
    cut = low.shape[0]
    gsum[...] = keep[0:group_cols, :].astype(F32) + low[0:group_cols, :].astype(F32)
    base[0 : cut - group_cols, :] = keep[group_cols:cut, :].astype(F32) + low[group_cols:, :].astype(F32)
    base[cut - group_cols :, :] = keep[cut:, :].astype(F32) + high[...].astype(F32)
    solved = dot(inv[...], (-gsum[...]).astype(BF)).astype(BF)
    for k in range(n_pos):
        p = pos ^ k
        rows = pl.ds(pl.multiple_of(p * sec, sec), sec)
        loads[k].wait()
        terms = (dot(panel[k], solved) + base[rows, :]).astype(BF)
        for j in range(n_leaf):
            stage[j ^ leaf, k * q : (k + 1) * q, :] = terms[j * q : (j + 1) * q, :]
        begin = pl.multiple_of(core * (group_cols // 2) + p * gq, gq)
        group[k * gq : (k + 1) * gq, :] = gsum[pl.ds(begin, gq), :].astype(BF)
    for k in range(n_leaf):
        parts[k][...] = stage[k]


def fold(keep, recv, inverse, panel, n_leaf):
    width = keep.shape[-1]
    n_pos, sec, _ = panel.shape
    part = (n_pos * sec // n_leaf, width)
    outs = pl.pallas_call(
        functools.partial(fold_kernel, n_leaf, n_pos),
        out_shape=[pltpu.VMEM(part, BF)] * n_leaf
        + [pltpu.VMEM((inverse.shape[0] // 2, width), BF)],
        in_specs=[VMEM] * 4 + [HBM],
        out_specs=[VMEM] * (n_leaf + 1),
        scratch_shapes=[
            pltpu.VMEM((inverse.shape[0], width), F32),
            pltpu.VMEM((n_pos * sec, width), F32),
            pltpu.VMEM((n_leaf,) + part, BF),
            pltpu.VMEM(panel.shape, BF),
            pltpu.SemaphoreType.DMA((n_pos,)),
        ],
        compiler_params=pltpu.CompilerParams(vmem_limit_bytes=SMALL),
        name="fold_group",
    )(*in_vmem(keep, *recv, inverse), *in_hbm(panel))
    return list(outs[:n_leaf]), outs[n_leaf]


def sum_leaf_kernel(n_leaf, *refs):
    group, outs = refs[n_leaf], refs[n_leaf + 1 :]
    n_pos = len(outs)
    q = refs[0].shape[0] // n_pos
    gq = group.shape[0] // n_pos
    total = total_of(refs[:n_leaf]).astype(BF)
    for k, out in enumerate(outs):
        out[0:q, :] = total[k * q : (k + 1) * q, :]
        out[q:, :] = group[k * gq : (k + 1) * gq, :]


def sum_leaf(parts, group, n_pos):
    rows = (parts[0].shape[0] + group.shape[0]) // n_pos
    kernel = functools.partial(sum_leaf_kernel, len(parts))
    shapes = [(rows, group.shape[1])] * n_pos
    return list(small(kernel, "sum_leaf", shapes, [], *parts, group))


def sum_pos_kernel(high, *refs):
    parts, out = refs[:-1], refs[-1]
    q = high.shape[0]
    total = total_of(parts)
    out[0:q, :] = (high[...] - total[0:q, :]).astype(BF)
    out[q:, :] = (-total[q:, :]).astype(BF)


def sum_pos(high, parts):
    return small(sum_pos_kernel, "sum_pos", [parts[0].shape], [], high, *parts)[0]


def stack_pos_kernel(q, *refs):
    parts, (uppers, groups) = refs[:-2], refs[-2:]
    gq = parts[0].shape[0] - q
    for k, part in enumerate(parts):
        uppers[k * q : (k + 1) * q, :] = part[0:q, :]
        groups[k * gq : (k + 1) * gq, :] = part[q:, :]


def stack_pos(parts, q):
    n_pos, (rows, width) = len(parts), parts[0].shape
    shapes = [(n_pos * q, width), (n_pos * (rows - q), width)]
    return small(functools.partial(stack_pos_kernel, q), "stack_pos", shapes, [], *parts)


def stack_kernel(*refs):
    begin = 0
    for part in refs[:-1]:
        rows = part.shape[0]
        refs[-1][begin : begin + rows, :] = part[...]
        begin += rows


def stack(parts):
    rows = sum(part.shape[0] for part in parts)
    return small(stack_kernel, "stack", [(rows, parts[0].shape[1])], [], *parts)[0]


def weave_kernel(n_leaf, n_pos, own, other, out):
    leaf, pos, core = place()
    rows = own.shape[0] // (n_leaf * n_pos)
    for kc, part in enumerate((own, other)):
        for kl in range(n_leaf):
            for k in range(n_pos):
                block = (leaf ^ kl) * (2 * n_pos) + 2 * (pos ^ k) + (core ^ kc)
                span = pl.ds(pl.multiple_of(block * rows, rows), rows)
                begin = (kl * n_pos + k) * rows
                out[span, :] = part[begin : begin + rows, :]


def weave(own, other, n_leaf, n_pos):
    shape = (2 * own.shape[0], own.shape[1])
    kernel = functools.partial(weave_kernel, n_leaf, n_pos)
    return small(kernel, "weave", [shape], [], own, other)[0]


def lower_dot(lower, x):
    n = lower.shape[0]
    step = min(n, max(n // 4, 256))
    parts = []
    for i in range(0, n, step):
        parts.append(dot(lower[i : i + step, 0 : i + step], x[0 : i + step, :]))
    return jnp.concatenate(parts, axis=0)


def dot_lower(x, lower):
    n = lower.shape[0]
    step = min(n, max(n // 4, 256))
    parts = []
    for i in range(0, n, step):
        parts.append(dot(x[:, i:], lower[i:, i : i + step]))
    return jnp.concatenate(parts, axis=1)


def backward_kernel(
    n_leaf,
    n_pos,
    mine,
    theirs,
    inv_mid,
    panel_mid,
    inv_top_hbm,
    inv_group_hbm,
    panel_own_hbm,
    panel_other_hbm,
    leaf_solved_hbm,
    inv_leaf_hbm,
    dense_hbm,
    leaf_hbm,
    group_hbm,
    mid_hbm,
    top_hbm,
    inv_top,
    inv_group,
    panel_group,
    leaf_solved,
    inv_leaf,
    dense,
    leaf_out,
    group_out,
    mid_out,
    top_out,
    upper,
    residual,
    above,
    sems,
    panel_sems,
    out_sems,
):
    leaf, pos, core = place()
    pairs = (
        (inv_top_hbm, inv_top),
        (inv_group_hbm, inv_group),
        (leaf_solved_hbm, leaf_solved),
        (inv_leaf_hbm, inv_leaf),
        (dense_hbm, dense),
    )
    loads = [pltpu.make_async_copy(a, b, sems.at[i]) for i, (a, b) in enumerate(pairs)]
    for kc, got in enumerate((panel_own_hbm, panel_other_hbm)):
        target = panel_group.at[:, core ^ kc]
        loads.append(pltpu.make_async_copy(got, target, panel_sems.at[kc]))
    for i in (0, 1, 5, 6, 2, 3, 4):
        loads[i].start()
    mid_rows = inv_mid.shape[0]
    top_rows = inv_top.shape[0]
    group_rows = inv_group.shape[0]
    supernodes, block, _ = inv_leaf.shape
    upper_cols = pl.ds(group_rows, mid_rows + top_rows)
    mid_cols = pl.ds(group_rows, mid_rows)
    top_cols = pl.ds(group_rows + mid_rows, top_rows)
    sec = (mid_rows + top_rows) // (2 * n_pos)
    q = sec // n_leaf
    gq = group_rows // (2 * n_pos)
    for kc, got in enumerate((mine, theirs)):
        for kz in range(n_pos):
            for kl in range(n_leaf):
                row = sec * (2 * (pos ^ kz) + (core ^ kc)) + q * (leaf ^ kl)
                begin = (kl * n_pos + kz) * q
                upper[pl.ds(pl.multiple_of(row, q), q), :] = got[begin : begin + q, :]
            row = (group_rows // 2) * (core ^ kc) + gq * (pos ^ kz)
            begin = n_leaf * n_pos * q + kz * gq
            residual[pl.ds(pl.multiple_of(row, gq), gq), :] = got[begin : begin + gq, :]

    mid_solved = lower_dot(inv_mid, upper[0:mid_rows, :]).astype(BF)
    top_residual = upper[mid_rows:, :].astype(F32) - dot(panel_mid[...], mid_solved)
    loads[0].wait()
    top_solved = lower_dot(inv_top, top_residual.astype(BF))
    top_t = dot_lower(top_solved.T.astype(BF), inv_top)
    above[:, top_cols] = top_t.astype(BF)
    top_out[...] = top_t.T
    stores = [pltpu.make_async_copy(top_out, top_hbm, out_sems.at[0])]
    stores[0].start()
    mid_back = mid_solved.astype(F32).T - dot(above[:, top_cols], panel_mid[...])
    mid_t = dot_lower(mid_back.astype(BF), inv_mid)
    above[:, mid_cols] = mid_t.astype(BF)
    mid_out[...] = mid_t.T
    stores.append(pltpu.make_async_copy(mid_out, mid_hbm, out_sems.at[1]))
    stores[1].start()
    for load in loads[1:]:
        load.wait()
    group_solved = lower_dot(inv_group, residual).astype(BF).astype(F32).T
    panel = panel_group[...].reshape(mid_rows + top_rows, group_rows)
    group_back = group_solved - dot(above[:, upper_cols], panel)
    group_t = dot_lower(group_back.astype(BF), inv_group)
    above[:, 0:group_rows] = group_t.astype(BF)
    group_out[...] = group_t.T
    stores.append(pltpu.make_async_copy(group_out, group_hbm, out_sems.at[2]))
    stores[2].start()
    pair = 2 * block
    for i in range(supernodes // 2):
        cols = pl.ds(i * pair, pair)
        terms = dot(above[...], dense[:, cols])
        back = (leaf_solved[cols, :].astype(F32).T - terms).astype(BF)
        for j in range(2):
            span = pl.ds(i * pair + j * block, block)
            out = dot(back[:, j * block : (j + 1) * block], inv_leaf[2 * i + j])
            leaf_out[span, :] = out.T
        sem = out_sems.at[3 + i]
        stores.append(pltpu.make_async_copy(leaf_out.at[cols], leaf_hbm.at[cols], sem))
        stores[-1].start()
    for store in stores:
        store.wait()


def backward(close, far, n_leaf, n_pos):
    mine, _, inv_mid, _ = close
    inv_top, inv_group, panel, _, leaf_solved, inv_leaf, dense = far
    width = mine.shape[-1]
    held = (inv_top.shape, inv_group.shape, (n_pos, 2) + panel.shape[1:])
    held += (leaf_solved.shape, inv_leaf.shape, dense.shape)
    outs = (
        leaf_solved.shape,
        (inv_group.shape[0], width),
        (inv_mid.shape[0], width),
        (inv_top.shape[0], width),
    )
    return pl.pallas_call(
        functools.partial(backward_kernel, n_leaf, n_pos),
        out_shape=[pltpu.HBM(shape, F32) for shape in outs],
        in_specs=[VMEM] * len(close) + [HBM] * len(far),
        out_specs=[HBM] * 4,
        scratch_shapes=[pltpu.VMEM(shape, BF) for shape in held]
        + [pltpu.VMEM(shape, F32) for shape in outs]
        + [
            pltpu.VMEM((inv_mid.shape[0] + inv_top.shape[0], width), BF),
            pltpu.VMEM((inv_group.shape[0], width), BF),
            pltpu.VMEM((width, dense.shape[0]), BF),
            pltpu.SemaphoreType.DMA((5,)),
            pltpu.SemaphoreType.DMA((2,)),
            pltpu.SemaphoreType.DMA((3 + leaf_solved.shape[0] // (2 * inv_leaf.shape[1]),)),
        ],
        compiler_params=pltpu.CompilerParams(vmem_limit_bytes=BIG),
        name="backward",
    )(*in_vmem(*close), *in_hbm(*far))


def swap(x, axis, size, bits):
    return lax.ppermute(x, axis, [(i, i ^ bits) for i in range(size)])


def swaps(x, axis, size, unit=1):
    return [x] + [swap(x, axis, size, unit * k) for k in range(1, size // unit)]


def after(x, *others):
    return lax.optimization_barrier((x, others))[0]


def body(
    n_leaf,
    n_grp,
    rhs_leaf,
    rhs_group,
    rhs_middle,
    rhs_top,
    inv_leaf,
    inv_group,
    inv_middle,
    inv_top,
    leaf_tiles,
    tile_column,
    tile_target,
    tile_count,
    group_panel,
    middle_panel,
):
    n_pos = n_grp // 2
    group_cols = rhs_group.shape[1]
    mid_cols = rhs_middle.shape[0]
    upper_cols = mid_cols + rhs_top.shape[0]
    sec = upper_cols // n_grp
    q = sec // n_leaf
    gq = group_cols // n_grp
    leaf, pos, core = place()
    by_parts = middle_panel.shape[0] % 16 == 0
    pos_groups = [[2 * p + c for p in range(n_pos)] for c in range(2)]
    with jax.named_scope("gather_group_panel"):
        panel = lax.all_gather(group_panel[0], "grp", axis_index_groups=pos_groups)
    with jax.named_scope("gather_middle_panel"):
        if by_parts:
            middles = swaps(middle_panel, "grp", n_grp, 2)
        else:
            middle = lax.all_gather(middle_panel, ("leaf", "grp"), axis=0, tiled=True)
    begin = sec * lax.axis_index("grp") + q * leaf
    low = lax.dynamic_slice_in_dim(rhs_middle, jnp.minimum(begin, mid_cols - q), q, 0)
    high = lax.dynamic_slice_in_dim(rhs_top, jnp.maximum(begin - mid_cols, 0), q, 0)
    rhs_mine = jnp.where(begin < mid_cols, low, high)
    keep, *send, inv_here, leaf_solved, dense = leaf_forward(
        rhs_leaf[0],
        inv_leaf[0],
        leaf_tiles[0],
        tile_column,
        tile_target,
        tile_count,
        inv_group[0],
        rhs_group[0],
        sec,
        upper_cols,
    )
    with jax.named_scope("swap_cores"):
        if by_parts:
            send = after(send, middles)
        recv = [swap(x, "grp", n_grp, 1) for x in send]
    with jax.named_scope("gather_middle_panel"):
        if by_parts:
            middles = swaps(stack(after(middles, send)), "leaf", n_leaf)
            recv = after(recv, middles)
            middle = stack(after(middles, rhs_mine))
    parts, group = fold(keep, recv, inv_here, panel, n_leaf)
    with jax.named_scope("sum_over_leaf"):
        parts = parts[:1] + [swap(parts[k], "leaf", n_leaf, k) for k in range(1, n_leaf)]
    with jax.named_scope("gather_middle_panel"):
        if by_parts:
            other = swap(after(middle, group), "grp", n_grp, 1)
            middle = weave(middle, other, n_leaf, n_pos)
    sends = sum_leaf(parts, group, n_pos)
    with jax.named_scope("sum_over_pos"):
        got = sends[:1] + [swap(sends[k], "grp", n_grp, 2 * k) for k in range(1, n_pos)]
    residual = sum_pos(rhs_mine, got)
    with jax.named_scope("gather_pos"):
        uppers, groups = stack_pos(swaps(residual, "grp", n_grp, 2), q)
    with jax.named_scope("swap_group_panel"):
        panel_other = swap(after(panel, uppers), "grp", n_grp, 1)
    with jax.named_scope("gather_leaf"):
        stacks = swaps(uppers, "leaf", n_leaf)
    with jax.named_scope("gather_cores"):
        mine = stack(after(stacks, middle) + [groups])
        theirs = swap(mine, "grp", n_grp, 1)
    leaf_out, group_out, mid_out, top_out = backward(
        (mine, theirs, inv_middle, middle),
        (inv_top, inv_group[0], panel, panel_other, leaf_solved, inv_leaf[0], dense),
        n_leaf,
        n_pos,
    )
    return leaf_out[None], group_out[None], mid_out, top_out


def solution(mesh):
    n_leaf = mesh.shape["leaf"]
    n_grp = mesh.shape["grp"]
    placed = (
        P("leaf", "grp", None),
        P("leaf", None, None),
        P(),
        P(),
        P("leaf", "grp", None, None),
        P("leaf", None, None),
        P(),
        P(),
        P("leaf", "grp", None, None),
        P("leaf", "grp"),
        P("leaf", "grp"),
        P("leaf", "grp"),
        P("leaf", "grp", None),
        P(("leaf", "grp"), None),
    )
    return jax.shard_map(
        functools.partial(body, n_leaf, n_grp),
        mesh=mesh,
        in_specs=placed,
        out_specs=(P("leaf", "grp", None), P("leaf", None, None), P(), P()),
        check_vma=False,
    )
```
